256 devices in a mesh: rows: 128 (over z, x, y), sub: 2 (over core).
Axes of the slice: x: 4, y: 4, z: 8, core: 2. Of those that a mesh axis runs over, the one named last changes fastest.
Arguments:
- locations: float32 [3, 524288], P(None, ('rows', 'sub')), may hold values from 0 to 1
- amplitude: float32 [524288], P(('rows', 'sub')), may hold values from 0.6 to 3.2
- noise: float32 [524288], P(('rows', 'sub')), may hold values from 0.25 to 1
- covariates: float32 [524288, 256], P(('rows', 'sub')), may hold values from -0.6 to 0.6
- pivot_owner: int32 [4, 128], replicated, may hold values from 0 to 255, as said below
- pivot_offset: int32 [4, 128], replicated, may hold values from 0 to 2047, as said below
Outputs:
- factor: float32 [524288, 512], P(('rows', 'sub'))
- weights: float32 [524288], P(('rows', 'sub'))
- mean_residual: float32 [4], replicated
The draws below stay inside these ranges and needn't reach their ends.
Inputs may be any that keep to these rules, and one draw needn't show every extreme that they name: `pivot_owner`: an index of a device along rows+sub; in each block no device holds more than 2 pivots and some device holds exactly 2. `pivot_offset`: a row of the owner's shard; no (owner, offset) pair appears twice in the whole table.
All inputs are finite; a program needn't handle non-finite values.
Results may differ from the reference program's by a relative error of at most 0.0003.
Values sent between devices are 32-bit elements; how exact they have to be, the bound alone decides.
No kernel may reach another device: no remote copies, remote signals or barrier semaphores. Data moves between devices by JAX's collectives and lax.ppermute only.
A program may use at most 64 MiB of HBM per device.

```python
import math
import jax
import jax.numpy as jnp
from jax import lax

ROWS_DEV = 2048
PIV = 128
COV = 256
BLOCKS = 4
CAP = 2
LOCS = 524288
DEVICES = 256


def pivot_table(key):
    hot_key, rest_key, mix_key, order_key = jax.random.split(key, 4)
    hottest = jax.random.randint(hot_key, (BLOCKS,), 0, DEVICES).astype(jnp.int32)
    hottest = hottest.at[0].set(DEVICES - 1)

    def block_owners(rest_one, mix_one, hot_one):
        picked = jax.random.permutation(rest_one, (DEVICES - 1) * CAP)[:PIV - CAP]
        others = (hot_one + 1 + picked // CAP) % DEVICES
        owners = jnp.concatenate([jnp.full((CAP,), hot_one, jnp.int32), others.astype(jnp.int32)])
        return jax.random.permutation(mix_one, owners)
    owners = jax.vmap(block_owners)(jax.random.split(rest_key, BLOCKS), jax.random.split(mix_key, BLOCKS), hottest)

    def row_order(order_one):
        shuffled = jax.random.permutation(order_one, ROWS_DEV).astype(jnp.int32)
        return ((shuffled + (ROWS_DEV - 1) - shuffled[0]) % ROWS_DEV).astype(jnp.int32)
    orders = jax.vmap(row_order)(jax.random.split(order_key, DEVICES))
    flat_owner = owners.reshape(-1).astype(jnp.int32)
    onehot = (flat_owner[:, None] == jnp.arange(DEVICES, dtype=jnp.int32)[None, :]).astype(jnp.int32)
    before = jnp.cumsum(onehot, axis=0) - onehot
    ranks = jnp.sum(before * onehot, axis=1).astype(jnp.int32)
    offsets = orders[flat_owner, ranks].astype(jnp.int32)
    return (owners.astype(jnp.int32), offsets.reshape(BLOCKS, PIV))


def draw_pivot_owner(key, part):
    owners, offsets = pivot_table(key)
    return owners


def draw_pivot_offset(key, part):
    owners, offsets = pivot_table(key)
    return offsets


def draw_amplitude(key, part):
    key = jax.random.fold_in(key, 11)
    place = jnp.arange(LOCS, dtype=jnp.float32) / LOCS
    rough = jax.random.uniform(key, (LOCS,), jnp.float32, -0.35, 0.35)
    trend = 0.55
    return jnp.exp(rough + trend * place)


def shard_levels(key, dims, cuts, least, largest):
    level = 1.0
    for dim, blocks in cuts:
        heights = jax.random.uniform(jax.random.fold_in(jax.random.fold_in(key, 6), dim), (blocks,), jnp.float32, least / len(cuts), largest / len(cuts))
        level = level * jnp.repeat(jnp.exp(heights), dims[dim] // blocks).reshape((-1,) + (1,) * (len(dims) - 1 - dim))
    return level


def centred(stream_key, dims, width, limit, cuts=(), held_as=jnp.bfloat16):
    values = width * jax.random.normal(stream_key, dims, jnp.float32)
    if cuts:
        values = values * shard_levels(stream_key, dims, cuts, -0.22, 0.18)
    return jnp.clip(values, -limit, limit).astype(held_as)


def setup_inputs(seed: int = 0) -> dict:
    splits = jax.random.split(jax.random.key(seed), 7)
    locations = jnp.clip(1.0 * jax.random.uniform(splits[0], (3, LOCS), jnp.float32) ** shard_levels(splits[0], (3, LOCS), ((1, 256),), -0.2, 0.2), 0.0, 1.0)
    amplitude = draw_amplitude(jax.random.fold_in(splits[6], 71), 0)
    noise = jnp.clip(jnp.exp(math.log(1.0) - 1.3862944 * jax.random.uniform(splits[2], (LOCS,), jnp.float32) ** shard_levels(splits[2], (LOCS,), ((0, 256),), -0.2, 0.2)), 0.25, 1.0)
    covariates = centred(splits[3], (LOCS, COV), (1.6 / COV ** 0.5), 0.6, ((0, 256),), jnp.float32)
    pivot_owner = draw_pivot_owner(jax.random.fold_in(splits[6], 71), 0)
    pivot_offset = draw_pivot_offset(jax.random.fold_in(splits[6], 71), 0)
    return {"locations": locations, "amplitude": amplitude, "noise": noise, "covariates": covariates, "pivot_owner": pivot_owner, "pivot_offset": pivot_offset}


LENGTH_SCALE = 0.3

def matern_block(points, scales, piv_points, piv_scales):
    dist_sq = jnp.zeros((points.shape[1], piv_points.shape[1]), jnp.float32)
    for axis_id in range(3):
        offset = points[axis_id][:, None] - piv_points[axis_id][None, :]
        dist_sq = dist_sq + offset * offset
    scaled = jnp.sqrt(5.0 * dist_sq) / LENGTH_SCALE
    shape_term = (1.0 + scaled + scaled * scaled / 3.0) * jnp.exp(-scaled)
    return scales[:, None] * piv_scales[None, :] * shape_term

def reference(locations, amplitude, noise, covariates, pivot_owner, pivot_offset):
    pivots = (pivot_owner * ROWS_DEV + pivot_offset).astype(jnp.int32)
    residual = amplitude * amplitude + noise + lax.optimization_barrier(jnp.sum(covariates * covariates, axis=1))
    shard_points = locations.reshape(3, DEVICES, ROWS_DEV).transpose(1, 0, 2)
    shard_scales = amplitude.reshape(DEVICES, ROWS_DEV)
    shard_noise = noise.reshape(DEVICES, ROWS_DEV)
    shard_cov = covariates.reshape(DEVICES, ROWS_DEV, COV)
    shard_first = (lax.iota(jnp.int32, DEVICES) * ROWS_DEV).astype(jnp.int32)
    columns = []
    mean_list = []
    for block_id in range(BLOCKS):
        chosen = pivots[block_id]
        piv_points = locations[:, chosen]
        piv_scales = amplitude[chosen]
        piv_noise = noise[chosen]
        piv_cov = covariates[chosen]
        pivot_matrix = matern_block(piv_points, piv_scales, piv_points, piv_scales) + jnp.diag(piv_noise)
        pivot_matrix = pivot_matrix + jnp.dot(piv_cov, piv_cov.T, precision=lax.Precision.HIGHEST)
        pivot_rows = None
        if columns:
            pivot_rows = jnp.concatenate([column_block[chosen] for column_block in columns], axis=1)
            pivot_matrix = pivot_matrix - jnp.dot(pivot_rows, pivot_rows.T, precision=lax.Precision.HIGHEST)
        pivot_matrix = 0.5 * (pivot_matrix + pivot_matrix.T)
        lower_factor = jnp.linalg.cholesky(pivot_matrix)
        earlier_cols = tuple((column_block.reshape(DEVICES, ROWS_DEV, PIV) for column_block in columns))

        def one_shard(bundle):
            points, scales, nugget, cov_rows, first_row, shard_cols = bundle
            kernel = matern_block(points, scales, piv_points, piv_scales)
            self_match = (first_row + lax.iota(jnp.int32, ROWS_DEV))[:, None] == chosen[None, :]
            kernel = kernel + jnp.where(self_match, nugget[:, None], 0.0)
            kernel = kernel + jnp.dot(cov_rows, piv_cov.T, precision=lax.Precision.HIGHEST)
            if shard_cols:
                approx = jnp.dot(shard_cols[0], pivot_rows[:, :PIV].T, precision=lax.Precision.HIGHEST)
                for position in range(1, len(shard_cols)):
                    approx = approx + jnp.dot(shard_cols[position], pivot_rows[:, position * PIV:(position + 1) * PIV].T, precision=lax.Precision.HIGHEST)
                kernel = kernel - approx
            return jax.scipy.linalg.solve_triangular(lower_factor, kernel.T, lower=True).T
        new_columns = lax.map(one_shard, (shard_points, shard_scales, shard_noise, shard_cov, shard_first, earlier_cols)).reshape(LOCS, PIV)
        columns.append(new_columns)
        residual = residual - lax.optimization_barrier(jnp.sum(new_columns * new_columns, axis=1))
        mean_list.append(jnp.sum(residual) / LOCS)
    factor = jnp.concatenate(columns, axis=1)
    mean_residual = jnp.stack(mean_list)
    weights = residual / mean_residual[BLOCKS - 1]
    return (factor, weights, mean_residual)
```

```python
import jax
import jax.numpy as jnp
from jax import lax
from jax.sharding import Mesh
from jax.sharding import PartitionSpec as P

LENGTH_SCALE = 0.3
CAP = 2
AXES = ("z", "x", "y", "c")
HIGHEST = lax.Precision.HIGHEST


def matern_block(points, scales, piv_points, piv_scales):
    dist_sq = jnp.zeros((points.shape[1], piv_points.shape[1]), jnp.float32)
    for axis_id in range(3):
        offset = points[axis_id][:, None] - piv_points[axis_id][None, :]
        dist_sq = dist_sq + offset * offset
    scaled = jnp.sqrt(5.0 * dist_sq) / LENGTH_SCALE
    shape_term = (1.0 + scaled + scaled * scaled / 3.0) * jnp.exp(-scaled)
    return scales[:, None] * piv_scales[None, :] * shape_term


def broadcast_over(value, axes, count):
    copies = jnp.broadcast_to(value[None], (count,) + value.shape)
    return lax.all_to_all(copies, axes, 0, 0, tiled=True)


def local(locations, amplitude, noise, covariates, pivot_owner, pivot_offset):
    device_id = lax.axis_index(AXES)
    core = lax.axis_index("c")
    blocks_total, block_width = pivot_owner.shape
    pivots = blocks_total * block_width
    cov_width = covariates.shape[1]
    half = cov_width // 2
    local_rows = locations.shape[1]
    sizes = [lax.axis_size(name) for name in AXES]
    devices = sizes[0] * sizes[1] * sizes[2] * sizes[3]
    slots = CAP * blocks_total

    same = pivot_owner[:, :, None] == pivot_owner[:, None, :]
    before = lax.iota(jnp.int32, block_width)[None, :] < lax.iota(jnp.int32, block_width)[:, None]
    rank = jnp.sum(jnp.where(same & before[None], 1, 0), axis=2)
    slot = (rank + CAP * lax.iota(jnp.int32, blocks_total)[:, None]).reshape(-1)
    owner = pivot_owner.reshape(-1)
    offset = pivot_offset.reshape(-1)
    here = (owner == device_id)[None, :] & (slot[None, :] == lax.iota(jnp.int32, slots)[:, None])
    my_offset = jnp.sum(jnp.where(here, offset[None, :], 0), axis=1)
    features = jnp.concatenate(
        [
            covariates[my_offset],
            locations[:, my_offset].T,
            amplitude[my_offset][:, None],
            noise[my_offset][:, None],
            jnp.zeros((slots, 123), jnp.float32),
        ],
        axis=1,
    )

    column = broadcast_over(features, ("z", "c"), sizes[0] * sizes[3])
    column = column.reshape(-1, features.shape[1])
    cov_half = jnp.where(core == 0, column[:, :half], column[:, half:cov_width])
    message = jnp.concatenate([cov_half, column[:, cov_width : cov_width + 8].T], axis=0)
    plane = broadcast_over(message, ("x", "y"), sizes[1] * sizes[2])
    mine = plane[:, : column.shape[0]]
    scalars = jnp.moveaxis(plane[:, column.shape[0] :], 0, 1).reshape(8, -1)
    other = lax.ppermute(mine, "c", [(0, 1), (1, 0)])
    table = jnp.concatenate(
        [jnp.where(core == 0, mine, other), jnp.where(core == 0, other, mine)], axis=2
    ).reshape(-1, cov_width)

    own_c = owner % sizes[3]
    chip = owner // sizes[3]
    per_plane = sizes[1] * sizes[2]
    row = ((chip % per_plane) * sizes[0] + chip // per_plane) * sizes[3] + own_c
    row = row * slots + slot
    piv_cov = table[row]
    piv_scal = scalars[:, row]
    piv_points, piv_scales, piv_noise = piv_scal[0:3], piv_scal[3], piv_scal[4]

    pivot_matrix = matern_block(piv_points, piv_scales, piv_points, piv_scales)
    pivot_matrix = pivot_matrix + jnp.diag(piv_noise)
    pivot_matrix = pivot_matrix + jnp.dot(piv_cov, piv_cov.T, precision=HIGHEST)
    pivot_matrix = 0.5 * (pivot_matrix + pivot_matrix.T)
    lower_factor = jnp.linalg.cholesky(pivot_matrix)

    kernel = matern_block(locations, amplitude, piv_points, piv_scales)
    row_ids = lax.iota(jnp.int32, local_rows)
    mine_at = jnp.where(owner == device_id, offset, -1)
    kernel = kernel + jnp.where(row_ids[:, None] == mine_at[None, :], noise[:, None], 0.0)
    kernel = kernel + jnp.dot(covariates, piv_cov.T, precision=HIGHEST)
    factor = jax.scipy.linalg.solve_triangular(lower_factor, kernel.T, lower=True).T
    residual = amplitude * amplitude + noise + jnp.sum(covariates * covariates, axis=1)
    taken = jnp.sum((factor * factor).reshape(local_rows, blocks_total, block_width), axis=2)
    sums = jnp.sum(residual) - jnp.cumsum(jnp.sum(taken, axis=0))
    all_sums = lax.all_to_all(
        jnp.broadcast_to(sums[None], (devices, blocks_total)), AXES, 0, 0, tiled=True
    )
    mean_residual = jnp.sum(all_sums, axis=0) / float(local_rows * devices)
    weights = (residual - jnp.sum(taken, axis=1)) / mean_residual[blocks_total - 1]
    return (factor, weights, mean_residual)


def solution(mesh):
    shape = (8, 4, 4, 2)
    named = Mesh(mesh.devices.reshape(shape), AXES)
    return jax.shard_map(
        local,
        mesh=named,
        in_specs=(P(None, AXES), P(AXES), P(AXES), P(AXES, None), P(), P()),
        out_specs=(P(AXES, None), P(AXES), P()),
        check_vma=False,
    )
```

```python
import jax
import jax.numpy as jnp
from jax import lax
from jax.experimental import pallas as pl
from jax.experimental.pallas import tpu as pltpu
from jax.sharding import Mesh
from jax.sharding import PartitionSpec as P

LENGTH_SCALE = 0.3
CAP = 2
AXES = ("z", "x", "y", "c")
HIGHEST = lax.Precision.HIGHEST
BLOCK = 128
PANEL = 16
SUB = 8
TILE = 256


def dot(left, right, dims):
    return lax.dot_general(
        left, right, (dims, ((), ())), precision=HIGHEST, preferred_element_type=jnp.float32
    )


def panel_inverse(low, high):
    sub = lax.broadcasted_iota(jnp.int32, (SUB, BLOCK), 0)
    low, high = list(low), list(high)
    root_low = jnp.zeros((SUB, BLOCK), jnp.float32)
    root_high = root_low
    for k in range(PANEL):
        if k < SUB:
            pivot = jnp.broadcast_to(low[k][k : k + 1, :], (SUB, BLOCK))
            inverse = pl.reciprocal(pivot, approx=True)
            take_low = jnp.where(sub > k, low[k] * inverse, 0.0)
            take_high = high[k] * inverse
            root_low = jnp.where(sub == k, lax.rsqrt(pivot), root_low)
            for j in range(PANEL):
                if j != k:
                    entry = low[j][k : k + 1, :]
                    low[j] = low[j] - take_low * entry
                    high[j] = high[j] - take_high * entry
            low[k] = jnp.where(sub == k, 1.0, -take_low)
            high[k] = -take_high
        else:
            s = k - SUB
            pivot = jnp.broadcast_to(high[k][s : s + 1, :], (SUB, BLOCK))
            inverse = pl.reciprocal(pivot, approx=True)
            take_high = jnp.where(sub > s, high[k] * inverse, 0.0)
            root_high = jnp.where(sub == s, lax.rsqrt(pivot), root_high)
            for j in range(PANEL):
                if j != k:
                    high[j] = high[j] - take_high * high[j][s : s + 1, :]
            high[k] = jnp.where(sub == s, 1.0, -take_high)
    return [low[j] * root_low for j in range(SUB)], [high[j] * root_high for j in range(PANEL)]


def block_inverse(rows):
    lane = lax.broadcasted_iota(jnp.int32, (SUB, BLOCK), 1)
    sub = lax.broadcasted_iota(jnp.int32, (SUB, BLOCK), 0)
    rows = list(rows)
    out = [None] * len(rows)
    for panel in range(BLOCK // PANEL):
        first = PANEL * panel
        at = 2 * panel

        def splat(piece, j):
            return jnp.broadcast_to(piece[:, first + j : first + j + 1], (SUB, BLOCK))

        rest = range(at + 2, len(rows))
        low = [splat(rows[at], j) for j in range(PANEL)]
        high = [splat(rows[at + 1], j) for j in range(PANEL)]
        coef = {r: [splat(rows[r], j) for j in range(PANEL)] for r in rest}
        inv_low, inv_high = panel_inverse(low, high)
        in_panel = (lane >= first) & (lane < first + PANEL)
        top = jnp.where(in_panel, jnp.where(lane - first == sub, 1.0, 0.0), rows[at])
        bottom = jnp.where(in_panel, jnp.where(lane - first - SUB == sub, 1.0, 0.0), rows[at + 1])
        new_low = jnp.zeros((SUB, BLOCK), jnp.float32)
        new_high = new_low
        for j in range(PANEL):
            entry = top[j : j + 1, :] if j < SUB else bottom[j - SUB : j - SUB + 1, :]
            if j < SUB:
                new_low = new_low + inv_low[j] * entry
            new_high = new_high + inv_high[j] * entry
        out[at] = jnp.where(lane <= first + sub, new_low, 0.0)
        out[at + 1] = jnp.where(lane <= first + SUB + sub, new_high, 0.0)
        if len(rest):
            weights = []
            for j in range(PANEL):
                term = inv_high[j] * new_high
                if j < SUB:
                    term = term + inv_low[j] * new_low
                weights.append(jnp.sum(term, axis=0, keepdims=True))
            for r in rest:
                piece = jnp.where(in_panel, 0.0, rows[r])
                for j in range(PANEL):
                    piece = piece - coef[r][j] * weights[j]
                rows[r] = piece
    return out


def factor_inverse(z_ref, r_ref):
    size = z_ref.shape[0]
    lane = lax.broadcasted_iota(jnp.int32, (1, size), 1)

    def step(b, carry):
        at = pl.ds(pl.multiple_of(b * BLOCK, BLOCK), BLOCK)
        pieces = [
            z_ref[pl.ds(pl.multiple_of(b * BLOCK + SUB * i, SUB), SUB), at]
            for i in range(BLOCK // SUB)
        ]
        inverse = jnp.concatenate(block_inverse(pieces), axis=0)
        r_ref[...] = dot(inverse, z_ref[at, :], ((1,), (0,)))
        r_ref[:, at] = inverse
        z_ref[:, at] = jnp.zeros((size, BLOCK), jnp.float32)
        row = r_ref[...]
        coef = jnp.where(lane >= (b + 1) * BLOCK, row, 0.0)
        z_ref[...] -= dot(coef, row, ((0,), (0,)))
        z_ref[at, :] = row
        return carry

    lax.fori_loop(0, size // BLOCK, step, 0)


def matern(cols, rows, col_scale, row_scale):
    dist_sq = None
    for axis_id in range(3):
        offset = cols[axis_id] - rows[axis_id]
        dist_sq = offset * offset if dist_sq is None else dist_sq + offset * offset
    scaled = dist_sq * lax.rsqrt(jnp.maximum(dist_sq, 1e-30))
    shape_term = (1.0 + scaled + dist_sq * (1.0 / 3.0)) * jnp.exp(-scaled)
    return col_scale * row_scale * shape_term


def main_kernel(
    mine_ref,
    other_ref,
    place_ref,
    match_ref,
    core_ref,
    feat_ref,
    cov_hbm,
    out_hbm,
    resid_ref,
    sums_ref,
    cov_ref,
    table_ref,
    scal_ref,
    z_ref,
    r_ref,
    col_ref,
    tile_ref,
    load_sem,
    store_sem,
):
    pivots = z_ref.shape[0]
    local_rows, cov_width = cov_ref.shape
    half = cov_width // 2
    planes = mine_ref.shape[0]
    blocks = pivots // BLOCK
    load = pltpu.make_async_copy(cov_hbm, cov_ref, load_sem)
    load.start()
    core = core_ref[0]

    per_block = BLOCK // blocks
    candidates = planes * per_block
    lane = lax.broadcasted_iota(jnp.int32, (SUB, BLOCK), 1)
    scale = (5.0**0.5) / LENGTH_SCALE
    for b in range(blocks):
        slots = pl.ds(b * per_block, per_block)
        pick = (
            lax.broadcasted_iota(jnp.int32, (BLOCK, candidates), 1) == place_ref[:, b : b + 1]
        ).astype(jnp.float32)
        own = dot(pick, mine_ref[:, slots, :].reshape(candidates, half), ((1,), (0,)))
        far = dot(pick, other_ref[:, slots, :].reshape(candidates, half), ((1,), (0,)))
        here = pl.ds(b * BLOCK, BLOCK)
        table_ref[here, :half] = jnp.where(core == 0, own, far)
        table_ref[here, half:] = jnp.where(core == 0, far, own)
        parts = []
        for q in range(planes // blocks):
            part = jnp.zeros((SUB, BLOCK), jnp.float32)
            for t in range(blocks):
                piece = mine_ref[q * blocks + t, BLOCK : BLOCK + SUB, :]
                shift = (per_block * (t - b)) % BLOCK
                piece = pltpu.roll(piece, shift, 1) if shift else piece
                part = jnp.where(lane // per_block == t, piece, part)
            parts.append(part)
        scalars = jnp.concatenate(parts, axis=1)
        scal_ref[:, here] = dot(scalars, pick, ((1,), (1,)))

    load.wait()
    for t in range(local_rows // BLOCK):
        at = pl.ds(t * BLOCK, BLOCK)
        col_ref[at, :] = feat_ref[:, at].T
    piv = scal_ref[...]
    piv_rows = [piv[i : i + 1, :] * scale for i in range(3)]
    piv_scale, piv_noise = piv[3:4, :], piv[4:5, :]

    for b in range(blocks):
        here = pl.ds(b * BLOCK, BLOCK)
        cols = scal_ref[:, here].T
        piece = matern([cols[:, i : i + 1] * scale for i in range(3)], piv_rows, cols[:, 3:4], piv_scale)
        same = lax.broadcasted_iota(jnp.int32, (BLOCK, 1), 0) + b * BLOCK == lax.broadcasted_iota(
            jnp.int32, (1, pivots), 1
        )
        piece = piece + jnp.where(same, piv_noise, 0.0)
        z_ref[here, :] = piece + dot(table_ref[here, :], table_ref[...], ((1,), (1,)))
    factor_inverse(z_ref, r_ref)

    match = match_ref[...]
    diagonal = lax.broadcasted_iota(jnp.int32, (BLOCK, BLOCK), 0) == lax.broadcasted_iota(
        jnp.int32, (BLOCK, BLOCK), 1
    )
    left = pivots // 2
    half_tiles = TILE // BLOCK

    def tile_step(t, taken):
        at = pl.ds(pl.multiple_of(t * TILE, TILE), TILE)
        cols = col_ref[at, :]
        cov = cov_ref[at, :]
        kernel = matern([cols[:, i : i + 1] * scale for i in range(3)], piv_rows, cols[:, 3:4], piv_scale)
        row_ids = lax.broadcasted_iota(jnp.int32, (TILE, 1), 0) + t * TILE
        kernel = kernel + jnp.where(row_ids == match, cols[:, 4:5], 0.0)
        kernel = kernel + dot(cov, table_ref[...], ((1,), (1,)))
        slot = lax.rem(t, 2)

        @pl.when(t >= 2)
        def _():
            pltpu.make_async_copy(tile_ref.at[slot], out_hbm.at[at, :], store_sem.at[slot]).wait()

        first = dot(kernel[:, :left], z_ref[:left, :left], ((1,), (1,)))
        second = dot(kernel, z_ref[left:, :], ((1,), (1,)))
        tile_ref[slot, :, :left] = first
        tile_ref[slot, :, left:] = second
        pltpu.make_async_copy(tile_ref.at[slot], out_hbm.at[at, :], store_sem.at[slot]).start()
        squares = []
        for b in range(blocks):
            source = first if b * BLOCK < left else second
            piece = source[:, (b * BLOCK) % left : (b * BLOCK) % left + BLOCK]
            squares.append(piece * piece)
        cov_sq = cov * cov
        total = cov_sq[:, :half] + cov_sq[:, half:]
        new_taken = []
        for b in range(blocks):
            total = total - squares[b]
            new_taken.append(
                taken[b] + jnp.sum(squares[b].reshape(TILE // SUB, SUB, BLOCK), axis=0)
            )
        cov_total = jnp.sum((cov_sq[:, :half] + cov_sq[:, half:]).reshape(TILE // SUB, SUB, BLOCK), axis=0)
        new_taken.append(taken[blocks] + cov_total)
        line = jnp.sum(total, axis=1, keepdims=True)
        for h in range(half_tiles):
            spread = jnp.where(diagonal, line[h * BLOCK : (h + 1) * BLOCK, :], 0.0)
            where = pl.ds(t * half_tiles + h, 1)
            resid_ref[where, :] = jnp.sum(spread, axis=0, keepdims=True)
        return tuple(new_taken)

    zero = jnp.zeros((SUB, BLOCK), jnp.float32)
    taken = lax.fori_loop(0, local_rows // TILE, tile_step, (zero,) * (blocks + 1))
    for slot in range(2):
        tile = local_rows // TILE - 2 + slot
        at = pl.ds(tile * TILE, TILE)
        pltpu.make_async_copy(tile_ref.at[tile % 2], out_hbm.at[at, :], store_sem.at[tile % 2]).wait()

    amplitude, noise = feat_ref[3:4, :], feat_ref[4:5, :]
    base = amplitude * amplitude + noise
    total = jnp.sum(taken[blocks]) + jnp.sum(base)
    resid_ref[...] += jnp.concatenate(
        [base[:, t * BLOCK : (t + 1) * BLOCK] for t in range(local_rows // BLOCK)], axis=0
    )
    lanes = lax.broadcasted_iota(jnp.int32, sums_ref.shape, 1)
    sums = jnp.zeros(sums_ref.shape, jnp.float32)
    for b in range(blocks):
        total = total - jnp.sum(taken[b])
        sums = jnp.where(lanes == b, total, sums)
    sums_ref[...] = sums


def broadcast_over(value, axes, count):
    copies = jnp.broadcast_to(value[None], (count,) + value.shape)
    return lax.all_to_all(copies, axes, 0, 0, tiled=True)


def local(locations, amplitude, noise, covariates, pivot_owner, pivot_offset):
    device_id = lax.axis_index(AXES)
    core = lax.axis_index("c")
    blocks_total, block_width = pivot_owner.shape
    pivots = blocks_total * block_width
    cov_width = covariates.shape[1]
    half = cov_width // 2
    local_rows = locations.shape[1]
    sizes = [lax.axis_size(name) for name in AXES]
    devices = sizes[0] * sizes[1] * sizes[2] * sizes[3]
    slots = CAP * blocks_total
    column = sizes[0] * sizes[3]
    planes = sizes[1] * sizes[2]

    same = pivot_owner[:, :, None] == pivot_owner[:, None, :]
    before = lax.iota(jnp.int32, block_width)[None, :] < lax.iota(jnp.int32, block_width)[:, None]
    rank = jnp.sum(jnp.where(same & before[None], 1, 0), axis=2)
    slot = (rank + CAP * lax.iota(jnp.int32, blocks_total)[:, None]).reshape(-1)
    owner = pivot_owner.reshape(-1)
    offset = pivot_offset.reshape(-1)
    here = (owner == device_id)[None, :] & (slot[None, :] == lax.iota(jnp.int32, slots)[:, None])
    my_offset = jnp.sum(jnp.where(here, offset[None, :], 0), axis=1)
    features = jnp.concatenate(
        [
            covariates[my_offset],
            locations[:, my_offset].T,
            amplitude[my_offset][:, None],
            noise[my_offset][:, None],
            jnp.zeros((slots, 123), jnp.float32),
        ],
        axis=1,
    )

    gathered = broadcast_over(features, ("z", "c"), column)
    gathered = gathered.reshape(column, blocks_total, CAP, -1).transpose(1, 0, 2, 3)
    gathered = gathered.reshape(column * slots, -1)
    cov_half = jnp.where(core == 0, gathered[:, :half], gathered[:, half:cov_width])
    message = jnp.concatenate([cov_half, gathered[:, cov_width : cov_width + 8].T], axis=0)
    mine = broadcast_over(message, ("x", "y"), planes)
    other = lax.ppermute(mine, "c", [(0, 1), (1, 0)])

    own_c = pivot_owner % sizes[3]
    chip = pivot_owner // sizes[3]
    place = (chip % planes) * (column * CAP) + ((chip // planes) * sizes[3] + own_c) * CAP + rank
    match = jnp.where(owner == device_id, offset, -1)[None, :]
    feat = jnp.concatenate(
        [locations, amplitude[None], noise[None], jnp.zeros((3, local_rows), jnp.float32)], axis=0
    )
    vmem = pl.BlockSpec(memory_space=pltpu.VMEM)
    hbm = pl.BlockSpec(memory_space=pl.ANY)
    factor, resid, sums = pl.pallas_call(
        main_kernel,
        out_shape=(
            jax.ShapeDtypeStruct((local_rows, pivots), jnp.float32),
            jax.ShapeDtypeStruct((local_rows // BLOCK, BLOCK), jnp.float32),
            jax.ShapeDtypeStruct((devices, BLOCK), jnp.float32),
        ),
        in_specs=[vmem, vmem, vmem, vmem, pl.BlockSpec(memory_space=pltpu.SMEM), vmem, hbm],
        out_specs=(hbm, vmem, vmem),
        scratch_shapes=[
            pltpu.VMEM((local_rows, cov_width), jnp.float32),
            pltpu.VMEM((pivots, cov_width), jnp.float32),
            pltpu.VMEM((SUB, pivots), jnp.float32),
            pltpu.VMEM((pivots, pivots), jnp.float32),
            pltpu.VMEM((BLOCK, pivots), jnp.float32),
            pltpu.VMEM((local_rows, SUB), jnp.float32),
            pltpu.VMEM((2, TILE, pivots), jnp.float32),
            pltpu.SemaphoreType.DMA,
            pltpu.SemaphoreType.DMA((2,)),
        ],
        compiler_params=pltpu.CompilerParams(vmem_limit_bytes=40 << 20),
        name="factor_rows",
    )(mine, other, place.T, match, core[None].astype(jnp.int32), feat, covariates)

    all_sums = lax.all_to_all(sums, AXES, 0, 0, tiled=True)
    mean_residual = jnp.sum(all_sums, axis=0)[:blocks_total] / float(local_rows * devices)
    weights = resid.reshape(-1) / mean_residual[blocks_total - 1]
    return (factor, weights, mean_residual)


def solution(mesh):
    named = Mesh(mesh.devices.reshape(8, 4, 4, 2), AXES)
    return jax.shard_map(
        local,
        mesh=named,
        in_specs=(P(None, AXES), P(AXES), P(AXES), P(AXES, None), P(), P()),
        out_specs=(P(AXES, None), P(AXES), P()),
        check_vma=False,
    )
```

```python
import jax
import jax.numpy as jnp
from jax import lax
from jax.experimental import pallas as pl
from jax.experimental.pallas import tpu as pltpu
from jax.sharding import Mesh
from jax.sharding import PartitionSpec as P

LENGTH_SCALE = 0.3
CAP = 2
AXES = ("z", "x", "y", "c")
HIGHEST = lax.Precision.HIGHEST
BLOCK = 128
PANEL = 16
SUB = 8
TILE = 256
FEW = 56


def dot(left, right, dims):
    return lax.dot_general(
        left, right, (dims, ((), ())), precision=HIGHEST, preferred_element_type=jnp.float32
    )


def panel_inverse(low, high):
    sub = lax.broadcasted_iota(jnp.int32, (SUB, BLOCK), 0)
    low, high = list(low), list(high)
    root_low = jnp.zeros((SUB, BLOCK), jnp.float32)
    root_high = root_low
    for k in range(PANEL):
        if k < SUB:
            pivot = jnp.broadcast_to(low[k][k : k + 1, :], (SUB, BLOCK))
            inverse = pl.reciprocal(pivot, approx=True)
            take_low = jnp.where(sub > k, low[k], 0.0) * inverse
            take_high = high[k] * inverse
            across = high[k]
            root_low = jnp.where(sub == k, lax.rsqrt(pivot), root_low)
            for j in range(PANEL):
                if j < SUB and j != k:
                    entry = low[j][k : k + 1, :]
                    low[j] = low[j] - take_low * entry
                    high[j] = high[j] - take_high * entry
                elif j >= SUB:
                    high[j] = high[j] - take_high * across[j - SUB : j - SUB + 1, :]
            low[k] = jnp.where(sub == k, 1.0, -take_low)
            high[k] = -take_high
        else:
            s = k - SUB
            pivot = jnp.broadcast_to(high[k][s : s + 1, :], (SUB, BLOCK))
            inverse = pl.reciprocal(pivot, approx=True)
            take_high = jnp.where(sub > s, high[k], 0.0) * inverse
            root_high = jnp.where(sub == s, lax.rsqrt(pivot), root_high)
            for j in range(PANEL):
                if j != k:
                    high[j] = high[j] - take_high * high[j][s : s + 1, :]
            high[k] = jnp.where(sub == s, 1.0, -take_high)
    return [low[j] * root_low for j in range(SUB)], [high[j] * root_high for j in range(PANEL)]


def tree_sum(terms):
    while len(terms) > 1:
        pairs = [terms[i] + terms[i + 1] for i in range(0, len(terms) - 1, 2)]
        terms = pairs + terms[2 * len(pairs) :]
    return terms[0]


def block_inverse(rows):
    lane = lax.broadcasted_iota(jnp.int32, (SUB, BLOCK), 1)
    sub = lax.broadcasted_iota(jnp.int32, (SUB, BLOCK), 0)
    rows = list(rows)
    out = [None] * len(rows)
    for panel in range(BLOCK // PANEL):
        first = PANEL * panel
        at = 2 * panel

        def splat(piece, j):
            return jnp.broadcast_to(piece[:, first + j : first + j + 1], (SUB, BLOCK))

        rest = range(at + 2, len(rows))
        near, far = rest[:2], rest[2:]
        low = [splat(rows[at], j) for j in range(SUB)]
        high = [splat(rows[at + 1], j) for j in range(PANEL)]
        coef = {r: [splat(rows[r], j) for j in range(PANEL)] for r in near}
        inv_low, inv_high = panel_inverse(low, high)
        in_panel = (lane >= first) & (lane < first + PANEL)
        top = jnp.where(in_panel, jnp.where(lane - first == sub, 1.0, 0.0), rows[at])
        bottom = jnp.where(in_panel, jnp.where(lane - first - SUB == sub, 1.0, 0.0), rows[at + 1])
        entries = [top[j : j + 1, :] for j in range(SUB)] + [bottom[j : j + 1, :] for j in range(SUB)]
        new_low = tree_sum([inv_low[j] * entries[j] for j in range(SUB)])
        new_high = tree_sum([inv_high[j] * entries[j] for j in range(PANEL)])
        out[at] = jnp.where(lane <= first + sub, new_low, 0.0)
        out[at + 1] = jnp.where(lane <= first + SUB + sub, new_high, 0.0)
        if len(near):
            weights = []
            for j in range(PANEL):
                term = inv_high[j] * new_high
                if j < SUB:
                    term = term + inv_low[j] * new_low
                weights.append(jnp.sum(term, axis=0, keepdims=True))
            for r in near:
                piece = jnp.where(in_panel, 0.0, rows[r])
                for j in range(PANEL):
                    piece = piece - coef[r][j] * weights[j]
                rows[r] = piece
        if len(far):
            spread = [jnp.zeros((size, BLOCK), jnp.float32) for size in (first, BLOCK - first - PANEL)]
            spread = ([spread[0]] if first else []) + weights + [spread[1]]
            change = dot(
                jnp.concatenate([rows[r] for r in far], axis=0),
                jnp.concatenate(spread, axis=0),
                ((1,), (0,)),
            )
            for i, r in enumerate(far):
                rows[r] = jnp.where(in_panel, 0.0, rows[r]) - change[SUB * i : SUB * (i + 1)]
    return out


def parts_of(value):
    high = value.astype(jnp.bfloat16)
    rest = value - high.astype(jnp.float32)
    middle = rest.astype(jnp.bfloat16)
    low = (rest - middle.astype(jnp.float32)).astype(jnp.bfloat16)
    return high, middle, low


def product(left, right, dims):
    return lax.dot_general(left, right, (dims, ((), ())), preferred_element_type=jnp.float32)


def dot_parts(left, right, dims):
    high, middle, low = left
    other_high, other_middle, other_low = right
    one = jnp.concatenate([low, high, middle, middle, high, high], axis=dims[0][0])
    two = jnp.concatenate(
        [other_high, other_low, other_middle, other_high, other_middle, other_high], axis=dims[1][0]
    )
    return product(one, two, dims)


def pick_rows(pick, value, dims):
    high, middle, low = parts_of(value)
    return product(pick, high, dims) + product(pick, middle, dims) + product(pick, low, dims)


def matern(cols, rows, col_scale, row_scale):
    dist_sq = None
    for axis_id in range(3):
        offset = cols[axis_id] - rows[axis_id]
        dist_sq = offset * offset if dist_sq is None else dist_sq + offset * offset
    scaled = dist_sq * lax.rsqrt(jnp.maximum(dist_sq, 1e-30))
    shape_term = (1.0 + scaled + dist_sq * (1.0 / 3.0)) * jnp.exp(-scaled)
    return col_scale * row_scale * shape_term


def prep_kernel(
    me_ref,
    owner_hbm,
    offset_hbm,
    points_hbm,
    amp_hbm,
    noise_hbm,
    cov_hbm,
    keep_ref,
    send_ref,
    owner_ref,
    offset_ref,
    points_ref,
    amp_ref,
    noise_ref,
    rows_ref,
    sem,
    load_sem,
):
    pairs = (
        (owner_hbm, owner_ref),
        (offset_hbm, offset_ref),
        (points_hbm, points_ref),
        (amp_hbm, amp_ref),
        (noise_hbm, noise_ref),
    )
    loads = [pltpu.make_async_copy(*pair, load_sem.at[i]) for i, pair in enumerate(pairs)]
    for load in loads:
        load.start()
    me = me_ref[0]
    core = lax.rem(me, 2)
    blocks, width = owner_ref.shape
    slots = CAP * blocks
    for load in loads:
        load.wait()
    lane = lax.broadcasted_iota(jnp.int32, (blocks, width), 1).astype(jnp.float32)
    block = lax.broadcasted_iota(jnp.int32, (blocks, width), 0)
    mine = owner_ref[...] == me
    offset = offset_ref[...].astype(jnp.float32)
    first = jnp.min(jnp.where(mine, lane, 1e4), axis=1, keepdims=True)
    last = jnp.max(jnp.where(mine, lane, -1.0), axis=1, keepdims=True)
    chosen = [jnp.where(mine & (lane == at), offset, 0.0) for at in (first, last)]
    copies = []
    slot_row = lax.broadcasted_iota(jnp.int32, (slots, 1), 0)
    offsets = jnp.zeros((slots, 1), jnp.int32)
    for s in range(slots):
        value = jnp.sum(jnp.where(block == s // CAP, chosen[s % CAP], 0.0)).astype(jnp.int32)
        copy = pltpu.make_async_copy(cov_hbm.at[pl.ds(value, 1), :], rows_ref.at[pl.ds(s, 1), :], sem.at[s])
        copy.start()
        copies.append(copy)
        offsets = jnp.where(slot_row == s, value, offsets)
    local_rows = points_ref.shape[1]
    hit = lax.broadcasted_iota(jnp.int32, (slots, local_rows), 1) == offsets
    sources = [points_ref[i : i + 1, :] for i in range(3)] + [amp_ref[...], noise_ref[...]]
    sub = lax.broadcasted_iota(jnp.int32, (SUB, BLOCK), 0)
    diagonal = sub == lax.broadcasted_iota(jnp.int32, (SUB, BLOCK), 1)
    scalars = jnp.zeros((SUB, BLOCK), jnp.float32)
    for i, source in enumerate(sources):
        column = jnp.sum(jnp.where(hit, source, 0.0), axis=1, keepdims=True)
        line = jnp.sum(jnp.where(diagonal, column, 0.0), axis=0, keepdims=True)
        scalars = jnp.where(sub == i, line, scalars)
    for copy in copies:
        copy.wait()
    half = rows_ref.shape[1] // 2
    left, right = rows_ref[:, :half], rows_ref[:, half:]
    keep_ref[:slots, :] = jnp.where(core == 0, left, right)
    send_ref[:slots, :] = jnp.where(core == 0, right, left)
    keep_ref[slots:, :] = scalars
    send_ref[slots:, :] = scalars


def pair_kernel(me_ref, keep_ref, got_ref, out_ref):
    core = lax.rem(me_ref[0], 2)
    keep, got = keep_ref[...], got_ref[...]
    one = jnp.where(core == 0, keep, got)
    two = jnp.where(core == 0, got, keep)
    lane = lax.broadcasted_iota(jnp.int32, (SUB, BLOCK), 1)
    scalars = jnp.where(lane < SUB, one[SUB:], pltpu.roll(two[SUB:], SUB, 1))
    for i in range(out_ref.shape[0]):
        out_ref[i, :SUB] = one[:SUB]
        out_ref[i, SUB : 2 * SUB] = two[:SUB]
        out_ref[i, 2 * SUB :] = scalars


def aux_kernel(
    me_ref,
    owner_ref,
    offset_ref,
    points_ref,
    amp_ref,
    noise_ref,
    cov_ref,
    high_ref,
    middle_ref,
    low_ref,
    feat_ref,
    base_ref,
    info_ref,
    match_ref,
    comb_ref,
    most_ref,
):
    me = me_ref[0]
    blocks, width = owner_ref.shape
    local_rows, cov_width = cov_ref.shape
    half = cov_width // 2
    owner = owner_ref[...]
    padded = jnp.concatenate([owner, jnp.zeros((SUB - blocks, width), jnp.int32)], axis=0)
    owner_t = padded.astype(jnp.float32).T.astype(jnp.int32)
    sub = lax.broadcasted_iota(jnp.int32, (width, width), 0)
    lane = lax.broadcasted_iota(jnp.int32, (width, width), 1)
    xy = (owner >> 1) & 15
    xy_t = (owner_t >> 1) & 15
    my_xy = lax.rem(lax.div(me, 2), 16)
    seats = []
    candidates = []
    infos = []
    for b in range(blocks):
        count = jnp.zeros((1, width), jnp.float32)
        for earlier in range(b + 1):
            same = xy_t[:, earlier : earlier + 1] == xy[b : b + 1, :]
            if earlier == b:
                same = same & (sub < lane)
            count = count + jnp.sum(jnp.where(same, 1.0, 0.0), axis=0, keepdims=True)
        twin = (owner_t[:, b : b + 1] == owner[b : b + 1, :]) & (sub < lane)
        rank = jnp.sum(jnp.where(twin, 1.0, 0.0), axis=0, keepdims=True).astype(jnp.int32)
        count = count.astype(jnp.int32)
        row = owner[b : b + 1, :]
        seats.append(jnp.where(xy[b : b + 1, :] == my_xy, count, -1))
        candidates.append((row >> 5) * 16 + (row & 1) * SUB + CAP * b + rank)
        infos.append(count)
    info_ref[:blocks, :] = xy.astype(jnp.float32)
    counts = jnp.concatenate(infos, axis=0).astype(jnp.float32)
    info_ref[blocks:, :] = counts
    most_ref[0] = jnp.max(counts).astype(jnp.int32) + 1
    match = jnp.where(owner == me, offset_ref[...], -1)
    match_ref[...] = jnp.concatenate([match[b : b + 1, :] for b in range(blocks)], axis=1)
    seat = jnp.concatenate(seats, axis=1)
    candidate = jnp.concatenate(candidates, axis=1)
    ids = lax.broadcasted_iota(jnp.int32, (BLOCK, blocks * width), 0)
    seat_hit = (ids == seat).astype(jnp.float32).astype(jnp.bfloat16)
    candidate_hit = (ids == candidate).astype(jnp.float32).astype(jnp.bfloat16)
    comb_ref[...] = product(seat_hit, candidate_hit, ((1,), (1,)))

    feat_ref[:3, :] = points_ref[...]
    feat_ref[3:4, :] = amp_ref[...]
    feat_ref[4:5, :] = noise_ref[...]
    feat_ref[5:, :] = jnp.zeros((3, local_rows), jnp.float32)
    diagonal = sub == lane

    def step(t, carry):
        at = pl.ds(pl.multiple_of(t * BLOCK, BLOCK), BLOCK)
        cov = cov_ref[at, :]
        high, middle, low = parts_of(cov)
        high_ref[at, :] = high
        middle_ref[at, :] = middle
        low_ref[at, :] = low
        squares = cov * cov
        line = jnp.sum(squares[:, :half] + squares[:, half:], axis=1, keepdims=True)
        total = jnp.sum(jnp.where(diagonal, line, 0.0), axis=0, keepdims=True)
        amplitude = amp_ref[:, at]
        base_ref[pl.ds(t, 1), :] = amplitude * amplitude + noise_ref[:, at] + total
        return carry

    lax.fori_loop(0, local_rows // BLOCK, step, 0)


def seat_kernel(comb_ref, got_ref, out_ref):
    chips = got_ref.shape[0]
    per_chip = got_ref.shape[1] - SUB
    seats = out_ref.shape[1] - SUB
    comb = comb_ref[...].astype(jnp.bfloat16)
    rows = jnp.concatenate([got_ref[z, :per_chip, :] for z in range(chips)], axis=0)
    packed = pick_rows(comb[: -(-seats // 16) * 16], rows, ((1,), (0,)))[:seats]
    lane = lax.broadcasted_iota(jnp.int32, (SUB, BLOCK), 1)
    scalars = jnp.zeros((SUB, BLOCK), jnp.float32)
    for z in range(chips):
        piece = got_ref[z, per_chip:, :]
        piece = pltpu.roll(piece, z * per_chip, 1) if z else piece
        scalars = jnp.where(lane // per_chip == z, piece, scalars)
    high, middle, low = parts_of(scalars)
    dims = ((1,), (1,))
    seated = product(high, comb, dims) + product(middle, comb, dims) + product(low, comb, dims)
    for i in range(out_ref.shape[0]):
        out_ref[i, :seats, :] = packed
        out_ref[i, seats:, :] = seated


def main_kernel(
    me_ref,
    mine_ref,
    other_ref,
    info_ref,
    match_ref,
    feat_ref,
    base_ref,
    high_hbm,
    middle_hbm,
    low_hbm,
    out_hbm,
    resid_ref,
    sums_ref,
    cov_high,
    cov_middle,
    cov_low,
    table_high,
    table_middle,
    table_low,
    kernel_high,
    kernel_middle,
    kernel_low,
    scal_ref,
    z_ref,
    r_ref,
    col_ref,
    tile_ref,
    load_sem,
    store_sem,
):
    core = lax.rem(me_ref[0], 2)
    pivots = z_ref.shape[0]
    local_rows, cov_width = cov_high.shape
    planes, plane_rows, half = mine_ref.shape
    seats = plane_rows - SUB
    blocks = pivots // BLOCK
    loads = [
        pltpu.make_async_copy(source, target, load_sem.at[i])
        for i, (source, target) in enumerate(
            ((high_hbm, cov_high), (middle_hbm, cov_middle), (low_hbm, cov_low))
        )
    ]
    for load in loads:
        load.start()
    nt = ((1,), (1,))

    scale = (5.0**0.5) / LENGTH_SCALE
    candidates = planes * plane_rows
    mine = mine_ref[...].reshape(candidates, half)
    other = other_ref[...].reshape(candidates, half)
    both = jnp.concatenate([jnp.where(core == 0, mine, other), jnp.where(core == 0, other, mine)], axis=1)
    both_parts = parts_of(both)
    packed = BLOCK // plane_rows if BLOCK % plane_rows == 0 else 1
    stride = BLOCK // packed
    lane = lax.broadcasted_iota(jnp.int32, (SUB, BLOCK), 1)
    lines = []
    for q in range(planes // packed):
        line = mine_ref[q * packed, seats:, :]
        for t in range(1, packed):
            piece = pltpu.roll(mine_ref[q * packed + t, seats:, :], t * stride, 1)
            line = jnp.where(lane // stride == t, piece, line)
        lines.append(line)
    line_parts = parts_of(jnp.concatenate(lines, axis=1))
    info_t = info_ref[...].T
    for b in range(blocks):
        here = pl.ds(b * BLOCK, BLOCK)
        xy, seat = info_t[:, b : b + 1], info_t[:, blocks + b : blocks + b + 1]
        place = (xy * plane_rows + seat).astype(jnp.int32)
        ids = lax.broadcasted_iota(jnp.int32, (BLOCK, candidates), 1)
        pick = (ids == place).astype(jnp.float32).astype(jnp.bfloat16)
        for part, table in zip(both_parts, (table_high, table_middle, table_low)):
            table[here, :] = product(pick, part, ((1,), (0,))).astype(jnp.bfloat16)
        if packed * plane_rows == BLOCK:
            line_pick = pick
        else:
            place = (xy * stride + seat).astype(jnp.int32)
            ids = lax.broadcasted_iota(jnp.int32, (BLOCK, planes * stride), 1)
            line_pick = (ids == place).astype(jnp.float32).astype(jnp.bfloat16)
        scal_ref[:, here] = (
            product(line_parts[0], line_pick, nt)
            + product(line_parts[1], line_pick, nt)
            + product(line_parts[2], line_pick, nt)
        )

    for t in range(local_rows // BLOCK):
        at = pl.ds(t * BLOCK, BLOCK)
        col_ref[at, :] = feat_ref[:, at].T
    piv = scal_ref[...]
    piv_rows = [piv[i : i + 1, :] * scale for i in range(3)]
    piv_scale, piv_noise = piv[3:4, :], piv[4:5, :]

    for b in range(blocks):
        here = pl.ds(b * BLOCK, BLOCK)
        right = slice(b * BLOCK, pivots)
        cols = scal_ref[:, here].T
        piece = matern(
            [cols[:, i : i + 1] * scale for i in range(3)],
            [row[:, right] for row in piv_rows],
            cols[:, 3:4],
            piv_scale[:, right],
        )
        same = lax.broadcasted_iota(jnp.int32, (BLOCK, 1), 0) == lax.broadcasted_iota(
            jnp.int32, (1, pivots - b * BLOCK), 1
        )
        piece = piece + jnp.where(same, piv_noise[:, right], 0.0)
        left_parts = [table[here, :] for table in (table_high, table_middle, table_low)]
        right_parts = [table[right, :] for table in (table_high, table_middle, table_low)]
        z_ref[here, right] = piece + dot_parts(left_parts, right_parts, nt)
        if b:
            z_ref[here, : b * BLOCK] = jnp.zeros((BLOCK, b * BLOCK), jnp.float32)
    for load in loads:
        load.wait()
    match = match_ref[...]

    def kernel_tile(t):
        at = pl.ds(pl.multiple_of(t * TILE, TILE), TILE)
        cols = col_ref[at, :]
        kernel = matern([cols[:, i : i + 1] * scale for i in range(3)], piv_rows, cols[:, 3:4], piv_scale)
        row_ids = lax.broadcasted_iota(jnp.int32, (TILE, 1), 0) + t * TILE
        kernel = kernel + jnp.where(row_ids == match, cols[:, 4:5], 0.0)
        cov = [part[at, :] for part in (cov_high, cov_middle, cov_low)]
        kernel = kernel + dot_parts(cov, (table_high[...], table_middle[...], table_low[...]), nt)
        for part, target in zip(parts_of(kernel), (kernel_high, kernel_middle, kernel_low)):
            target[at, :] = part

    per_step = local_rows // TILE // blocks

    def step(b, carry):
        at = pl.ds(pl.multiple_of(b * BLOCK, BLOCK), BLOCK)
        pieces = [
            z_ref[pl.ds(pl.multiple_of(b * BLOCK + SUB * i, SUB), SUB), at]
            for i in range(BLOCK // SUB)
        ]
        inverse = jnp.concatenate(block_inverse(pieces), axis=0)
        for i in range(per_step):
            kernel_tile(b * per_step + i)
        r_ref[...] = dot(inverse, z_ref[at, :], ((1,), (0,)))
        r_ref[:, at] = inverse
        z_ref[:, at] = jnp.zeros((pivots, BLOCK), jnp.float32)
        row = r_ref[...]
        row_parts = parts_of(row)
        for later in range(1, blocks):
            there = slice(later * BLOCK, (later + 1) * BLOCK)

            @pl.when(later > b)
            def _():
                coef = [part[:, there] for part in row_parts]
                z_ref[there, :] -= dot_parts(coef, row_parts, ((0,), (0,)))

        z_ref[at, :] = row
        return carry

    lax.fori_loop(0, blocks, step, 0)

    diagonal = lax.broadcasted_iota(jnp.int32, (BLOCK, BLOCK), 0) == lax.broadcasted_iota(
        jnp.int32, (BLOCK, BLOCK), 1
    )
    left = pivots // 2
    half_tiles = TILE // BLOCK
    tiles = local_rows // TILE
    inverse_parts = parts_of(z_ref[...])
    for part, target in zip(inverse_parts, (table_high, table_middle, table_low)):
        target[:, :] = part[:, :left]
    late = [part[left:, left:] for part in inverse_parts]

    def tile_step(t, taken):
        at = pl.ds(pl.multiple_of(t * TILE, TILE), TILE)
        slot = lax.rem(t, 2)

        @pl.when(t >= 2)
        def _():
            pltpu.make_async_copy(tile_ref.at[slot], out_hbm.at[at, :], store_sem.at[slot]).wait()

        kernels = [part[at, :] for part in (kernel_high, kernel_middle, kernel_low)]
        early = [part[:, :left] for part in kernels]
        first = dot_parts(early, [table[:left, :] for table in (table_high, table_middle, table_low)], nt)
        second = dot_parts(early, [table[left:, :] for table in (table_high, table_middle, table_low)], nt)
        second = second + dot_parts([part[:, left:] for part in kernels], late, nt)
        tile_ref[slot, :, :left] = first
        tile_ref[slot, :, left:] = second
        pltpu.make_async_copy(tile_ref.at[slot], out_hbm.at[at, :], store_sem.at[slot]).start()
        total = jnp.zeros((TILE, BLOCK), jnp.float32)
        new_taken = []
        for b in range(blocks):
            source = first if b * BLOCK < left else second
            piece = source[:, (b * BLOCK) % left : (b * BLOCK) % left + BLOCK]
            square = piece * piece
            total = total + square
            new_taken.append(taken[b] + jnp.sum(square.reshape(TILE // SUB, SUB, BLOCK), axis=0))
        line = jnp.sum(total, axis=1, keepdims=True)
        for h in range(half_tiles):
            spread = jnp.where(diagonal, line[h * BLOCK : (h + 1) * BLOCK, :], 0.0)
            where = pl.ds(t * half_tiles + h, 1)
            resid_ref[where, :] = base_ref[where, :] - jnp.sum(spread, axis=0, keepdims=True)
        return tuple(new_taken)

    zero = jnp.zeros((SUB, BLOCK), jnp.float32)
    taken = lax.fori_loop(0, tiles, tile_step, (zero,) * blocks)
    for tile in (tiles - 2, tiles - 1):
        at = pl.ds(tile * TILE, TILE)
        pltpu.make_async_copy(tile_ref.at[tile % 2], out_hbm.at[at, :], store_sem.at[tile % 2]).wait()

    total = jnp.sum(base_ref[...])
    lanes = lax.broadcasted_iota(jnp.int32, sums_ref.shape, 1)
    sums = jnp.zeros(sums_ref.shape, jnp.float32)
    for b in range(blocks):
        total = total - jnp.sum(taken[b])
        sums = jnp.where(lanes == b, total, sums)
    sums_ref[...] = sums


def last_kernel(sums_ref, resid_ref, weights_ref, mean_ref):
    devices, _, width = sums_ref.shape
    rows = resid_ref.shape[0] * resid_ref.shape[1] * devices
    total = jnp.sum(sums_ref[...].reshape(devices, width), axis=0, keepdims=True)
    mean = total * (1.0 / rows)
    count = mean_ref.shape[1]
    mean_ref[...] = mean[:, :count]
    weights_ref[...] = resid_ref[...] / mean[:, count - 1 : count]


def shape(dims, dtype=jnp.float32):
    return jax.ShapeDtypeStruct(dims, dtype)


VMEM = pl.BlockSpec(memory_space=pltpu.VMEM)
SMEM = pl.BlockSpec(memory_space=pltpu.SMEM)
ANY = pl.BlockSpec(memory_space=pl.ANY)
PARAMS = pltpu.CompilerParams(vmem_limit_bytes=40 << 20)


def prep(me, owner, offset, points, amp, noise, cov):
    rows = 2 * CAP * owner.shape[0]
    return pl.pallas_call(
        prep_kernel,
        out_shape=(shape((rows, BLOCK)), shape((rows, BLOCK))),
        in_specs=[SMEM] + [ANY] * 6,
        out_specs=(VMEM, VMEM),
        scratch_shapes=[pltpu.VMEM(value.shape, value.dtype) for value in (owner, offset, points, amp, noise)]
        + [
            pltpu.VMEM((rows // 2, cov.shape[1]), jnp.float32),
            pltpu.SemaphoreType.DMA((rows // 2,)),
            pltpu.SemaphoreType.DMA((5,)),
        ],
        compiler_params=pltpu.CompilerParams(vmem_limit_bytes=60 << 20),
        name="prep",
    )(me, owner, offset, points, amp, noise, cov)


def pair(me, keep, got, copies):
    return pl.pallas_call(
        pair_kernel,
        out_shape=shape((copies, 24, BLOCK)),
        in_specs=[SMEM, VMEM, VMEM],
        out_specs=VMEM,
        compiler_params=PARAMS,
        name="pair",
    )(me, keep, got)


def aux(me, owner, offset, points, amp, noise, cov):
    rows, width = cov.shape
    return pl.pallas_call(
        aux_kernel,
        out_shape=(
            shape((rows, width), jnp.bfloat16),
            shape((rows, width), jnp.bfloat16),
            shape((rows, width), jnp.bfloat16),
            shape((SUB, rows)),
            shape((rows // BLOCK, BLOCK)),
            shape((SUB, BLOCK)),
            shape((1, owner.size), jnp.int32),
            shape((BLOCK, BLOCK)),
            shape((1,), jnp.int32),
        ),
        in_specs=[SMEM] + [VMEM] * 6,
        out_specs=(VMEM,) * 8 + (SMEM,),
        compiler_params=PARAMS,
        cost_estimate=pl.CostEstimate(flops=10**8, bytes_accessed=6 << 20, transcendentals=0),
        name="aux",
    )(me, owner, offset, points, amp, noise, cov)


def seat(comb, got, copies, seats):
    return pl.pallas_call(
        seat_kernel,
        out_shape=shape((copies, seats + SUB, BLOCK)),
        in_specs=[VMEM, VMEM],
        out_specs=VMEM,
        compiler_params=PARAMS,
        name="seat",
    )(comb, got)


def main(me, mine, other, info, match, feat, base, high, middle, low, devices):
    rows, width = high.shape
    pivots = match.shape[1]
    bf = jnp.bfloat16
    return pl.pallas_call(
        main_kernel,
        out_shape=(shape((rows, pivots)), shape((rows // BLOCK, BLOCK)), shape((devices, BLOCK))),
        in_specs=[SMEM] + [VMEM] * 6 + [ANY] * 3,
        out_specs=(ANY, VMEM, VMEM),
        scratch_shapes=[pltpu.VMEM((rows, width), bf)] * 3
        + [pltpu.VMEM((pivots, width), bf)] * 3
        + [pltpu.VMEM((rows, pivots), bf)] * 3
        + [
            pltpu.VMEM((SUB, pivots), jnp.float32),
            pltpu.VMEM((pivots, pivots), jnp.float32),
            pltpu.VMEM((BLOCK, pivots), jnp.float32),
            pltpu.VMEM((rows, SUB), jnp.float32),
            pltpu.VMEM((2, TILE, pivots), jnp.float32),
            pltpu.SemaphoreType.DMA((3,)),
            pltpu.SemaphoreType.DMA((2,)),
        ],
        compiler_params=PARAMS,
        name="factor_rows",
    )(me, mine, other, info, match, feat, base, high, middle, low)


def last(sums, resid, blocks):
    return pl.pallas_call(
        last_kernel,
        out_shape=(shape(resid.shape), shape((1, blocks))),
        in_specs=[VMEM, VMEM],
        out_specs=(VMEM, VMEM),
        compiler_params=PARAMS,
        name="last",
    )(sums, resid)


def local(locations, amplitude, noise, covariates, pivot_owner, pivot_offset):
    me = lax.axis_index(AXES).astype(jnp.int32)[None]
    blocks = pivot_owner.shape[0]
    sizes = [lax.axis_size(name) for name in AXES]
    devices = sizes[0] * sizes[1] * sizes[2] * sizes[3]
    swap = [(0, 1), (1, 0)]
    amp, nugget = amplitude[None], noise[None]
    args = (me, pivot_owner, pivot_offset, locations, amp, nugget, covariates)

    keep, send = prep(*args)
    got = lax.ppermute(send, "c", swap)
    column = lax.all_to_all(pair(me, keep, got, sizes[0]), "z", 0, 0, tiled=True)
    high, middle, low, feat, base, info, match, comb, most = aux(*args)

    def rest(seats):
        def run(column, comb, info, match, feat, base, high, middle, low):
            message = seat(comb, column, sizes[1] * sizes[2], seats)
            mine = lax.all_to_all(message, ("x", "y"), 0, 0, tiled=True)
            other = lax.ppermute(mine, "c", swap)
            return main(me, mine, other, info, match, feat, base, high, middle, low, devices)

        return run

    operands = (column, comb, info, match, feat, base, high, middle, low)
    if FEW:
        factor, resid, sums = lax.cond(most[0] <= FEW, rest(FEW), rest(BLOCK), *operands)
    else:
        factor, resid, sums = rest(BLOCK)(*operands)
    all_sums = lax.all_to_all(sums[:, None, :], AXES, 0, 0, tiled=True)
    weights, mean_residual = last(all_sums, resid, blocks)
    return (factor, weights.reshape(-1), mean_residual.reshape(-1))


def solution(mesh):
    named = Mesh(mesh.devices.reshape(8, 4, 4, 2), AXES)
    return jax.shard_map(
        local,
        mesh=named,
        in_specs=(P(None, AXES), P(AXES), P(AXES), P(AXES, None), P(), P()),
        out_specs=(P(AXES, None), P(AXES), P()),
        check_vma=False,
    )
```

```python
import jax
import jax.numpy as jnp
from jax import lax
from jax.experimental import pallas as pl
from jax.experimental.pallas import tpu as pltpu
from jax.sharding import Mesh
from jax.sharding import PartitionSpec as P

LENGTH_SCALE = 0.3
CAP = 2
AXES = ("z", "x", "y", "c")
HIGHEST = lax.Precision.HIGHEST
BLOCK = 128
PANEL = 16
SUB = 8
TILE = 256
FEW = 56
WIDE = 512


def dot(left, right, dims):
    return lax.dot_general(
        left, right, (dims, ((), ())), precision=HIGHEST, preferred_element_type=jnp.float32
    )


def panel_inverse(low, high):
    sub = lax.broadcasted_iota(jnp.int32, (SUB, BLOCK), 0)
    low, high = list(low), list(high)
    root_low = jnp.zeros((SUB, BLOCK), jnp.float32)
    root_high = root_low
    for k in range(PANEL):
        if k < SUB:
            pivot = jnp.broadcast_to(low[k][k : k + 1, :], (SUB, BLOCK))
            inverse = pl.reciprocal(pivot, approx=True)
            take_low = jnp.where(sub > k, low[k], 0.0) * inverse
            take_high = high[k] * inverse
            across = high[k]
            root_low = jnp.where(sub == k, lax.rsqrt(pivot), root_low)
            for j in range(PANEL):
                if j < SUB and j != k:
                    entry = low[j][k : k + 1, :]
                    low[j] = low[j] - take_low * entry
                    high[j] = high[j] - take_high * entry
                elif j >= SUB:
                    high[j] = high[j] - take_high * across[j - SUB : j - SUB + 1, :]
            low[k] = jnp.where(sub == k, 1.0, -take_low)
            high[k] = -take_high
        else:
            s = k - SUB
            pivot = jnp.broadcast_to(high[k][s : s + 1, :], (SUB, BLOCK))
            inverse = pl.reciprocal(pivot, approx=True)
            take_high = jnp.where(sub > s, high[k], 0.0) * inverse
            root_high = jnp.where(sub == s, lax.rsqrt(pivot), root_high)
            for j in range(PANEL):
                if j != k:
                    high[j] = high[j] - take_high * high[j][s : s + 1, :]
            high[k] = jnp.where(sub == s, 1.0, -take_high)
    return [low[j] * root_low for j in range(SUB)], [high[j] * root_high for j in range(PANEL)]


def tree_sum(terms):
    while len(terms) > 1:
        pairs = [terms[i] + terms[i + 1] for i in range(0, len(terms) - 1, 2)]
        terms = pairs + terms[2 * len(pairs) :]
    return terms[0]


def block_inverse(rows):
    lane = lax.broadcasted_iota(jnp.int32, (SUB, BLOCK), 1)
    sub = lax.broadcasted_iota(jnp.int32, (SUB, BLOCK), 0)
    rows = list(rows)
    out = [None] * len(rows)
    for panel in range(BLOCK // PANEL):
        first = PANEL * panel
        at = 2 * panel

        def splat(piece, j):
            return jnp.broadcast_to(piece[:, first + j : first + j + 1], (SUB, BLOCK))

        rest = range(at + 2, len(rows))
        near, far = rest[:2], rest[2:]
        low = [splat(rows[at], j) for j in range(SUB)]
        high = [splat(rows[at + 1], j) for j in range(PANEL)]
        coef = {r: [splat(rows[r], j) for j in range(PANEL)] for r in near}
        inv_low, inv_high = panel_inverse(low, high)
        in_panel = (lane >= first) & (lane < first + PANEL)
        top = jnp.where(in_panel, jnp.where(lane - first == sub, 1.0, 0.0), rows[at])
        bottom = jnp.where(in_panel, jnp.where(lane - first - SUB == sub, 1.0, 0.0), rows[at + 1])
        entries = [top[j : j + 1, :] for j in range(SUB)] + [bottom[j : j + 1, :] for j in range(SUB)]
        new_low = tree_sum([inv_low[j] * entries[j] for j in range(SUB)])
        new_high = tree_sum([inv_high[j] * entries[j] for j in range(PANEL)])
        out[at] = jnp.where(lane <= first + sub, new_low, 0.0)
        out[at + 1] = jnp.where(lane <= first + SUB + sub, new_high, 0.0)
        if len(near):
            weights = []
            for j in range(PANEL):
                term = inv_high[j] * new_high
                if j < SUB:
                    term = term + inv_low[j] * new_low
                weights.append(jnp.sum(term, axis=0, keepdims=True))
            for r in near:
                piece = jnp.where(in_panel, 0.0, rows[r])
                for j in range(PANEL):
                    piece = piece - coef[r][j] * weights[j]
                rows[r] = piece
        if len(far):
            spread = [jnp.zeros((size, BLOCK), jnp.float32) for size in (first, BLOCK - first - PANEL)]
            spread = ([spread[0]] if first else []) + weights + [spread[1]]
            change = dot(
                jnp.concatenate([rows[r] for r in far], axis=0),
                jnp.concatenate(spread, axis=0),
                ((1,), (0,)),
            )
            for i, r in enumerate(far):
                rows[r] = jnp.where(in_panel, 0.0, rows[r]) - change[SUB * i : SUB * (i + 1)]
    return out


def parts_of(value):
    high = value.astype(jnp.bfloat16)
    rest = value - high.astype(jnp.float32)
    middle = rest.astype(jnp.bfloat16)
    low = (rest - middle.astype(jnp.float32)).astype(jnp.bfloat16)
    return high, middle, low


def product(left, right, dims):
    return lax.dot_general(left, right, (dims, ((), ())), preferred_element_type=jnp.float32)


def dot_parts(left, right, dims):
    high, middle, low = left
    other_high, other_middle, other_low = right
    one = jnp.concatenate([low, high, middle, middle, high, high], axis=dims[0][0])
    two = jnp.concatenate(
        [other_high, other_low, other_middle, other_high, other_middle, other_high], axis=dims[1][0]
    )
    return product(one, two, dims)


def pick_rows(pick, value, dims):
    high, middle, low = parts_of(value)
    return product(pick, high, dims) + product(pick, middle, dims) + product(pick, low, dims)


def matern(cols, rows, col_scale, row_scale):
    dist_sq = None
    for axis_id in range(3):
        offset = cols[axis_id] - rows[axis_id]
        dist_sq = offset * offset if dist_sq is None else dist_sq + offset * offset
    scaled = dist_sq * lax.rsqrt(jnp.maximum(dist_sq, 1e-30))
    shape_term = (1.0 + scaled + dist_sq * (1.0 / 3.0)) * jnp.exp(-scaled)
    return col_scale * row_scale * shape_term


def prep_kernel(
    me_ref,
    owner_hbm,
    offset_hbm,
    points_hbm,
    amp_hbm,
    noise_hbm,
    cov_hbm,
    out_ref,
    owner_ref,
    offset_ref,
    points_ref,
    amp_ref,
    noise_ref,
    rows_ref,
    sem,
    load_sem,
):
    pairs = (
        (owner_hbm, owner_ref),
        (offset_hbm, offset_ref),
        (points_hbm, points_ref),
        (amp_hbm, amp_ref),
        (noise_hbm, noise_ref),
    )
    loads = [pltpu.make_async_copy(*pair, load_sem.at[i]) for i, pair in enumerate(pairs)]
    for load in loads:
        load.start()
    me = me_ref[0]
    blocks, width = owner_ref.shape
    slots = CAP * blocks
    for load in loads[:2]:
        load.wait()
    lane = lax.broadcasted_iota(jnp.int32, (blocks, width), 1).astype(jnp.float32)
    block = lax.broadcasted_iota(jnp.int32, (blocks, width), 0)
    mine = owner_ref[...] == me
    offset = offset_ref[...].astype(jnp.float32)
    first = jnp.min(jnp.where(mine, lane, 1e4), axis=1, keepdims=True)
    last = jnp.max(jnp.where(mine, lane, -1.0), axis=1, keepdims=True)
    chosen = [jnp.where(mine & (lane == at), offset, 0.0) for at in (first, last)]
    copies = []
    slot_row = lax.broadcasted_iota(jnp.int32, (slots, 1), 0)
    offsets = jnp.zeros((slots, 1), jnp.int32)
    for s in range(slots):
        value = jnp.sum(jnp.where(block == s // CAP, chosen[s % CAP], 0.0)).astype(jnp.int32)
        copy = pltpu.make_async_copy(cov_hbm.at[pl.ds(value, 1), :], rows_ref.at[pl.ds(s, 1), :], sem.at[s])
        copy.start()
        copies.append(copy)
        offsets = jnp.where(slot_row == s, value, offsets)
    for load in loads[2:]:
        load.wait()
    local_rows = points_ref.shape[1]
    hit = lax.broadcasted_iota(jnp.int32, (slots, local_rows), 1) == offsets
    sources = [points_ref[i : i + 1, :] for i in range(3)] + [amp_ref[...], noise_ref[...]]
    sub = lax.broadcasted_iota(jnp.int32, (SUB, BLOCK), 0)
    diagonal = sub == lax.broadcasted_iota(jnp.int32, (SUB, BLOCK), 1)
    scalars = jnp.zeros((SUB, BLOCK), jnp.float32)
    for i, source in enumerate(sources):
        column = jnp.sum(jnp.where(hit, source, 0.0), axis=1, keepdims=True)
        line = jnp.sum(jnp.where(diagonal, column, 0.0), axis=0, keepdims=True)
        scalars = jnp.where(sub == i, line, scalars)
    for copy in copies:
        copy.wait()
    half = rows_ref.shape[1] // 2
    left, right = rows_ref[:, :half], rows_ref[:, half:]
    for i in range(out_ref.shape[0]):
        out_ref[i, :slots, :] = left
        out_ref[i, slots : 2 * slots, :] = right
        out_ref[i, 2 * slots :, :] = scalars


def aux_kernel(
    me_ref,
    owner_ref,
    offset_ref,
    points_ref,
    amp_ref,
    noise_ref,
    cov_ref,
    high_ref,
    middle_ref,
    low_ref,
    feat_ref,
    base_ref,
    info_ref,
    match_ref,
    comb_ref,
    most_ref,
):
    me = me_ref[0]
    blocks, width = owner_ref.shape
    local_rows, cov_width = cov_ref.shape
    half = cov_width // 2
    owner = owner_ref[...]
    padded = jnp.concatenate([owner, jnp.zeros((SUB - blocks, width), jnp.int32)], axis=0)
    owner_t = padded.astype(jnp.float32).T.astype(jnp.int32)
    sub = lax.broadcasted_iota(jnp.int32, (width, width), 0)
    lane = lax.broadcasted_iota(jnp.int32, (width, width), 1)
    xy = (owner >> 1) & 15
    xy_t = (owner_t >> 1) & 15
    my_xy = lax.rem(lax.div(me, 2), 16)
    seats = []
    candidates = []
    infos = []
    for b in range(blocks):
        count = jnp.zeros((1, width), jnp.float32)
        for earlier in range(b + 1):
            same = xy_t[:, earlier : earlier + 1] == xy[b : b + 1, :]
            if earlier == b:
                same = same & (sub < lane)
            count = count + jnp.sum(jnp.where(same, 1.0, 0.0), axis=0, keepdims=True)
        twin = (owner_t[:, b : b + 1] == owner[b : b + 1, :]) & (sub < lane)
        rank = jnp.sum(jnp.where(twin, 1.0, 0.0), axis=0, keepdims=True).astype(jnp.int32)
        count = count.astype(jnp.int32)
        row = owner[b : b + 1, :]
        seats.append(jnp.where(xy[b : b + 1, :] == my_xy, count, -1))
        candidates.append((row >> 5) * 16 + (row & 1) * SUB + CAP * b + rank)
        infos.append(count)
    info_ref[:blocks, :] = xy.astype(jnp.float32)
    counts = jnp.concatenate(infos, axis=0).astype(jnp.float32)
    info_ref[blocks:, :] = counts
    most_ref[0] = jnp.max(counts).astype(jnp.int32) + 1
    match = jnp.where(owner == me, offset_ref[...], -1)
    match_ref[...] = jnp.concatenate([match[b : b + 1, :] for b in range(blocks)], axis=1)
    seat = jnp.concatenate(seats, axis=1)
    candidate = jnp.concatenate(candidates, axis=1)
    ids = lax.broadcasted_iota(jnp.int32, (BLOCK, blocks * width), 0)
    seat_hit = (ids == seat).astype(jnp.float32).astype(jnp.bfloat16)
    candidate_hit = (ids == candidate).astype(jnp.float32).astype(jnp.bfloat16)
    comb_ref[...] = product(seat_hit, candidate_hit, ((1,), (1,)))

    feat_ref[:3, :] = points_ref[...]
    feat_ref[3:4, :] = amp_ref[...]
    feat_ref[4:5, :] = noise_ref[...]
    feat_ref[5:, :] = jnp.zeros((3, local_rows), jnp.float32)
    diagonal = sub == lane

    def step(t, carry):
        at = pl.ds(pl.multiple_of(t * BLOCK, BLOCK), BLOCK)
        cov = cov_ref[at, :]
        high, middle, low = parts_of(cov)
        high_ref[at, :] = high
        middle_ref[at, :] = middle
        low_ref[at, :] = low
        squares = cov * cov
        line = jnp.sum(squares[:, :half] + squares[:, half:], axis=1, keepdims=True)
        total = jnp.sum(jnp.where(diagonal, line, 0.0), axis=0, keepdims=True)
        amplitude = amp_ref[:, at]
        base_ref[pl.ds(t, 1), :] = amplitude * amplitude + noise_ref[:, at] + total
        return carry

    lax.fori_loop(0, local_rows // BLOCK, step, 0)


def seat_kernel(me_ref, comb_ref, got_ref, out_ref):
    core = lax.rem(me_ref[0], 2)
    senders = got_ref.shape[0]
    slots = (got_ref.shape[1] - SUB) // 2
    seats = out_ref.shape[1] - SUB
    comb = comb_ref[...].astype(jnp.bfloat16)
    left = jnp.concatenate([got_ref[i, :slots, :] for i in range(senders)], axis=0)
    right = jnp.concatenate([got_ref[i, slots : 2 * slots, :] for i in range(senders)], axis=0)
    rows = jnp.where(core == 0, left, right)
    packed = pick_rows(comb[: -(-seats // 16) * 16], rows, ((1,), (0,)))[:seats]
    lane = lax.broadcasted_iota(jnp.int32, (SUB, BLOCK), 1)
    scalars = jnp.zeros((SUB, BLOCK), jnp.float32)
    for i in range(senders):
        piece = got_ref[i, 2 * slots :, :]
        piece = pltpu.roll(piece, i * slots, 1) if i else piece
        scalars = jnp.where(lane // slots == i, piece, scalars)
    high, middle, low = parts_of(scalars)
    dims = ((1,), (1,))
    seated = product(high, comb, dims) + product(middle, comb, dims) + product(low, comb, dims)
    for i in range(out_ref.shape[0]):
        out_ref[i, :seats, :] = packed
        out_ref[i, seats:, :] = seated


def main_kernel(
    me_ref,
    mine_ref,
    other_ref,
    info_ref,
    match_ref,
    feat_ref,
    base_ref,
    high_hbm,
    middle_hbm,
    low_hbm,
    out_hbm,
    resid_ref,
    sums_ref,
    cov_high,
    cov_middle,
    cov_low,
    table_high,
    table_middle,
    table_low,
    kernel_high,
    kernel_middle,
    kernel_low,
    scal_ref,
    z_ref,
    r_ref,
    col_ref,
    tile_ref,
    load_sem,
    store_sem,
):
    core = lax.rem(me_ref[0], 2)
    pivots = z_ref.shape[0]
    local_rows, cov_width = cov_high.shape
    planes, plane_rows, half = mine_ref.shape
    seats = plane_rows - SUB
    blocks = pivots // BLOCK
    loads = [
        pltpu.make_async_copy(source, target, load_sem.at[i])
        for i, (source, target) in enumerate(
            ((high_hbm, cov_high), (middle_hbm, cov_middle), (low_hbm, cov_low))
        )
    ]
    for load in loads:
        load.start()
    nt = ((1,), (1,))

    scale = (5.0**0.5) / LENGTH_SCALE
    candidates = planes * plane_rows
    mine = mine_ref[...].reshape(candidates, half)
    other = other_ref[...].reshape(candidates, half)
    both = jnp.concatenate([jnp.where(core == 0, mine, other), jnp.where(core == 0, other, mine)], axis=1)
    both_parts = parts_of(both)
    packed = BLOCK // plane_rows if BLOCK % plane_rows == 0 else 1
    stride = BLOCK // packed
    lane = lax.broadcasted_iota(jnp.int32, (SUB, BLOCK), 1)
    lines = []
    for q in range(planes // packed):
        line = mine_ref[q * packed, seats:, :]
        for t in range(1, packed):
            piece = pltpu.roll(mine_ref[q * packed + t, seats:, :], t * stride, 1)
            line = jnp.where(lane // stride == t, piece, line)
        lines.append(line)
    line_parts = parts_of(jnp.concatenate(lines, axis=1))
    info_t = info_ref[...].T
    for b in range(blocks):
        here = pl.ds(b * BLOCK, BLOCK)
        xy, seat = info_t[:, b : b + 1], info_t[:, blocks + b : blocks + b + 1]
        place = (xy * plane_rows + seat).astype(jnp.int32)
        ids = lax.broadcasted_iota(jnp.int32, (BLOCK, candidates), 1)
        pick = (ids == place).astype(jnp.float32).astype(jnp.bfloat16)
        for part, table in zip(both_parts, (table_high, table_middle, table_low)):
            table[here, :] = product(pick, part, ((1,), (0,))).astype(jnp.bfloat16)
        if packed * plane_rows == BLOCK:
            line_pick = pick
        else:
            place = (xy * stride + seat).astype(jnp.int32)
            ids = lax.broadcasted_iota(jnp.int32, (BLOCK, planes * stride), 1)
            line_pick = (ids == place).astype(jnp.float32).astype(jnp.bfloat16)
        scal_ref[:, here] = (
            product(line_parts[0], line_pick, nt)
            + product(line_parts[1], line_pick, nt)
            + product(line_parts[2], line_pick, nt)
        )

    for t in range(local_rows // BLOCK):
        at = pl.ds(t * BLOCK, BLOCK)
        col_ref[at, :] = feat_ref[:, at].T
    piv = scal_ref[...]
    piv_rows = [piv[i : i + 1, :] * scale for i in range(3)]
    piv_scale, piv_noise = piv[3:4, :], piv[4:5, :]

    for b in range(blocks):
        here = pl.ds(b * BLOCK, BLOCK)
        right = slice(b * BLOCK, pivots)
        cols = scal_ref[:, here].T
        piece = matern(
            [cols[:, i : i + 1] * scale for i in range(3)],
            [row[:, right] for row in piv_rows],
            cols[:, 3:4],
            piv_scale[:, right],
        )
        same = lax.broadcasted_iota(jnp.int32, (BLOCK, 1), 0) == lax.broadcasted_iota(
            jnp.int32, (1, pivots - b * BLOCK), 1
        )
        piece = piece + jnp.where(same, piv_noise[:, right], 0.0)
        left_parts = [table[here, :] for table in (table_high, table_middle, table_low)]
        right_parts = [table[right, :] for table in (table_high, table_middle, table_low)]
        z_ref[here, right] = piece + dot_parts(left_parts, right_parts, nt)
        if b:
            z_ref[here, : b * BLOCK] = jnp.zeros((BLOCK, b * BLOCK), jnp.float32)
    for load in loads:
        load.wait()
    match = match_ref[...]

    def kernel_tile(t):
        at = pl.ds(pl.multiple_of(t * TILE, TILE), TILE)
        cols = col_ref[at, :]
        kernel = matern([cols[:, i : i + 1] * scale for i in range(3)], piv_rows, cols[:, 3:4], piv_scale)
        row_ids = lax.broadcasted_iota(jnp.int32, (TILE, 1), 0) + t * TILE
        kernel = kernel + jnp.where(row_ids == match, cols[:, 4:5], 0.0)
        cov = [part[at, :] for part in (cov_high, cov_middle, cov_low)]
        kernel = kernel + dot_parts(cov, (table_high[...], table_middle[...], table_low[...]), nt)
        for part, target in zip(parts_of(kernel), (kernel_high, kernel_middle, kernel_low)):
            target[at, :] = part

    per_step = local_rows // TILE // blocks

    def step(b, carry):
        at = pl.ds(pl.multiple_of(b * BLOCK, BLOCK), BLOCK)
        pieces = [
            z_ref[pl.ds(pl.multiple_of(b * BLOCK + SUB * i, SUB), SUB), at]
            for i in range(BLOCK // SUB)
        ]
        inverse = jnp.concatenate(block_inverse(pieces), axis=0)
        for i in range(per_step):
            kernel_tile(b * per_step + i)
        r_ref[...] = dot(inverse, z_ref[at, :], ((1,), (0,)))
        r_ref[:, at] = inverse
        z_ref[:, at] = jnp.zeros((pivots, BLOCK), jnp.float32)
        row = r_ref[...]
        row_parts = parts_of(row)
        for later in range(1, blocks):
            there = slice(later * BLOCK, (later + 1) * BLOCK)

            @pl.when(later > b)
            def _():
                coef = [part[:, there] for part in row_parts]
                z_ref[there, :] -= dot_parts(coef, row_parts, ((0,), (0,)))

        z_ref[at, :] = row
        return carry

    lax.fori_loop(0, blocks, step, 0)

    diagonal = lax.broadcasted_iota(jnp.int32, (BLOCK, BLOCK), 0) == lax.broadcasted_iota(
        jnp.int32, (BLOCK, BLOCK), 1
    )
    left = pivots // 2
    half_tiles = WIDE // BLOCK
    tiles = local_rows // WIDE
    inverse_parts = parts_of(z_ref[...])
    for part, target in zip(inverse_parts, (table_high, table_middle, table_low)):
        target[:, :] = part[:, :left]
    late = [part[left:, left:] for part in inverse_parts]

    def tile_step(t, taken):
        at = pl.ds(pl.multiple_of(t * WIDE, WIDE), WIDE)
        slot = lax.rem(t, 2)

        @pl.when(t >= 2)
        def _():
            pltpu.make_async_copy(tile_ref.at[slot], out_hbm.at[at, :], store_sem.at[slot]).wait()

        kernels = [part[at, :] for part in (kernel_high, kernel_middle, kernel_low)]
        early = [part[:, :left] for part in kernels]
        first = dot_parts(early, [table[:left, :] for table in (table_high, table_middle, table_low)], nt)
        second = dot_parts(early, [table[left:, :] for table in (table_high, table_middle, table_low)], nt)
        second = second + dot_parts([part[:, left:] for part in kernels], late, nt)
        tile_ref[slot, :, :left] = first
        tile_ref[slot, :, left:] = second
        pltpu.make_async_copy(tile_ref.at[slot], out_hbm.at[at, :], store_sem.at[slot]).start()
        total = jnp.zeros((WIDE, BLOCK), jnp.float32)
        new_taken = []
        for b in range(blocks):
            source = first if b * BLOCK < left else second
            piece = source[:, (b * BLOCK) % left : (b * BLOCK) % left + BLOCK]
            square = piece * piece
            total = total + square
            new_taken.append(taken[b] + jnp.sum(square.reshape(WIDE // SUB, SUB, BLOCK), axis=0))
        line = jnp.sum(total, axis=1, keepdims=True)
        for h in range(half_tiles):
            spread = jnp.where(diagonal, line[h * BLOCK : (h + 1) * BLOCK, :], 0.0)
            where = pl.ds(t * half_tiles + h, 1)
            resid_ref[where, :] = base_ref[where, :] - jnp.sum(spread, axis=0, keepdims=True)
        return tuple(new_taken)

    zero = jnp.zeros((SUB, BLOCK), jnp.float32)
    taken = lax.fori_loop(0, tiles, tile_step, (zero,) * blocks)
    for tile in (tiles - 2, tiles - 1):
        at = pl.ds(tile * WIDE, WIDE)
        pltpu.make_async_copy(tile_ref.at[tile % 2], out_hbm.at[at, :], store_sem.at[tile % 2]).wait()

    total = jnp.sum(base_ref[...])
    lanes = lax.broadcasted_iota(jnp.int32, sums_ref.shape, 1)
    sums = jnp.zeros(sums_ref.shape, jnp.float32)
    for b in range(blocks):
        total = total - jnp.sum(taken[b])
        sums = jnp.where(lanes == b, total, sums)
    sums_ref[...] = sums


def last_kernel(sums_ref, resid_ref, weights_ref, mean_ref):
    devices, _, width = sums_ref.shape
    rows = resid_ref.shape[0] * resid_ref.shape[1] * devices
    total = jnp.sum(sums_ref[...].reshape(devices, width), axis=0, keepdims=True)
    mean = total * (1.0 / rows)
    count = mean_ref.shape[1]
    mean_ref[...] = mean[:, :count]
    weights_ref[...] = resid_ref[...] / mean[:, count - 1 : count]


def shape(dims, dtype=jnp.float32):
    return jax.ShapeDtypeStruct(dims, dtype)


VMEM = pl.BlockSpec(memory_space=pltpu.VMEM)
SMEM = pl.BlockSpec(memory_space=pltpu.SMEM)
ANY = pl.BlockSpec(memory_space=pl.ANY)
PARAMS = pltpu.CompilerParams(vmem_limit_bytes=40 << 20)


def prep(me, owner, offset, points, amp, noise, cov, copies):
    slots = CAP * owner.shape[0]
    return pl.pallas_call(
        prep_kernel,
        out_shape=shape((copies, 2 * slots + SUB, BLOCK)),
        in_specs=[SMEM] + [ANY] * 6,
        out_specs=VMEM,
        scratch_shapes=[pltpu.VMEM(value.shape, value.dtype) for value in (owner, offset, points, amp, noise)]
        + [
            pltpu.VMEM((slots, cov.shape[1]), jnp.float32),
            pltpu.SemaphoreType.DMA((slots,)),
            pltpu.SemaphoreType.DMA((5,)),
        ],
        compiler_params=pltpu.CompilerParams(vmem_limit_bytes=60 << 20),
        name="prep",
    )(me, owner, offset, points, amp, noise, cov)


def aux(me, owner, offset, points, amp, noise, cov):
    rows, width = cov.shape
    return pl.pallas_call(
        aux_kernel,
        out_shape=(
            shape((rows, width), jnp.bfloat16),
            shape((rows, width), jnp.bfloat16),
            shape((rows, width), jnp.bfloat16),
            shape((SUB, rows)),
            shape((rows // BLOCK, BLOCK)),
            shape((SUB, BLOCK)),
            shape((1, owner.size), jnp.int32),
            shape((BLOCK, BLOCK)),
            shape((1,), jnp.int32),
        ),
        in_specs=[SMEM] + [VMEM] * 6,
        out_specs=(VMEM,) * 8 + (SMEM,),
        compiler_params=PARAMS,
        cost_estimate=pl.CostEstimate(flops=10**8, bytes_accessed=6 << 20, transcendentals=0),
        name="aux",
    )(me, owner, offset, points, amp, noise, cov)


def seat(me, comb, got, copies, seats):
    return pl.pallas_call(
        seat_kernel,
        out_shape=shape((copies, seats + SUB, BLOCK)),
        in_specs=[SMEM, VMEM, VMEM],
        out_specs=VMEM,
        compiler_params=PARAMS,
        name="seat",
    )(me, comb, got)


def main(me, mine, other, info, match, feat, base, high, middle, low, devices):
    rows, width = high.shape
    pivots = match.shape[1]
    bf = jnp.bfloat16
    return pl.pallas_call(
        main_kernel,
        out_shape=(shape((rows, pivots)), shape((rows // BLOCK, BLOCK)), shape((devices, BLOCK))),
        in_specs=[SMEM] + [VMEM] * 6 + [ANY] * 3,
        out_specs=(ANY, VMEM, VMEM),
        scratch_shapes=[pltpu.VMEM((rows, width), bf)] * 3
        + [pltpu.VMEM((pivots, width), bf)] * 3
        + [pltpu.VMEM((rows, pivots), bf)] * 3
        + [
            pltpu.VMEM((SUB, pivots), jnp.float32),
            pltpu.VMEM((pivots, pivots), jnp.float32),
            pltpu.VMEM((BLOCK, pivots), jnp.float32),
            pltpu.VMEM((rows, SUB), jnp.float32),
            pltpu.VMEM((2, WIDE, pivots), jnp.float32),
            pltpu.SemaphoreType.DMA((3,)),
            pltpu.SemaphoreType.DMA((2,)),
        ],
        compiler_params=PARAMS,
        name="factor_rows",
    )(me, mine, other, info, match, feat, base, high, middle, low)


def last(sums, resid, blocks):
    return pl.pallas_call(
        last_kernel,
        out_shape=(shape(resid.shape), shape((1, blocks))),
        in_specs=[VMEM, VMEM],
        out_specs=(VMEM, VMEM),
        compiler_params=PARAMS,
        name="last",
    )(sums, resid)


def local(locations, amplitude, noise, covariates, pivot_owner, pivot_offset):
    me = lax.axis_index(AXES).astype(jnp.int32)[None]
    blocks = pivot_owner.shape[0]
    sizes = [lax.axis_size(name) for name in AXES]
    devices = sizes[0] * sizes[1] * sizes[2] * sizes[3]
    swap = [(0, 1), (1, 0)]
    amp, nugget = amplitude[None], noise[None]
    args = (me, pivot_owner, pivot_offset, locations, amp, nugget, covariates)

    column = lax.all_to_all(prep(*args, sizes[0] * sizes[3]), ("z", "c"), 0, 0, tiled=True)
    high, middle, low, feat, base, info, match, comb, most = aux(*args)

    def rest(seats):
        def run(column, comb, info, match, feat, base, high, middle, low):
            message = seat(me, comb, column, sizes[1] * sizes[2], seats)
            mine = lax.all_to_all(message, ("x", "y"), 0, 0, tiled=True)
            other = lax.ppermute(mine, "c", swap)
            return main(me, mine, other, info, match, feat, base, high, middle, low, devices)

        return run

    operands = (column, comb, info, match, feat, base, high, middle, low)
    if FEW:
        factor, resid, sums = lax.cond(most[0] <= FEW, rest(FEW), rest(BLOCK), *operands)
    else:
        factor, resid, sums = rest(BLOCK)(*operands)
    all_sums = lax.all_to_all(sums[:, None, :], AXES, 0, 0, tiled=True)
    weights, mean_residual = last(all_sums, resid, blocks)
    return (factor, weights.reshape(-1), mean_residual.reshape(-1))


def solution(mesh):
    named = Mesh(mesh.devices.reshape(8, 4, 4, 2), AXES)
    return jax.shard_map(
        local,
        mesh=named,
        in_specs=(P(None, AXES), P(AXES), P(AXES), P(AXES, None), P(), P()),
        out_specs=(P(AXES, None), P(AXES), P()),
        check_vma=False,
    )
```

```python
import functools

import jax
import jax.numpy as jnp
from jax import lax
from jax.experimental import pallas as pl
from jax.experimental.pallas import tpu as pltpu
from jax.sharding import Mesh
from jax.sharding import PartitionSpec as P

LENGTH_SCALE = 0.3
CAP = 2
AXES = ("z", "x", "y", "c")
HIGHEST = lax.Precision.HIGHEST
BLOCK = 128
PANEL = 16
SUB = 8
TILE = 256
FEW = 56
WIDE = 512
LOG2E = 1.4426950408889634


def dot(left, right, dims):
    return lax.dot_general(
        left, right, (dims, ((), ())), precision=HIGHEST, preferred_element_type=jnp.float32
    )


def panel_inverse(low, high):
    sub = lax.broadcasted_iota(jnp.int32, (SUB, BLOCK), 0)
    low, high = list(low), list(high)
    root_low = jnp.zeros((SUB, BLOCK), jnp.float32)
    root_high = root_low

    def entry(j, i):
        piece = low[j][i : i + 1, :] if i < SUB else high[j][i - SUB : i - SUB + 1, :]
        return jnp.broadcast_to(piece, (SUB, BLOCK))

    pivot = entry(0, 0)
    for k in range(PANEL):
        inverse = pl.reciprocal(pivot, approx=True)
        root = lax.rsqrt(pivot)
        if k + 1 < PANEL:
            side = entry(k, k + 1)
            pivot = entry(k + 1, k + 1) - (side * side) * inverse
        if k < SUB:
            take_low = jnp.where(sub > k, low[k], 0.0) * inverse
            take_high = high[k] * inverse
            across = high[k]
            root_low = jnp.where(sub == k, root, root_low)
            for j in range(PANEL):
                if j < SUB and j != k:
                    line = low[j][k : k + 1, :]
                    low[j] = low[j] - take_low * line
                    high[j] = high[j] - take_high * line
                elif j >= SUB:
                    high[j] = high[j] - take_high * across[j - SUB : j - SUB + 1, :]
            low[k] = jnp.where(sub == k, 1.0, -take_low)
            high[k] = -take_high
        else:
            s = k - SUB
            take_high = jnp.where(sub > s, high[k], 0.0) * inverse
            root_high = jnp.where(sub == s, root, root_high)
            for j in range(PANEL):
                if j != k:
                    high[j] = high[j] - take_high * high[j][s : s + 1, :]
            high[k] = jnp.where(sub == s, 1.0, -take_high)
    return [low[j] * root_low for j in range(SUB)], [high[j] * root_high for j in range(PANEL)]


def tree_sum(terms):
    while len(terms) > 1:
        pairs = [terms[i] + terms[i + 1] for i in range(0, len(terms) - 1, 2)]
        terms = pairs + terms[2 * len(pairs) :]
    return terms[0]


def block_inverse(rows):
    lane = lax.broadcasted_iota(jnp.int32, (SUB, BLOCK), 1)
    sub = lax.broadcasted_iota(jnp.int32, (SUB, BLOCK), 0)
    rows = list(rows)
    out = [None] * len(rows)
    for panel in range(BLOCK // PANEL):
        first = PANEL * panel
        at = 2 * panel

        def splat(piece, j):
            return jnp.broadcast_to(piece[:, first + j : first + j + 1], (SUB, BLOCK))

        rest = range(at + 2, len(rows))
        near, far = rest[:2], rest[2:]
        low = [splat(rows[at], j) for j in range(SUB)]
        high = [splat(rows[at + 1], j) for j in range(PANEL)]
        coef = {r: [splat(rows[r], j) for j in range(PANEL)] for r in near}
        inv_low, inv_high = panel_inverse(low, high)
        in_panel = (lane >= first) & (lane < first + PANEL)
        top = jnp.where(in_panel, jnp.where(lane - first == sub, 1.0, 0.0), rows[at])
        bottom = jnp.where(in_panel, jnp.where(lane - first - SUB == sub, 1.0, 0.0), rows[at + 1])
        entries = [top[j : j + 1, :] for j in range(SUB)] + [bottom[j : j + 1, :] for j in range(SUB)]
        new_low = tree_sum([inv_low[j] * entries[j] for j in range(SUB)])
        new_high = tree_sum([inv_high[j] * entries[j] for j in range(PANEL)])
        out[at] = jnp.where(lane <= first + sub, new_low, 0.0)
        out[at + 1] = jnp.where(lane <= first + SUB + sub, new_high, 0.0)
        if len(near):
            weights = []
            for j in range(PANEL):
                term = inv_high[j] * new_high
                if j < SUB:
                    term = term + inv_low[j] * new_low
                weights.append(jnp.sum(term, axis=0, keepdims=True))
            for r in near:
                piece = jnp.where(in_panel, 0.0, rows[r])
                for j in range(PANEL):
                    piece = piece - coef[r][j] * weights[j]
                rows[r] = piece
        if len(far):
            spread = []
            for part in parts_of(jnp.concatenate(weights, axis=0)):
                above = [jnp.zeros((first, BLOCK), jnp.bfloat16)] if first else []
                below = [jnp.zeros((BLOCK - first - PANEL, BLOCK), jnp.bfloat16)]
                spread.append(jnp.concatenate(above + [part] + below, axis=0))
            far_rows = parts_of(jnp.concatenate([rows[r] for r in far], axis=0))
            change = dot_parts(far_rows, spread, ((1,), (0,)))
            for i, r in enumerate(far):
                rows[r] = jnp.where(in_panel, 0.0, rows[r]) - change[SUB * i : SUB * (i + 1)]
    return out


def parts_of(value):
    high = value.astype(jnp.bfloat16)
    rest = value - high.astype(jnp.float32)
    middle = rest.astype(jnp.bfloat16)
    low = (rest - middle.astype(jnp.float32)).astype(jnp.bfloat16)
    return high, middle, low


def product(left, right, dims):
    return lax.dot_general(left, right, (dims, ((), ())), preferred_element_type=jnp.float32)


def dot_parts(left, right, dims):
    high, middle, low = left
    other_high, other_middle, other_low = right
    one = jnp.concatenate([low, high, middle, middle, high, high], axis=dims[0][0])
    two = jnp.concatenate(
        [other_high, other_low, other_middle, other_high, other_middle, other_high], axis=dims[1][0]
    )
    return product(one, two, dims)


def pick_rows(pick, value, dims):
    high, middle, low = parts_of(value)
    return product(pick, high, dims) + product(pick, middle, dims) + product(pick, low, dims)


def matern(cols, rows, col_scale, row_scale):
    dist_sq = None
    for axis_id in range(3):
        offset = cols[axis_id] - rows[axis_id]
        dist_sq = offset * offset if dist_sq is None else dist_sq + offset * offset
    scaled = dist_sq * lax.rsqrt(jnp.maximum(dist_sq, 1e-30))
    shape_term = (1.0 + scaled + dist_sq * (1.0 / 3.0)) * jnp.exp(-scaled)
    return col_scale * row_scale * shape_term


def prep_kernel(
    me_ref,
    owner_hbm,
    offset_hbm,
    points_hbm,
    amp_hbm,
    noise_hbm,
    cov_hbm,
    out_ref,
    owner_ref,
    offset_ref,
    points_ref,
    amp_ref,
    noise_ref,
    rows_ref,
    sem,
    load_sem,
):
    pairs = (
        (owner_hbm, owner_ref),
        (offset_hbm, offset_ref),
        (points_hbm, points_ref),
        (amp_hbm, amp_ref),
        (noise_hbm, noise_ref),
    )
    loads = [pltpu.make_async_copy(*pair, load_sem.at[i]) for i, pair in enumerate(pairs)]
    for load in loads:
        load.start()
    me = me_ref[0]
    blocks, width = owner_ref.shape
    slots = CAP * blocks
    for load in loads[:2]:
        load.wait()
    lane = lax.broadcasted_iota(jnp.int32, (blocks, width), 1).astype(jnp.float32)
    block = lax.broadcasted_iota(jnp.int32, (blocks, width), 0)
    mine = owner_ref[...] == me
    offset = offset_ref[...].astype(jnp.float32)
    first = jnp.min(jnp.where(mine, lane, 1e4), axis=1, keepdims=True)
    last = jnp.max(jnp.where(mine, lane, -1.0), axis=1, keepdims=True)
    chosen = [jnp.where(mine & (lane == at), offset, 0.0) for at in (first, last)]
    copies = []
    slot_row = lax.broadcasted_iota(jnp.int32, (slots, 1), 0)
    offsets = jnp.zeros((slots, 1), jnp.int32)
    for s in range(slots):
        value = jnp.sum(jnp.where(block == s // CAP, chosen[s % CAP], 0.0)).astype(jnp.int32)
        copy = pltpu.make_async_copy(cov_hbm.at[pl.ds(value, 1), :], rows_ref.at[pl.ds(s, 1), :], sem.at[s])
        copy.start()
        copies.append(copy)
        offsets = jnp.where(slot_row == s, value, offsets)
    for load in loads[2:]:
        load.wait()
    local_rows = points_ref.shape[1]
    hit = lax.broadcasted_iota(jnp.int32, (slots, local_rows), 1) == offsets
    sources = [points_ref[i : i + 1, :] for i in range(3)] + [amp_ref[...], noise_ref[...]]
    sub = lax.broadcasted_iota(jnp.int32, (SUB, BLOCK), 0)
    diagonal = sub == lax.broadcasted_iota(jnp.int32, (SUB, BLOCK), 1)
    scalars = jnp.zeros((SUB, BLOCK), jnp.float32)
    for i, source in enumerate(sources):
        column = jnp.sum(jnp.where(hit, source, 0.0), axis=1, keepdims=True)
        line = jnp.sum(jnp.where(diagonal, column, 0.0), axis=0, keepdims=True)
        scalars = jnp.where(sub == i, line, scalars)
    for copy in copies:
        copy.wait()
    half = rows_ref.shape[1] // 2
    left, right = rows_ref[:, :half], rows_ref[:, half:]
    for i in range(out_ref.shape[0]):
        out_ref[i, :slots, :] = left
        out_ref[i, slots : 2 * slots, :] = right
        out_ref[i, 2 * slots :, :] = scalars


def aux_kernel(
    me_ref,
    owner_ref,
    offset_ref,
    points_ref,
    amp_ref,
    noise_ref,
    cov_ref,
    high_ref,
    middle_ref,
    low_ref,
    feat_ref,
    base_ref,
    info_ref,
    match_ref,
    comb_ref,
    left_ref,
    most_ref,
):
    me = me_ref[0]
    blocks, width = owner_ref.shape
    local_rows, cov_width = cov_ref.shape
    half = cov_width // 2
    owner = owner_ref[...]
    padded = jnp.concatenate([owner, jnp.zeros((SUB - blocks, width), jnp.int32)], axis=0)
    owner_t = padded.astype(jnp.float32).T.astype(jnp.int32)
    sub = lax.broadcasted_iota(jnp.int32, (width, width), 0)
    lane = lax.broadcasted_iota(jnp.int32, (width, width), 1)
    xy = (owner >> 1) & 15
    xy_t = (owner_t >> 1) & 15
    my_xy = lax.rem(lax.div(me, 2), 16)
    seats = []
    candidates = []
    infos = []
    for b in range(blocks):
        count = jnp.zeros((1, width), jnp.float32)
        for earlier in range(b + 1):
            same = xy_t[:, earlier : earlier + 1] == xy[b : b + 1, :]
            if earlier == b:
                same = same & (sub < lane)
            count = count + jnp.sum(jnp.where(same, 1.0, 0.0), axis=0, keepdims=True)
        twin = (owner_t[:, b : b + 1] == owner[b : b + 1, :]) & (sub < lane)
        rank = jnp.sum(jnp.where(twin, 1.0, 0.0), axis=0, keepdims=True).astype(jnp.int32)
        count = count.astype(jnp.int32)
        row = owner[b : b + 1, :]
        seats.append(jnp.where(xy[b : b + 1, :] == my_xy, count, -1))
        candidates.append((row >> 5) * 16 + (row & 1) * SUB + CAP * b + rank)
        infos.append(count)
    info_ref[:blocks, :] = xy.astype(jnp.float32)
    counts = jnp.concatenate(infos, axis=0).astype(jnp.float32)
    info_ref[blocks:, :] = counts
    most_ref[0] = jnp.max(counts).astype(jnp.int32) + 1
    match = jnp.where(owner == me, offset_ref[...], -1)
    match_ref[...] = jnp.concatenate([match[b : b + 1, :] for b in range(blocks)], axis=1)
    seat = jnp.concatenate(seats, axis=1)
    candidate = jnp.concatenate(candidates, axis=1)
    ids = lax.broadcasted_iota(jnp.int32, (BLOCK, blocks * width), 0)
    seat_hit = (ids == seat).astype(jnp.float32).astype(jnp.bfloat16)
    candidate_hit = (ids == candidate).astype(jnp.float32).astype(jnp.bfloat16)
    comb_ref[...] = product(seat_hit, candidate_hit, ((1,), (1,)))

    feat_ref[:3, :] = points_ref[...]
    feat_ref[3:4, :] = amp_ref[...]
    feat_ref[4:5, :] = noise_ref[...]
    feat_ref[5:, :] = jnp.zeros((3, local_rows), jnp.float32)
    diagonal = sub == lane
    scale = (5.0**0.5) / LENGTH_SCALE
    order = (0, 0, 1, 1, 0, 2)

    def step(t, carry):
        at = pl.ds(pl.multiple_of(t * BLOCK, BLOCK), BLOCK)
        cov = cov_ref[at, :]
        high, middle, low = parts_of(cov)
        high_ref[at, :] = high
        middle_ref[at, :] = middle
        low_ref[at, :] = low
        squares = cov * cov
        line = jnp.sum(squares[:, :half] + squares[:, half:], axis=1, keepdims=True)
        total = jnp.sum(jnp.where(diagonal, line, 0.0), axis=0, keepdims=True)
        points = (points_ref[:, at] - 0.5) * scale
        point_parts = [part.astype(jnp.float32) for part in parts_of(points)]
        length = jnp.sum(points * points, axis=0, keepdims=True)
        lines = [point_parts[k][i : i + 1, :] for i in range(3) for k in order]
        lines += [part.astype(jnp.float32) for part in parts_of(length)] + [jnp.ones((3, BLOCK), jnp.float32)]
        lines.append(jnp.zeros((BLOCK - 6 * len(order) + 12, BLOCK), jnp.float32))
        left_ref[at, :] = jnp.concatenate(lines, axis=0).T.astype(jnp.bfloat16)
        amplitude = amp_ref[:, at]
        base_ref[pl.ds(t, 1), :] = amplitude * amplitude + noise_ref[:, at] + total
        return carry

    lax.fori_loop(0, local_rows // BLOCK, step, 0)


def seat_kernel(me_ref, comb_ref, got_ref, out_ref):
    core = lax.rem(me_ref[0], 2)
    senders = got_ref.shape[0]
    slots = (got_ref.shape[1] - SUB) // 2
    seats = out_ref.shape[1] - SUB
    comb = comb_ref[...].astype(jnp.bfloat16)
    left = jnp.concatenate([got_ref[i, :slots, :] for i in range(senders)], axis=0)
    right = jnp.concatenate([got_ref[i, slots : 2 * slots, :] for i in range(senders)], axis=0)
    rows = jnp.where(core == 0, left, right)
    packed = pick_rows(comb[: -(-seats // 16) * 16], rows, ((1,), (0,)))[:seats]
    lane = lax.broadcasted_iota(jnp.int32, (SUB, BLOCK), 1)
    scalars = jnp.zeros((SUB, BLOCK), jnp.float32)
    for i in range(senders):
        piece = got_ref[i, 2 * slots :, :]
        piece = pltpu.roll(piece, i * slots, 1) if i else piece
        scalars = jnp.where(lane // slots == i, piece, scalars)
    high, middle, low = parts_of(scalars)
    dims = ((1,), (1,))
    seated = product(high, comb, dims) + product(middle, comb, dims) + product(low, comb, dims)
    for i in range(out_ref.shape[0]):
        out_ref[i, :seats, :] = packed
        out_ref[i, seats:, :] = seated


def field_kernel(mine_ref, info_ref, match_ref, feat_ref, left_ref, scal_ref, field_ref, col_ref):
    pivots = match_ref.shape[1]
    local_rows = feat_ref.shape[1]
    planes, plane_rows, _ = mine_ref.shape
    seats = plane_rows - SUB
    blocks = pivots // BLOCK
    nt = ((1,), (1,))
    packed = BLOCK // plane_rows if BLOCK % plane_rows == 0 else 1
    stride = BLOCK // packed
    lane = lax.broadcasted_iota(jnp.int32, (SUB, BLOCK), 1)
    lines = []
    for q in range(planes // packed):
        line = mine_ref[q * packed, seats:, :]
        for t in range(1, packed):
            piece = pltpu.roll(mine_ref[q * packed + t, seats:, :], t * stride, 1)
            line = jnp.where(lane // stride == t, piece, line)
        lines.append(line)
    line_parts = parts_of(jnp.concatenate(lines, axis=1))
    info_t = info_ref[...].T
    for b in range(blocks):
        here = pl.ds(b * BLOCK, BLOCK)
        xy, seat = info_t[:, b : b + 1], info_t[:, blocks + b : blocks + b + 1]
        place = (xy * stride + seat).astype(jnp.int32)
        ids = lax.broadcasted_iota(jnp.int32, (BLOCK, planes * stride), 1)
        line_pick = (ids == place).astype(jnp.float32).astype(jnp.bfloat16)
        scal_ref[:, here] = (
            product(line_parts[0], line_pick, nt)
            + product(line_parts[1], line_pick, nt)
            + product(line_parts[2], line_pick, nt)
        )
    for t in range(local_rows // BLOCK):
        at = pl.ds(t * BLOCK, BLOCK)
        col_ref[at, :] = feat_ref[:, at].T
    piv = scal_ref[...]
    piv_scale = piv[3:4, :]
    match = match_ref[...]

    scale = (5.0**0.5) / LENGTH_SCALE
    points = (piv[:3, :] - 0.5) * scale
    length = jnp.sum(points * points, axis=0, keepdims=True)
    point_parts = [part.astype(jnp.float32) * -2.0 for part in parts_of(points)]
    lines = [point_parts[k][i : i + 1, :] for i in range(3) for k in (0, 1, 0, 1, 2, 0)]
    lines += [jnp.ones((3, pivots), jnp.float32)] + [part.astype(jnp.float32) for part in parts_of(length)]
    lines.append(jnp.zeros((BLOCK - 24, pivots), jnp.float32))
    right = jnp.concatenate(lines, axis=0).astype(jnp.bfloat16)

    def step(t, carry):
        at = pl.ds(pl.multiple_of(t * WIDE, WIDE), WIDE)
        cols = col_ref[at, :]
        dist_sq = jnp.maximum(product(left_ref[at, :], right, ((1,), (0,))), 1e-30)
        scaled = dist_sq * lax.rsqrt(dist_sq)
        value = (1.0 + scaled + dist_sq * (1.0 / 3.0)) * jnp.exp2(scaled * -LOG2E)
        value = cols[:, 3:4] * piv_scale * value
        row_ids = lax.broadcasted_iota(jnp.int32, (WIDE, 1), 0) + t * WIDE
        field_ref[at, :] = value + jnp.where(row_ids == match, cols[:, 4:5], 0.0)
        return carry

    lax.fori_loop(0, local_rows // WIDE, step, 0)


def main_kernel(
    me_ref,
    mine_ref,
    other_ref,
    info_ref,
    scal_ref,
    field_ref,
    base_ref,
    high_hbm,
    middle_hbm,
    low_hbm,
    out_hbm,
    resid_ref,
    sums_ref,
    cov_high,
    cov_middle,
    cov_low,
    table_high,
    table_middle,
    table_low,
    kernel_high,
    kernel_middle,
    kernel_low,
    z_ref,
    r_ref,
    tile_ref,
    load_sem,
    store_sem,
):
    core = lax.rem(me_ref[0], 2)
    pivots = z_ref.shape[0]
    local_rows, cov_width = cov_high.shape
    planes, plane_rows, half = mine_ref.shape
    blocks = pivots // BLOCK
    loads = [
        pltpu.make_async_copy(source, target, load_sem.at[i])
        for i, (source, target) in enumerate(
            ((high_hbm, cov_high), (middle_hbm, cov_middle), (low_hbm, cov_low))
        )
    ]
    for load in loads:
        load.start()
    nt = ((1,), (1,))

    scale = (5.0**0.5) / LENGTH_SCALE
    candidates = planes * plane_rows
    mine = mine_ref[...].reshape(candidates, half)
    other = other_ref[...].reshape(candidates, half)
    both = jnp.concatenate([jnp.where(core == 0, mine, other), jnp.where(core == 0, other, mine)], axis=1)
    both_parts = parts_of(both)
    info_t = info_ref[...].T
    for b in range(blocks):
        here = pl.ds(b * BLOCK, BLOCK)
        xy, seat = info_t[:, b : b + 1], info_t[:, blocks + b : blocks + b + 1]
        place = (xy * plane_rows + seat).astype(jnp.int32)
        ids = lax.broadcasted_iota(jnp.int32, (BLOCK, candidates), 1)
        pick = (ids == place).astype(jnp.float32).astype(jnp.bfloat16)
        for part, table in zip(both_parts, (table_high, table_middle, table_low)):
            table[here, :] = product(pick, part, ((1,), (0,))).astype(jnp.bfloat16)

    piv = scal_ref[...]
    piv_rows = [piv[i : i + 1, :] * scale for i in range(3)]
    piv_scale, piv_noise = piv[3:4, :], piv[4:5, :]

    for b in range(blocks):
        here = pl.ds(b * BLOCK, BLOCK)
        right = slice(b * BLOCK, pivots)
        cols = scal_ref[:, here].T
        piece = matern(
            [cols[:, i : i + 1] * scale for i in range(3)],
            [row[:, right] for row in piv_rows],
            cols[:, 3:4],
            piv_scale[:, right],
        )
        same = lax.broadcasted_iota(jnp.int32, (BLOCK, 1), 0) == lax.broadcasted_iota(
            jnp.int32, (1, pivots - b * BLOCK), 1
        )
        piece = piece + jnp.where(same, piv_noise[:, right], 0.0)
        left_parts = [table[here, :] for table in (table_high, table_middle, table_low)]
        right_parts = [table[right, :] for table in (table_high, table_middle, table_low)]
        z_ref[here, right] = piece + dot_parts(left_parts, right_parts, nt)
        if b:
            z_ref[here, : b * BLOCK] = jnp.zeros((BLOCK, b * BLOCK), jnp.float32)
    for load in loads:
        load.wait()
    def kernel_tile(t):
        at = pl.ds(pl.multiple_of(t * WIDE, WIDE), WIDE)
        cov = [part[at, :] for part in (cov_high, cov_middle, cov_low)]
        kernel = field_ref[at, :] + dot_parts(cov, (table_high[...], table_middle[...], table_low[...]), nt)
        for part, target in zip(parts_of(kernel), (kernel_high, kernel_middle, kernel_low)):
            target[at, :] = part

    per_step = local_rows // WIDE // blocks

    def step(b, carry):
        at = pl.ds(pl.multiple_of(b * BLOCK, BLOCK), BLOCK)
        pieces = [
            z_ref[pl.ds(pl.multiple_of(b * BLOCK + SUB * i, SUB), SUB), at]
            for i in range(BLOCK // SUB)
        ]
        inverse = jnp.concatenate(block_inverse(pieces), axis=0)
        for i in range(per_step):
            kernel_tile(b * per_step + i)
        r_ref[...] = dot_parts(parts_of(inverse), parts_of(z_ref[at, :]), ((1,), (0,)))
        r_ref[:, at] = inverse
        z_ref[:, at] = jnp.zeros((pivots, BLOCK), jnp.float32)
        row = r_ref[...]
        for s in range(blocks - 1):

            @pl.when(b == s)
            def _():
                later = slice((s + 1) * BLOCK, pivots)
                coef = parts_of(row[:, later].T)
                z_ref[later, :] -= dot_parts(coef, parts_of(row), ((1,), (0,)))

        z_ref[at, :] = row
        return carry

    lax.fori_loop(0, blocks, step, 0)

    diagonal = lax.broadcasted_iota(jnp.int32, (BLOCK, BLOCK), 0) == lax.broadcasted_iota(
        jnp.int32, (BLOCK, BLOCK), 1
    )
    left = pivots // 2
    half_tiles = WIDE // BLOCK
    tiles = local_rows // WIDE
    inverse_parts = parts_of(z_ref[...])
    for part, target in zip(inverse_parts, (table_high, table_middle, table_low)):
        target[:, :] = part[:, :left]
    late = [part[left:, left:] for part in inverse_parts]

    def tile_step(t, taken):
        at = pl.ds(pl.multiple_of(t * WIDE, WIDE), WIDE)
        slot = lax.rem(t, 2)

        @pl.when(t >= 2)
        def _():
            pltpu.make_async_copy(tile_ref.at[slot], out_hbm.at[at, :], store_sem.at[slot]).wait()

        kernels = [part[at, :] for part in (kernel_high, kernel_middle, kernel_low)]
        early = [part[:, :left] for part in kernels]
        first = dot_parts(early, [table[:left, :] for table in (table_high, table_middle, table_low)], nt)
        second = dot_parts(early, [table[left:, :] for table in (table_high, table_middle, table_low)], nt)
        second = second + dot_parts([part[:, left:] for part in kernels], late, nt)
        tile_ref[slot, :, :left] = first
        tile_ref[slot, :, left:] = second
        pltpu.make_async_copy(tile_ref.at[slot], out_hbm.at[at, :], store_sem.at[slot]).start()
        total = jnp.zeros((WIDE, BLOCK), jnp.float32)
        new_taken = []
        for b in range(blocks):
            source = first if b * BLOCK < left else second
            piece = source[:, (b * BLOCK) % left : (b * BLOCK) % left + BLOCK]
            square = piece * piece
            total = total + square
            new_taken.append(taken[b] + jnp.sum(square.reshape(WIDE // SUB, SUB, BLOCK), axis=0))
        line = jnp.sum(total, axis=1, keepdims=True)
        for h in range(half_tiles):
            spread = jnp.where(diagonal, line[h * BLOCK : (h + 1) * BLOCK, :], 0.0)
            where = pl.ds(t * half_tiles + h, 1)
            resid_ref[where, :] = base_ref[where, :] - jnp.sum(spread, axis=0, keepdims=True)
        return tuple(new_taken)

    zero = jnp.zeros((SUB, BLOCK), jnp.float32)
    taken = lax.fori_loop(0, tiles, tile_step, (zero,) * blocks)
    for tile in (tiles - 2, tiles - 1):
        at = pl.ds(tile * WIDE, WIDE)
        pltpu.make_async_copy(tile_ref.at[tile % 2], out_hbm.at[at, :], store_sem.at[tile % 2]).wait()

    total = jnp.sum(base_ref[...])
    lanes = lax.broadcasted_iota(jnp.int32, sums_ref.shape, 1)
    sums = jnp.zeros(sums_ref.shape, jnp.float32)
    for b in range(blocks):
        total = total - jnp.sum(taken[b])
        sums = jnp.where(lanes == b, total, sums)
    sums_ref[...] = sums


def last_kernel(sums_ref, resid_ref, weights_ref, mean_ref, *, rows):
    devices, _, width = sums_ref.shape
    total = jnp.sum(sums_ref[...].reshape(devices, width), axis=0, keepdims=True)
    mean = total * (1.0 / rows)
    count = mean_ref.shape[1]
    mean_ref[...] = mean[:, :count]
    weights_ref[...] = resid_ref[...] / mean[:, count - 1 : count]


def shape(dims, dtype=jnp.float32):
    return jax.ShapeDtypeStruct(dims, dtype)


VMEM = pl.BlockSpec(memory_space=pltpu.VMEM)
SMEM = pl.BlockSpec(memory_space=pltpu.SMEM)
ANY = pl.BlockSpec(memory_space=pl.ANY)
PARAMS = pltpu.CompilerParams(vmem_limit_bytes=40 << 20)


def prep(me, owner, offset, points, amp, noise, cov, copies):
    slots = CAP * owner.shape[0]
    return pl.pallas_call(
        prep_kernel,
        out_shape=shape((copies, 2 * slots + SUB, BLOCK)),
        in_specs=[SMEM] + [ANY] * 6,
        out_specs=VMEM,
        scratch_shapes=[pltpu.VMEM(value.shape, value.dtype) for value in (owner, offset, points, amp, noise)]
        + [
            pltpu.VMEM((slots, cov.shape[1]), jnp.float32),
            pltpu.SemaphoreType.DMA((slots,)),
            pltpu.SemaphoreType.DMA((5,)),
        ],
        compiler_params=pltpu.CompilerParams(vmem_limit_bytes=60 << 20),
        name="prep",
    )(me, owner, offset, points, amp, noise, cov)


def aux(me, owner, offset, points, amp, noise, cov):
    rows, width = cov.shape
    return pl.pallas_call(
        aux_kernel,
        out_shape=(
            shape((rows, width), jnp.bfloat16),
            shape((rows, width), jnp.bfloat16),
            shape((rows, width), jnp.bfloat16),
            shape((SUB, rows)),
            shape((rows // BLOCK, BLOCK)),
            shape((SUB, BLOCK)),
            shape((1, owner.size), jnp.int32),
            shape((BLOCK, BLOCK)),
            shape((rows, BLOCK), jnp.bfloat16),
            shape((1,), jnp.int32),
        ),
        in_specs=[SMEM] + [VMEM] * 6,
        out_specs=(VMEM,) * 9 + (SMEM,),
        compiler_params=PARAMS,
        cost_estimate=pl.CostEstimate(flops=10**8, bytes_accessed=6 << 20, transcendentals=0),
        name="aux",
    )(me, owner, offset, points, amp, noise, cov)


def seat(me, comb, got, copies, seats):
    return pl.pallas_call(
        seat_kernel,
        out_shape=shape((copies, seats + SUB, BLOCK)),
        in_specs=[SMEM, VMEM, VMEM],
        out_specs=VMEM,
        compiler_params=PARAMS,
        name="seat",
    )(me, comb, got)


def field(mine, info, match, feat, left):
    pivots, rows = match.shape[1], feat.shape[1]
    return pl.pallas_call(
        field_kernel,
        out_shape=(shape((SUB, pivots)), shape((rows, pivots))),
        in_specs=[VMEM] * 5,
        out_specs=(VMEM, VMEM),
        scratch_shapes=[pltpu.VMEM((rows, SUB), jnp.float32)],
        compiler_params=PARAMS,
        cost_estimate=pl.CostEstimate(flops=10**8, bytes_accessed=6 << 20, transcendentals=0),
        name="field",
    )(mine, info, match, feat, left)


def main(me, mine, other, info, scal, local_field, base, high, middle, low, devices):
    rows, width = high.shape
    pivots = scal.shape[1]
    bf = jnp.bfloat16
    return pl.pallas_call(
        main_kernel,
        out_shape=(shape((rows, pivots)), shape((rows // BLOCK, BLOCK)), shape((devices, BLOCK))),
        in_specs=[SMEM] + [VMEM] * 6 + [ANY] * 3,
        out_specs=(ANY, VMEM, VMEM),
        scratch_shapes=[pltpu.VMEM((rows, width), bf)] * 3
        + [pltpu.VMEM((pivots, width), bf)] * 3
        + [pltpu.VMEM((rows, pivots), bf)] * 3
        + [
            pltpu.VMEM((pivots, pivots), jnp.float32),
            pltpu.VMEM((BLOCK, pivots), jnp.float32),
            pltpu.VMEM((2, WIDE, pivots), jnp.float32),
            pltpu.SemaphoreType.DMA((3,)),
            pltpu.SemaphoreType.DMA((2,)),
        ],
        compiler_params=PARAMS,
        name="factor_rows",
    )(me, mine, other, info, scal, local_field, base, high, middle, low)


def last(sums, resid, blocks, rows):
    return pl.pallas_call(
        functools.partial(last_kernel, rows=rows),
        out_shape=(shape(resid.shape), shape((1, blocks))),
        in_specs=[VMEM, VMEM],
        out_specs=(VMEM, VMEM),
        compiler_params=PARAMS,
        name="last",
    )(sums, resid)


def local(locations, amplitude, noise, covariates, pivot_owner, pivot_offset):
    me = lax.axis_index(AXES).astype(jnp.int32)[None]
    blocks = pivot_owner.shape[0]
    sizes = [lax.axis_size(name) for name in AXES]
    devices = sizes[0] * sizes[1] * sizes[2] * sizes[3]
    swap = [(0, 1), (1, 0)]
    amp, nugget = amplitude[None], noise[None]
    args = (me, pivot_owner, pivot_offset, locations, amp, nugget, covariates)

    column = lax.all_to_all(prep(*args, sizes[0] * sizes[3]), ("z", "c"), 0, 0, tiled=True)
    high, middle, low, feat, base, info, match, comb, left, most = aux(*args)

    def rest(seats):
        def run(column, comb, info, match, feat, left, base, high, middle, low):
            message = seat(me, comb, column, sizes[1] * sizes[2], seats)
            mine = lax.all_to_all(message, ("x", "y"), 0, 0, tiled=True)
            other = lax.ppermute(mine, "c", swap)
            scal, local_field = field(mine, info, match, feat, left)
            return main(me, mine, other, info, scal, local_field, base, high, middle, low, devices)

        return run

    operands = (column, comb, info, match, feat, left, base, high, middle, low)
    if FEW:
        factor, resid, sums = lax.cond(most[0] <= FEW, rest(FEW), rest(BLOCK), *operands)
    else:
        factor, resid, sums = rest(BLOCK)(*operands)
    all_sums = lax.all_to_all(sums[:, None, :], AXES, 0, 0, tiled=True)
    weights, mean_residual = last(all_sums, resid, blocks, locations.shape[1] * devices)
    return (factor, weights.reshape(-1), mean_residual.reshape(-1))


def solution(mesh):
    named = Mesh(mesh.devices.reshape(8, 4, 4, 2), AXES)
    return jax.shard_map(
        local,
        mesh=named,
        in_specs=(P(None, AXES), P(AXES), P(AXES), P(AXES, None), P(), P()),
        out_specs=(P(AXES, None), P(AXES), P()),
        check_vma=False,
    )
```

```python
import functools

import jax
import jax.numpy as jnp
from jax import lax
from jax.experimental import pallas as pl
from jax.experimental.pallas import tpu as pltpu
from jax.sharding import Mesh
from jax.sharding import PartitionSpec as P

LENGTH_SCALE = 0.3
CAP = 2
AXES = ("z", "x", "y", "c")
HIGHEST = lax.Precision.HIGHEST
BLOCK = 128
PANEL = 16
SUB = 8
TILE = 256
FEW = 56
WIDE = 512
LOG2E = 1.4426950408889634


def dot(left, right, dims):
    return lax.dot_general(
        left, right, (dims, ((), ())), precision=HIGHEST, preferred_element_type=jnp.float32
    )


def panel_inverse(low, high):
    sub = lax.broadcasted_iota(jnp.int32, (SUB, BLOCK), 0)
    low, high = list(low), list(high)
    root_low = jnp.zeros((SUB, BLOCK), jnp.float32)
    root_high = root_low

    def entry(j, i):
        piece = low[j][i : i + 1, :] if i < SUB else high[j][i - SUB : i - SUB + 1, :]
        return jnp.broadcast_to(piece, (SUB, BLOCK))

    pivot = entry(0, 0)
    for k in range(PANEL):
        inverse = pl.reciprocal(pivot, approx=True)
        root = lax.rsqrt(pivot)
        if k + 1 < PANEL:
            side = entry(k, k + 1)
            pivot = entry(k + 1, k + 1) - (side * side) * inverse
        if k < SUB:
            take_low = jnp.where(sub > k, low[k], 0.0) * inverse
            take_high = high[k] * inverse
            across = high[k]
            root_low = jnp.where(sub == k, root, root_low)
            for j in range(PANEL):
                if j < SUB and j != k:
                    line = low[j][k : k + 1, :]
                    low[j] = low[j] - take_low * line
                    high[j] = high[j] - take_high * line
                elif j >= SUB:
                    high[j] = high[j] - take_high * across[j - SUB : j - SUB + 1, :]
            low[k] = jnp.where(sub == k, 1.0, -take_low)
            high[k] = -take_high
        else:
            s = k - SUB
            take_high = jnp.where(sub > s, high[k], 0.0) * inverse
            root_high = jnp.where(sub == s, root, root_high)
            for j in range(PANEL):
                if j != k:
                    high[j] = high[j] - take_high * high[j][s : s + 1, :]
            high[k] = jnp.where(sub == s, 1.0, -take_high)
    return [low[j] * root_low for j in range(SUB)], [high[j] * root_high for j in range(PANEL)]


def tree_sum(terms):
    while len(terms) > 1:
        pairs = [terms[i] + terms[i + 1] for i in range(0, len(terms) - 1, 2)]
        terms = pairs + terms[2 * len(pairs) :]
    return terms[0]


def block_inverse(rows):
    lane = lax.broadcasted_iota(jnp.int32, (SUB, BLOCK), 1)
    sub = lax.broadcasted_iota(jnp.int32, (SUB, BLOCK), 0)
    rows = list(rows)
    out = [None] * len(rows)
    for panel in range(BLOCK // PANEL):
        first = PANEL * panel
        at = 2 * panel

        def splat(piece, j):
            return jnp.broadcast_to(piece[:, first + j : first + j + 1], (SUB, BLOCK))

        rest = range(at + 2, len(rows))
        near, far = rest[:2], rest[2:]
        low = [splat(rows[at], j) for j in range(SUB)]
        high = [splat(rows[at + 1], j) for j in range(PANEL)]
        coef = {r: [splat(rows[r], j) for j in range(PANEL)] for r in near}
        inv_low, inv_high = panel_inverse(low, high)
        in_panel = (lane >= first) & (lane < first + PANEL)
        top = jnp.where(in_panel, jnp.where(lane - first == sub, 1.0, 0.0), rows[at])
        bottom = jnp.where(in_panel, jnp.where(lane - first - SUB == sub, 1.0, 0.0), rows[at + 1])
        entries = [top[j : j + 1, :] for j in range(SUB)] + [bottom[j : j + 1, :] for j in range(SUB)]
        new_low = tree_sum([inv_low[j] * entries[j] for j in range(SUB)])
        new_high = tree_sum([inv_high[j] * entries[j] for j in range(PANEL)])
        out[at] = jnp.where(lane <= first + sub, new_low, 0.0)
        out[at + 1] = jnp.where(lane <= first + SUB + sub, new_high, 0.0)
        if len(near):
            weights = []
            for j in range(PANEL):
                term = inv_high[j] * new_high
                if j < SUB:
                    term = term + inv_low[j] * new_low
                weights.append(jnp.sum(term, axis=0, keepdims=True))
            for r in near:
                piece = jnp.where(in_panel, 0.0, rows[r])
                for j in range(PANEL):
                    piece = piece - coef[r][j] * weights[j]
                rows[r] = piece
        if len(far):
            spread = []
            for part in parts_of(jnp.concatenate(weights, axis=0)):
                above = [jnp.zeros((first, BLOCK), jnp.bfloat16)] if first else []
                below = [jnp.zeros((BLOCK - first - PANEL, BLOCK), jnp.bfloat16)]
                spread.append(jnp.concatenate(above + [part] + below, axis=0))
            far_rows = parts_of(jnp.concatenate([rows[r] for r in far], axis=0))
            change = dot_parts(far_rows, spread, ((1,), (0,)))
            for i, r in enumerate(far):
                rows[r] = jnp.where(in_panel, 0.0, rows[r]) - change[SUB * i : SUB * (i + 1)]
    return out


def parts_of(value):
    high = value.astype(jnp.bfloat16)
    rest = value - high.astype(jnp.float32)
    middle = rest.astype(jnp.bfloat16)
    low = (rest - middle.astype(jnp.float32)).astype(jnp.bfloat16)
    return high, middle, low


def product(left, right, dims):
    return lax.dot_general(left, right, (dims, ((), ())), preferred_element_type=jnp.float32)


def dot_parts(left, right, dims):
    high, middle, low = left
    other_high, other_middle, other_low = right
    one = jnp.concatenate([low, high, middle, middle, high, high], axis=dims[0][0])
    two = jnp.concatenate(
        [other_high, other_low, other_middle, other_high, other_middle, other_high], axis=dims[1][0]
    )
    return product(one, two, dims)


def pick_rows(pick, value, dims):
    high, middle, low = parts_of(value)
    return product(pick, high, dims) + product(pick, middle, dims) + product(pick, low, dims)


def matern(cols, rows, col_scale, row_scale):
    dist_sq = None
    for axis_id in range(3):
        offset = cols[axis_id] - rows[axis_id]
        dist_sq = offset * offset if dist_sq is None else dist_sq + offset * offset
    scaled = dist_sq * lax.rsqrt(jnp.maximum(dist_sq, 1e-30))
    shape_term = (1.0 + scaled + dist_sq * (1.0 / 3.0)) * jnp.exp(-scaled)
    return col_scale * row_scale * shape_term


def prep_kernel(
    me_ref,
    owner_hbm,
    offset_hbm,
    points_hbm,
    amp_hbm,
    noise_hbm,
    cov_hbm,
    out_ref,
    owner_ref,
    offset_ref,
    points_ref,
    amp_ref,
    noise_ref,
    rows_ref,
    sem,
    load_sem,
):
    pairs = (
        (owner_hbm, owner_ref),
        (offset_hbm, offset_ref),
        (points_hbm, points_ref),
        (amp_hbm, amp_ref),
        (noise_hbm, noise_ref),
    )
    loads = [pltpu.make_async_copy(*pair, load_sem.at[i]) for i, pair in enumerate(pairs)]
    for load in loads:
        load.start()
    me = me_ref[0]
    blocks, width = owner_ref.shape
    slots = CAP * blocks
    for load in loads[:2]:
        load.wait()
    lane = lax.broadcasted_iota(jnp.int32, (blocks, width), 1).astype(jnp.float32)
    block = lax.broadcasted_iota(jnp.int32, (blocks, width), 0)
    mine = owner_ref[...] == me
    offset = offset_ref[...].astype(jnp.float32)
    first = jnp.min(jnp.where(mine, lane, 1e4), axis=1, keepdims=True)
    last = jnp.max(jnp.where(mine, lane, -1.0), axis=1, keepdims=True)
    chosen = [jnp.where(mine & (lane == at), offset, 0.0) for at in (first, last)]
    copies = []
    slot_row = lax.broadcasted_iota(jnp.int32, (slots, 1), 0)
    offsets = jnp.zeros((slots, 1), jnp.int32)
    for s in range(slots):
        value = jnp.sum(jnp.where(block == s // CAP, chosen[s % CAP], 0.0)).astype(jnp.int32)
        copy = pltpu.make_async_copy(cov_hbm.at[pl.ds(value, 1), :], rows_ref.at[pl.ds(s, 1), :], sem.at[s])
        copy.start()
        copies.append(copy)
        offsets = jnp.where(slot_row == s, value, offsets)
    for load in loads[2:]:
        load.wait()
    local_rows = points_ref.shape[1]
    hit = lax.broadcasted_iota(jnp.int32, (slots, local_rows), 1) == offsets
    sources = [points_ref[i : i + 1, :] for i in range(3)] + [amp_ref[...], noise_ref[...]]
    sub = lax.broadcasted_iota(jnp.int32, (SUB, BLOCK), 0)
    diagonal = sub == lax.broadcasted_iota(jnp.int32, (SUB, BLOCK), 1)
    scalars = jnp.zeros((SUB, BLOCK), jnp.float32)
    for i, source in enumerate(sources):
        column = jnp.sum(jnp.where(hit, source, 0.0), axis=1, keepdims=True)
        line = jnp.sum(jnp.where(diagonal, column, 0.0), axis=0, keepdims=True)
        scalars = jnp.where(sub == i, line, scalars)
    for copy in copies:
        copy.wait()
    half = rows_ref.shape[1] // 2
    left, right = rows_ref[:, :half], rows_ref[:, half:]
    for i in range(out_ref.shape[0]):
        out_ref[i, :slots, :] = left
        out_ref[i, slots : 2 * slots, :] = right
        out_ref[i, 2 * slots :, :] = scalars


def aux_kernel(
    me_ref,
    owner_hbm,
    offset_hbm,
    points_hbm,
    amp_hbm,
    noise_hbm,
    cov_hbm,
    high_ref,
    middle_ref,
    low_ref,
    feat_ref,
    base_ref,
    info_ref,
    match_ref,
    comb_ref,
    left_ref,
    most_ref,
    owner_ref,
    offset_ref,
    points_ref,
    amp_ref,
    noise_ref,
    cov_ref,
    load_sem,
):
    pairs = (
        (owner_hbm, owner_ref),
        (offset_hbm, offset_ref),
        (points_hbm, points_ref),
        (amp_hbm, amp_ref),
        (noise_hbm, noise_ref),
        (cov_hbm, cov_ref),
    )
    loads = [pltpu.make_async_copy(*pair, load_sem.at[i]) for i, pair in enumerate(pairs)]
    for load in loads:
        load.start()
    me = me_ref[0]
    blocks, width = owner_ref.shape
    for load in loads[:2]:
        load.wait()
    local_rows, cov_width = cov_ref.shape
    half = cov_width // 2
    owner = owner_ref[...]
    padded = jnp.concatenate([owner, jnp.zeros((SUB - blocks, width), jnp.int32)], axis=0)
    owner_t = padded.astype(jnp.float32).T.astype(jnp.int32)
    sub = lax.broadcasted_iota(jnp.int32, (width, width), 0)
    lane = lax.broadcasted_iota(jnp.int32, (width, width), 1)
    xy = (owner >> 1) & 15
    xy_t = (owner_t >> 1) & 15
    my_xy = lax.rem(lax.div(me, 2), 16)
    seats = []
    candidates = []
    infos = []
    for b in range(blocks):
        count = jnp.zeros((1, width), jnp.float32)
        for earlier in range(b + 1):
            same = xy_t[:, earlier : earlier + 1] == xy[b : b + 1, :]
            if earlier == b:
                same = same & (sub < lane)
            count = count + jnp.sum(jnp.where(same, 1.0, 0.0), axis=0, keepdims=True)
        twin = (owner_t[:, b : b + 1] == owner[b : b + 1, :]) & (sub < lane)
        rank = jnp.sum(jnp.where(twin, 1.0, 0.0), axis=0, keepdims=True).astype(jnp.int32)
        count = count.astype(jnp.int32)
        row = owner[b : b + 1, :]
        seats.append(jnp.where(xy[b : b + 1, :] == my_xy, count, -1))
        candidates.append((row >> 5) * 16 + (row & 1) * SUB + CAP * b + rank)
        infos.append(count)
    info_ref[:blocks, :] = xy.astype(jnp.float32)
    counts = jnp.concatenate(infos, axis=0).astype(jnp.float32)
    info_ref[blocks:, :] = counts
    most_ref[0] = jnp.max(counts).astype(jnp.int32) + 1
    match = jnp.where(owner == me, offset_ref[...], -1)
    match_ref[...] = jnp.concatenate([match[b : b + 1, :] for b in range(blocks)], axis=1)
    seat = jnp.concatenate(seats, axis=1)
    candidate = jnp.concatenate(candidates, axis=1)
    ids = lax.broadcasted_iota(jnp.int32, (BLOCK, blocks * width), 0)
    seat_hit = (ids == seat).astype(jnp.float32).astype(jnp.bfloat16)
    candidate_hit = (ids == candidate).astype(jnp.float32).astype(jnp.bfloat16)
    comb_ref[...] = product(seat_hit, candidate_hit, ((1,), (1,)))

    for load in loads[2:]:
        load.wait()
    feat_ref[:3, :] = points_ref[...]
    feat_ref[3:4, :] = amp_ref[...]
    feat_ref[4:5, :] = noise_ref[...]
    feat_ref[5:, :] = jnp.zeros((3, local_rows), jnp.float32)
    diagonal = sub == lane
    scale = (5.0**0.5) / LENGTH_SCALE
    order = (0, 0, 1, 1, 0, 2)

    def step(t, carry):
        at = pl.ds(pl.multiple_of(t * BLOCK, BLOCK), BLOCK)
        cov = cov_ref[at, :]
        high, middle, low = parts_of(cov)
        high_ref[at, :] = high
        middle_ref[at, :] = middle
        low_ref[at, :] = low
        squares = cov * cov
        line = jnp.sum(squares[:, :half] + squares[:, half:], axis=1, keepdims=True)
        total = jnp.sum(jnp.where(diagonal, line, 0.0), axis=0, keepdims=True)
        points = (points_ref[:, at] - 0.5) * scale
        point_parts = [part.astype(jnp.float32) for part in parts_of(points)]
        length = jnp.sum(points * points, axis=0, keepdims=True)
        lines = [point_parts[k][i : i + 1, :] for i in range(3) for k in order]
        lines += [part.astype(jnp.float32) for part in parts_of(length)] + [jnp.ones((3, BLOCK), jnp.float32)]
        lines.append(jnp.zeros((BLOCK - 6 * len(order) + 12, BLOCK), jnp.float32))
        left_ref[at, :] = jnp.concatenate(lines, axis=0).T.astype(jnp.bfloat16)
        amplitude = amp_ref[:, at]
        base_ref[pl.ds(t, 1), :] = amplitude * amplitude + noise_ref[:, at] + total
        return carry

    lax.fori_loop(0, local_rows // BLOCK, step, 0)


def seat_kernel(me_ref, comb_ref, got_ref, out_ref):
    core = lax.rem(me_ref[0], 2)
    senders = got_ref.shape[0]
    slots = (got_ref.shape[1] - SUB) // 2
    seats = out_ref.shape[1] - SUB
    comb = comb_ref[...].astype(jnp.bfloat16)
    left = jnp.concatenate([got_ref[i, :slots, :] for i in range(senders)], axis=0)
    right = jnp.concatenate([got_ref[i, slots : 2 * slots, :] for i in range(senders)], axis=0)
    rows = jnp.where(core == 0, left, right)
    packed = pick_rows(comb[: -(-seats // 16) * 16], rows, ((1,), (0,)))[:seats]
    lane = lax.broadcasted_iota(jnp.int32, (SUB, BLOCK), 1)
    scalars = jnp.zeros((SUB, BLOCK), jnp.float32)
    for i in range(senders):
        piece = got_ref[i, 2 * slots :, :]
        piece = pltpu.roll(piece, i * slots, 1) if i else piece
        scalars = jnp.where(lane // slots == i, piece, scalars)
    high, middle, low = parts_of(scalars)
    dims = ((1,), (1,))
    seated = product(high, comb, dims) + product(middle, comb, dims) + product(low, comb, dims)
    for i in range(out_ref.shape[0]):
        out_ref[i, :seats, :] = packed
        out_ref[i, seats:, :] = seated


def field_kernel(mine_ref, info_ref, match_ref, feat_ref, left_ref, scal_ref, field_ref, col_ref):
    pivots = match_ref.shape[1]
    local_rows = feat_ref.shape[1]
    planes, plane_rows, _ = mine_ref.shape
    seats = plane_rows - SUB
    blocks = pivots // BLOCK
    nt = ((1,), (1,))
    packed = BLOCK // plane_rows if BLOCK % plane_rows == 0 else 1
    stride = BLOCK // packed
    lane = lax.broadcasted_iota(jnp.int32, (SUB, BLOCK), 1)
    lines = []
    for q in range(planes // packed):
        line = mine_ref[q * packed, seats:, :]
        for t in range(1, packed):
            piece = pltpu.roll(mine_ref[q * packed + t, seats:, :], t * stride, 1)
            line = jnp.where(lane // stride == t, piece, line)
        lines.append(line)
    line_parts = parts_of(jnp.concatenate(lines, axis=1))
    info_t = info_ref[...].T
    for b in range(blocks):
        here = pl.ds(b * BLOCK, BLOCK)
        xy, seat = info_t[:, b : b + 1], info_t[:, blocks + b : blocks + b + 1]
        place = (xy * stride + seat).astype(jnp.int32)
        ids = lax.broadcasted_iota(jnp.int32, (BLOCK, planes * stride), 1)
        line_pick = (ids == place).astype(jnp.float32).astype(jnp.bfloat16)
        scal_ref[:, here] = (
            product(line_parts[0], line_pick, nt)
            + product(line_parts[1], line_pick, nt)
            + product(line_parts[2], line_pick, nt)
        )
    for t in range(local_rows // BLOCK):
        at = pl.ds(t * BLOCK, BLOCK)
        col_ref[at, :] = feat_ref[:, at].T
    piv = scal_ref[...]
    piv_scale = piv[3:4, :]
    match = match_ref[...]

    scale = (5.0**0.5) / LENGTH_SCALE
    points = (piv[:3, :] - 0.5) * scale
    length = jnp.sum(points * points, axis=0, keepdims=True)
    point_parts = [part.astype(jnp.float32) * -2.0 for part in parts_of(points)]
    lines = [point_parts[k][i : i + 1, :] for i in range(3) for k in (0, 1, 0, 1, 2, 0)]
    lines += [jnp.ones((3, pivots), jnp.float32)] + [part.astype(jnp.float32) for part in parts_of(length)]
    lines.append(jnp.zeros((BLOCK - 24, pivots), jnp.float32))
    right = jnp.concatenate(lines, axis=0).astype(jnp.bfloat16)

    def step(t, carry):
        at = pl.ds(pl.multiple_of(t * WIDE, WIDE), WIDE)
        cols = col_ref[at, :]
        dist_sq = jnp.maximum(product(left_ref[at, :], right, ((1,), (0,))), 1e-30)
        scaled = dist_sq * lax.rsqrt(dist_sq)
        value = (1.0 + scaled + dist_sq * (1.0 / 3.0)) * jnp.exp2(scaled * -LOG2E)
        value = cols[:, 3:4] * piv_scale * value
        row_ids = lax.broadcasted_iota(jnp.int32, (WIDE, 1), 0) + t * WIDE
        field_ref[at, :] = value + jnp.where(row_ids == match, cols[:, 4:5], 0.0)
        return carry

    lax.fori_loop(0, local_rows // WIDE, step, 0)


def main_kernel(
    me_ref,
    mine_ref,
    other_ref,
    info_ref,
    scal_ref,
    field_ref,
    base_ref,
    high_hbm,
    middle_hbm,
    low_hbm,
    out_hbm,
    resid_ref,
    sums_ref,
    cov_high,
    cov_middle,
    cov_low,
    table_high,
    table_middle,
    table_low,
    kernel_high,
    kernel_middle,
    kernel_low,
    z_ref,
    r_ref,
    tile_ref,
    load_sem,
    store_sem,
):
    core = lax.rem(me_ref[0], 2)
    pivots = z_ref.shape[0]
    local_rows, cov_width = cov_high.shape
    planes, plane_rows, half = mine_ref.shape
    blocks = pivots // BLOCK
    loads = [
        pltpu.make_async_copy(source, target, load_sem.at[i])
        for i, (source, target) in enumerate(
            ((high_hbm, cov_high), (middle_hbm, cov_middle), (low_hbm, cov_low))
        )
    ]
    for load in loads:
        load.start()
    nt = ((1,), (1,))

    scale = (5.0**0.5) / LENGTH_SCALE
    candidates = planes * plane_rows
    mine = mine_ref[...].reshape(candidates, half)
    other = other_ref[...].reshape(candidates, half)
    both = jnp.concatenate([jnp.where(core == 0, mine, other), jnp.where(core == 0, other, mine)], axis=1)
    both_parts = parts_of(both)
    info_t = info_ref[...].T
    for b in range(blocks):
        here = pl.ds(b * BLOCK, BLOCK)
        xy, seat = info_t[:, b : b + 1], info_t[:, blocks + b : blocks + b + 1]
        place = (xy * plane_rows + seat).astype(jnp.int32)
        ids = lax.broadcasted_iota(jnp.int32, (BLOCK, candidates), 1)
        pick = (ids == place).astype(jnp.float32).astype(jnp.bfloat16)
        for part, table in zip(both_parts, (table_high, table_middle, table_low)):
            table[here, :] = product(pick, part, ((1,), (0,))).astype(jnp.bfloat16)

    piv = scal_ref[...]
    piv_rows = [piv[i : i + 1, :] * scale for i in range(3)]
    piv_scale, piv_noise = piv[3:4, :], piv[4:5, :]

    for b in range(blocks):
        here = pl.ds(b * BLOCK, BLOCK)
        right = slice(b * BLOCK, pivots)
        cols = scal_ref[:, here].T
        piece = matern(
            [cols[:, i : i + 1] * scale for i in range(3)],
            [row[:, right] for row in piv_rows],
            cols[:, 3:4],
            piv_scale[:, right],
        )
        same = lax.broadcasted_iota(jnp.int32, (BLOCK, 1), 0) == lax.broadcasted_iota(
            jnp.int32, (1, pivots - b * BLOCK), 1
        )
        piece = piece + jnp.where(same, piv_noise[:, right], 0.0)
        left_parts = [table[here, :] for table in (table_high, table_middle, table_low)]
        right_parts = [table[right, :] for table in (table_high, table_middle, table_low)]
        z_ref[here, right] = piece + dot_parts(left_parts, right_parts, nt)
        if b:
            z_ref[here, : b * BLOCK] = jnp.zeros((BLOCK, b * BLOCK), jnp.float32)
    for load in loads:
        load.wait()
    def kernel_tile(t):
        at = pl.ds(pl.multiple_of(t * WIDE, WIDE), WIDE)
        cov = [part[at, :] for part in (cov_high, cov_middle, cov_low)]
        kernel = field_ref[at, :] + dot_parts(cov, (table_high[...], table_middle[...], table_low[...]), nt)
        for part, target in zip(parts_of(kernel), (kernel_high, kernel_middle, kernel_low)):
            target[at, :] = part

    per_step = local_rows // WIDE // blocks

    def step(b, carry):
        at = pl.ds(pl.multiple_of(b * BLOCK, BLOCK), BLOCK)
        pieces = [
            z_ref[pl.ds(pl.multiple_of(b * BLOCK + SUB * i, SUB), SUB), at]
            for i in range(BLOCK // SUB)
        ]
        inverse = jnp.concatenate(block_inverse(pieces), axis=0)
        for i in range(per_step):
            kernel_tile(b * per_step + i)
        r_ref[...] = dot_parts(parts_of(inverse), parts_of(z_ref[at, :]), ((1,), (0,)))
        r_ref[:, at] = inverse
        z_ref[:, at] = jnp.zeros((pivots, BLOCK), jnp.float32)
        row = r_ref[...]
        for s in range(blocks - 1):

            @pl.when(b == s)
            def _():
                later = slice((s + 1) * BLOCK, pivots)
                coef = parts_of(row[:, later].T)
                z_ref[later, :] -= dot_parts(coef, parts_of(row), ((1,), (0,)))

        z_ref[at, :] = row
        return carry

    lax.fori_loop(0, blocks, step, 0)

    diagonal = lax.broadcasted_iota(jnp.int32, (BLOCK, BLOCK), 0) == lax.broadcasted_iota(
        jnp.int32, (BLOCK, BLOCK), 1
    )
    left = pivots // 2
    half_tiles = WIDE // BLOCK
    tiles = local_rows // WIDE
    inverse_parts = parts_of(z_ref[...])
    for part, target in zip(inverse_parts, (table_high, table_middle, table_low)):
        target[:, :] = part[:, :left]
    late = [part[left:, left:] for part in inverse_parts]

    def tile_step(t, taken):
        at = pl.ds(pl.multiple_of(t * WIDE, WIDE), WIDE)
        slot = lax.rem(t, 2)

        @pl.when(t >= 2)
        def _():
            pltpu.make_async_copy(tile_ref.at[slot], out_hbm.at[at, :], store_sem.at[slot]).wait()

        kernels = [part[at, :] for part in (kernel_high, kernel_middle, kernel_low)]
        early = [part[:, :left] for part in kernels]
        first = dot_parts(early, [table[:left, :] for table in (table_high, table_middle, table_low)], nt)
        second = dot_parts(early, [table[left:, :] for table in (table_high, table_middle, table_low)], nt)
        second = second + dot_parts([part[:, left:] for part in kernels], late, nt)
        tile_ref[slot, :, :left] = first
        tile_ref[slot, :, left:] = second
        pltpu.make_async_copy(tile_ref.at[slot], out_hbm.at[at, :], store_sem.at[slot]).start()
        total = jnp.zeros((WIDE, BLOCK), jnp.float32)
        new_taken = []
        for b in range(blocks):
            source = first if b * BLOCK < left else second
            piece = source[:, (b * BLOCK) % left : (b * BLOCK) % left + BLOCK]
            square = piece * piece
            total = total + square
            new_taken.append(taken[b] + jnp.sum(square.reshape(WIDE // SUB, SUB, BLOCK), axis=0))
        line = jnp.sum(total, axis=1, keepdims=True)
        for h in range(half_tiles):
            spread = jnp.where(diagonal, line[h * BLOCK : (h + 1) * BLOCK, :], 0.0)
            where = pl.ds(t * half_tiles + h, 1)
            resid_ref[where, :] = base_ref[where, :] - jnp.sum(spread, axis=0, keepdims=True)
        return tuple(new_taken)

    zero = jnp.zeros((SUB, BLOCK), jnp.float32)
    taken = lax.fori_loop(0, tiles, tile_step, (zero,) * blocks)
    for tile in (tiles - 2, tiles - 1):
        at = pl.ds(tile * WIDE, WIDE)
        pltpu.make_async_copy(tile_ref.at[tile % 2], out_hbm.at[at, :], store_sem.at[tile % 2]).wait()

    total = jnp.sum(base_ref[...])
    lanes = lax.broadcasted_iota(jnp.int32, sums_ref.shape, 1)
    sums = jnp.zeros(sums_ref.shape, jnp.float32)
    for b in range(blocks):
        total = total - jnp.sum(taken[b])
        sums = jnp.where(lanes == b, total, sums)
    sums_ref[...] = sums


def last_kernel(sums_ref, resid_ref, weights_ref, mean_ref, *, rows):
    devices, _, width = sums_ref.shape
    total = jnp.sum(sums_ref[...].reshape(devices, width), axis=0, keepdims=True)
    mean = total * (1.0 / rows)
    count = mean_ref.shape[1]
    mean_ref[...] = mean[:, :count]
    weights_ref[...] = resid_ref[...] / mean[:, count - 1 : count]


def shape(dims, dtype=jnp.float32):
    return jax.ShapeDtypeStruct(dims, dtype)


VMEM = pl.BlockSpec(memory_space=pltpu.VMEM)
SMEM = pl.BlockSpec(memory_space=pltpu.SMEM)
ANY = pl.BlockSpec(memory_space=pl.ANY)
PARAMS = pltpu.CompilerParams(vmem_limit_bytes=40 << 20)
AUX_PARAMS = pltpu.CompilerParams(vmem_limit_bytes=55 << 20)


def prep(me, owner, offset, points, amp, noise, cov, copies):
    slots = CAP * owner.shape[0]
    return pl.pallas_call(
        prep_kernel,
        out_shape=shape((copies, 2 * slots + SUB, BLOCK)),
        in_specs=[SMEM] + [ANY] * 6,
        out_specs=VMEM,
        scratch_shapes=[pltpu.VMEM(value.shape, value.dtype) for value in (owner, offset, points, amp, noise)]
        + [
            pltpu.VMEM((slots, cov.shape[1]), jnp.float32),
            pltpu.SemaphoreType.DMA((slots,)),
            pltpu.SemaphoreType.DMA((5,)),
        ],
        compiler_params=pltpu.CompilerParams(vmem_limit_bytes=60 << 20),
        name="prep",
    )(me, owner, offset, points, amp, noise, cov)


def aux(me, owner, offset, points, amp, noise, cov):
    rows, width = cov.shape
    return pl.pallas_call(
        aux_kernel,
        out_shape=(
            shape((rows, width), jnp.bfloat16),
            shape((rows, width), jnp.bfloat16),
            shape((rows, width), jnp.bfloat16),
            shape((SUB, rows)),
            shape((rows // BLOCK, BLOCK)),
            shape((SUB, BLOCK)),
            shape((1, owner.size), jnp.int32),
            shape((BLOCK, BLOCK)),
            shape((rows, BLOCK), jnp.bfloat16),
            shape((1,), jnp.int32),
        ),
        in_specs=[SMEM] + [ANY] * 6,
        out_specs=(VMEM,) * 9 + (SMEM,),
        scratch_shapes=[pltpu.VMEM(value.shape, value.dtype) for value in (owner, offset, points, amp, noise, cov)]
        + [pltpu.SemaphoreType.DMA((6,))],
        compiler_params=AUX_PARAMS,
        cost_estimate=pl.CostEstimate(flops=10**8, bytes_accessed=6 << 20, transcendentals=0),
        name="aux",
    )(me, owner, offset, points, amp, noise, cov)


def seat(me, comb, got, copies, seats):
    return pl.pallas_call(
        seat_kernel,
        out_shape=shape((copies, seats + SUB, BLOCK)),
        in_specs=[SMEM, VMEM, VMEM],
        out_specs=VMEM,
        compiler_params=PARAMS,
        name="seat",
    )(me, comb, got)


def field(mine, info, match, feat, left):
    pivots, rows = match.shape[1], feat.shape[1]
    return pl.pallas_call(
        field_kernel,
        out_shape=(shape((SUB, pivots)), shape((rows, pivots))),
        in_specs=[VMEM] * 5,
        out_specs=(VMEM, VMEM),
        scratch_shapes=[pltpu.VMEM((rows, SUB), jnp.float32)],
        compiler_params=PARAMS,
        cost_estimate=pl.CostEstimate(flops=10**8, bytes_accessed=6 << 20, transcendentals=0),
        name="field",
    )(mine, info, match, feat, left)


def main(me, mine, other, info, scal, local_field, base, high, middle, low, devices):
    rows, width = high.shape
    pivots = scal.shape[1]
    bf = jnp.bfloat16
    return pl.pallas_call(
        main_kernel,
        out_shape=(shape((rows, pivots)), shape((rows // BLOCK, BLOCK)), shape((devices, BLOCK))),
        in_specs=[SMEM] + [VMEM] * 6 + [ANY] * 3,
        out_specs=(ANY, VMEM, VMEM),
        scratch_shapes=[pltpu.VMEM((rows, width), bf)] * 3
        + [pltpu.VMEM((pivots, width), bf)] * 3
        + [pltpu.VMEM((rows, pivots), bf)] * 3
        + [
            pltpu.VMEM((pivots, pivots), jnp.float32),
            pltpu.VMEM((BLOCK, pivots), jnp.float32),
            pltpu.VMEM((2, WIDE, pivots), jnp.float32),
            pltpu.SemaphoreType.DMA((3,)),
            pltpu.SemaphoreType.DMA((2,)),
        ],
        compiler_params=PARAMS,
        name="factor_rows",
    )(me, mine, other, info, scal, local_field, base, high, middle, low)


def last(sums, resid, blocks, rows):
    return pl.pallas_call(
        functools.partial(last_kernel, rows=rows),
        out_shape=(shape(resid.shape), shape((1, blocks))),
        in_specs=[VMEM, VMEM],
        out_specs=(VMEM, VMEM),
        compiler_params=PARAMS,
        name="last",
    )(sums, resid)


def local(locations, amplitude, noise, covariates, pivot_owner, pivot_offset):
    me = lax.axis_index(AXES).astype(jnp.int32)[None]
    blocks = pivot_owner.shape[0]
    sizes = [lax.axis_size(name) for name in AXES]
    devices = sizes[0] * sizes[1] * sizes[2] * sizes[3]
    swap = [(0, 1), (1, 0)]
    amp, nugget = amplitude[None], noise[None]
    args = (me, pivot_owner, pivot_offset, locations, amp, nugget, covariates)

    column = lax.all_to_all(prep(*args, sizes[0] * sizes[3]), ("z", "c"), 0, 0, tiled=True)
    high, middle, low, feat, base, info, match, comb, left, most = aux(*args)

    def rest(seats):
        def run(column, comb, info, match, feat, left, base, high, middle, low):
            message = seat(me, comb, column, sizes[1] * sizes[2], seats)
            mine = lax.all_to_all(message, ("x", "y"), 0, 0, tiled=True)
            other = lax.ppermute(mine, "c", swap)
            scal, local_field = field(mine, info, match, feat, left)
            return main(me, mine, other, info, scal, local_field, base, high, middle, low, devices)

        return run

    operands = (column, comb, info, match, feat, left, base, high, middle, low)
    if FEW:
        factor, resid, sums = lax.cond(most[0] <= FEW, rest(FEW), rest(BLOCK), *operands)
    else:
        factor, resid, sums = rest(BLOCK)(*operands)
    all_sums = lax.all_to_all(sums[:, None, :], AXES, 0, 0, tiled=True)
    weights, mean_residual = last(all_sums, resid, blocks, locations.shape[1] * devices)
    return (factor, weights.reshape(-1), mean_residual.reshape(-1))


def solution(mesh):
    named = Mesh(mesh.devices.reshape(8, 4, 4, 2), AXES)
    return jax.shard_map(
        local,
        mesh=named,
        in_specs=(P(None, AXES), P(AXES), P(AXES), P(AXES, None), P(), P()),
        out_specs=(P(AXES, None), P(AXES), P()),
        check_vma=False,
    )
```

```python
import functools

import jax
import jax.numpy as jnp
from jax import lax
from jax.experimental import pallas as pl
from jax.experimental.pallas import tpu as pltpu
from jax.sharding import Mesh
from jax.sharding import PartitionSpec as P

LENGTH_SCALE = 0.3
CAP = 2
AXES = ("z", "x", "y", "c")
HIGHEST = lax.Precision.HIGHEST
BLOCK = 128
PANEL = 16
SUB = 8
TILE = 256
FEW = 56
WIDE = 512
LOG2E = 1.4426950408889634


def dot(left, right, dims):
    return lax.dot_general(
        left, right, (dims, ((), ())), precision=HIGHEST, preferred_element_type=jnp.float32
    )


def panel_rows(low, high, near, top, bottom, near_rows):
    sub = lax.broadcasted_iota(jnp.int32, (SUB, BLOCK), 0)
    low, high, near, near_rows = list(low), list(high), [list(one) for one in near], list(near_rows)
    root_low = jnp.zeros((SUB, BLOCK), jnp.float32)
    root_high = root_low

    def entry(j, i):
        piece = low[j][i : i + 1, :] if i < SUB else high[j][i - SUB : i - SUB + 1, :]
        return jnp.broadcast_to(piece, (SUB, BLOCK))

    pivot = entry(0, 0)
    for k in range(PANEL):
        inverse = pl.reciprocal(pivot, approx=True)
        root = lax.rsqrt(pivot)
        if k + 1 < PANEL:
            side = entry(k, k + 1)
            pivot = entry(k + 1, k + 1) - (side * side) * inverse
        take_near = [one[k] * inverse for one in near]
        if k < SUB:
            take_low = jnp.where(sub > k, low[k], 0.0) * inverse
            take_high = high[k] * inverse
            root_low = jnp.where(sub == k, root, root_low)
            line = top[k : k + 1, :]
        else:
            take_high = jnp.where(sub > k - SUB, high[k], 0.0) * inverse
            root_high = jnp.where(sub == k - SUB, root, root_high)
            line = bottom[k - SUB : k - SUB + 1, :]
        for j in range(k + 1, PANEL):
            across = entry(k, j)
            if j < SUB:
                low[j] = low[j] - take_low * across
            high[j] = high[j] - take_high * across
            for one, take in zip(near, take_near):
                one[j] = one[j] - take * across
        if k < SUB:
            top = top - take_low * line
        bottom = bottom - take_high * line
        near_rows = [row - take * line for row, take in zip(near_rows, take_near)]
    return top * root_low, bottom * root_high, near_rows


def block_inverse(rows):
    lane = lax.broadcasted_iota(jnp.int32, (SUB, BLOCK), 1)
    sub = lax.broadcasted_iota(jnp.int32, (SUB, BLOCK), 0)
    rows = list(rows)
    out = [None] * len(rows)
    for panel in range(BLOCK // PANEL):
        first = PANEL * panel
        at = 2 * panel

        def splat(piece, j):
            return jnp.broadcast_to(piece[:, first + j : first + j + 1], (SUB, BLOCK))

        rest = range(at + 2, len(rows))
        near, far = rest[:2], rest[2:]
        low = [splat(rows[at], j) for j in range(SUB)]
        high = [splat(rows[at + 1], j) for j in range(PANEL)]
        next_columns = [[splat(rows[r], j) for j in range(PANEL)] for r in near]
        in_panel = (lane >= first) & (lane < first + PANEL)
        top = jnp.where(in_panel, jnp.where(lane - first == sub, 1.0, 0.0), rows[at])
        bottom = jnp.where(in_panel, jnp.where(lane - first - SUB == sub, 1.0, 0.0), rows[at + 1])
        next_rows = [jnp.where(in_panel, 0.0, rows[r]) for r in near]
        new_low, new_high, next_rows = panel_rows(low, high, next_columns, top, bottom, next_rows)
        out[at] = jnp.where(lane <= first + sub, new_low, 0.0)
        out[at + 1] = jnp.where(lane <= first + SUB + sub, new_high, 0.0)
        for r, row in zip(near, next_rows):
            rows[r] = row
        if len(far):
            new_rows = jnp.concatenate([new_low, new_high], axis=0)
            filler = jnp.zeros((BLOCK - PANEL, BLOCK), jnp.float32)
            flipped = jnp.concatenate([new_rows, filler], axis=0).T
            far_parts = parts_of(flipped[SUB * far[0] : SUB * (far[-1] + 1), :])
            spread = [
                jnp.concatenate([part, filler.astype(jnp.bfloat16)], axis=0) for part in parts_of(new_rows)
            ]
            change = dot_parts(far_parts, spread, ((1,), (0,)))
            for i, r in enumerate(far):
                rows[r] = jnp.where(in_panel, 0.0, rows[r]) - change[SUB * i : SUB * (i + 1)]
    return out


def parts_of(value):
    high = value.astype(jnp.bfloat16)
    rest = value - high.astype(jnp.float32)
    middle = rest.astype(jnp.bfloat16)
    low = (rest - middle.astype(jnp.float32)).astype(jnp.bfloat16)
    return high, middle, low


def product(left, right, dims):
    return lax.dot_general(left, right, (dims, ((), ())), preferred_element_type=jnp.float32)


def dot_parts(left, right, dims):
    high, middle, low = left
    other_high, other_middle, other_low = right
    one = jnp.concatenate([low, high, middle, middle, high, high], axis=dims[0][0])
    two = jnp.concatenate(
        [other_high, other_low, other_middle, other_high, other_middle, other_high], axis=dims[1][0]
    )
    return product(one, two, dims)


def pick_rows(pick, value, dims):
    high, middle, low = parts_of(value)
    return product(pick, high, dims) + product(pick, middle, dims) + product(pick, low, dims)


def matern(cols, rows, col_scale, row_scale):
    dist_sq = None
    for axis_id in range(3):
        offset = cols[axis_id] - rows[axis_id]
        dist_sq = offset * offset if dist_sq is None else dist_sq + offset * offset
    scaled = dist_sq * lax.rsqrt(jnp.maximum(dist_sq, 1e-30))
    shape_term = (1.0 + scaled + dist_sq * (1.0 / 3.0)) * jnp.exp(-scaled)
    return col_scale * row_scale * shape_term


def prep_kernel(
    me_ref,
    owner_hbm,
    offset_hbm,
    points_hbm,
    amp_hbm,
    noise_hbm,
    cov_hbm,
    out_ref,
    owner_ref,
    offset_ref,
    points_ref,
    amp_ref,
    noise_ref,
    rows_ref,
    sem,
    load_sem,
):
    pairs = (
        (owner_hbm, owner_ref),
        (offset_hbm, offset_ref),
        (points_hbm, points_ref),
        (amp_hbm, amp_ref),
        (noise_hbm, noise_ref),
    )
    loads = [pltpu.make_async_copy(*pair, load_sem.at[i]) for i, pair in enumerate(pairs)]
    for load in loads:
        load.start()
    me = me_ref[0]
    blocks, width = owner_ref.shape
    slots = CAP * blocks
    for load in loads[:2]:
        load.wait()
    lane = lax.broadcasted_iota(jnp.int32, (blocks, width), 1).astype(jnp.float32)
    block = lax.broadcasted_iota(jnp.int32, (blocks, width), 0)
    mine = owner_ref[...] == me
    offset = offset_ref[...].astype(jnp.float32)
    first = jnp.min(jnp.where(mine, lane, 1e4), axis=1, keepdims=True)
    last = jnp.max(jnp.where(mine, lane, -1.0), axis=1, keepdims=True)
    chosen = [jnp.where(mine & (lane == at), offset, 0.0) for at in (first, last)]
    copies = []
    slot_row = lax.broadcasted_iota(jnp.int32, (slots, 1), 0)
    offsets = jnp.zeros((slots, 1), jnp.int32)
    for s in range(slots):
        value = jnp.sum(jnp.where(block == s // CAP, chosen[s % CAP], 0.0)).astype(jnp.int32)
        copy = pltpu.make_async_copy(cov_hbm.at[pl.ds(value, 1), :], rows_ref.at[pl.ds(s, 1), :], sem.at[s])
        copy.start()
        copies.append(copy)
        offsets = jnp.where(slot_row == s, value, offsets)
    for load in loads[2:]:
        load.wait()
    local_rows = points_ref.shape[1]
    hit = lax.broadcasted_iota(jnp.int32, (slots, local_rows), 1) == offsets
    sources = [points_ref[i : i + 1, :] for i in range(3)] + [amp_ref[...], noise_ref[...]]
    sub = lax.broadcasted_iota(jnp.int32, (SUB, BLOCK), 0)
    diagonal = sub == lax.broadcasted_iota(jnp.int32, (SUB, BLOCK), 1)
    scalars = jnp.zeros((SUB, BLOCK), jnp.float32)
    for i, source in enumerate(sources):
        column = jnp.sum(jnp.where(hit, source, 0.0), axis=1, keepdims=True)
        line = jnp.sum(jnp.where(diagonal, column, 0.0), axis=0, keepdims=True)
        scalars = jnp.where(sub == i, line, scalars)
    for copy in copies:
        copy.wait()
    half = rows_ref.shape[1] // 2
    left, right = rows_ref[:, :half], rows_ref[:, half:]
    for i in range(out_ref.shape[0]):
        out_ref[i, :slots, :] = left
        out_ref[i, slots : 2 * slots, :] = right
        out_ref[i, 2 * slots :, :] = scalars


def aux_kernel(
    me_ref,
    owner_hbm,
    offset_hbm,
    points_hbm,
    amp_hbm,
    noise_hbm,
    cov_hbm,
    high_ref,
    middle_ref,
    low_ref,
    feat_ref,
    base_ref,
    info_ref,
    match_ref,
    comb_ref,
    left_ref,
    most_ref,
    owner_ref,
    offset_ref,
    points_ref,
    amp_ref,
    noise_ref,
    cov_ref,
    load_sem,
):
    pairs = (
        (owner_hbm, owner_ref),
        (offset_hbm, offset_ref),
        (points_hbm, points_ref),
        (amp_hbm, amp_ref),
        (noise_hbm, noise_ref),
        (cov_hbm, cov_ref),
    )
    loads = [pltpu.make_async_copy(*pair, load_sem.at[i]) for i, pair in enumerate(pairs)]
    for load in loads:
        load.start()
    me = me_ref[0]
    blocks, width = owner_ref.shape
    for load in loads[:2]:
        load.wait()
    local_rows, cov_width = cov_ref.shape
    half = cov_width // 2
    owner = owner_ref[...]
    padded = jnp.concatenate([owner, jnp.zeros((SUB - blocks, width), jnp.int32)], axis=0)
    owner_t = padded.astype(jnp.float32).T.astype(jnp.int32)
    sub = lax.broadcasted_iota(jnp.int32, (width, width), 0)
    lane = lax.broadcasted_iota(jnp.int32, (width, width), 1)
    xy = (owner >> 1) & 15
    xy_t = (owner_t >> 1) & 15
    my_xy = lax.rem(lax.div(me, 2), 16)
    seats = []
    candidates = []
    infos = []
    for b in range(blocks):
        count = jnp.zeros((1, width), jnp.float32)
        for earlier in range(b + 1):
            same = xy_t[:, earlier : earlier + 1] == xy[b : b + 1, :]
            if earlier == b:
                same = same & (sub < lane)
            count = count + jnp.sum(jnp.where(same, 1.0, 0.0), axis=0, keepdims=True)
        twin = (owner_t[:, b : b + 1] == owner[b : b + 1, :]) & (sub < lane)
        rank = jnp.sum(jnp.where(twin, 1.0, 0.0), axis=0, keepdims=True).astype(jnp.int32)
        count = count.astype(jnp.int32)
        row = owner[b : b + 1, :]
        seats.append(jnp.where(xy[b : b + 1, :] == my_xy, count, -1))
        candidates.append((row >> 5) * 16 + (row & 1) * SUB + CAP * b + rank)
        infos.append(count)
    info_ref[:blocks, :] = xy.astype(jnp.float32)
    counts = jnp.concatenate(infos, axis=0).astype(jnp.float32)
    info_ref[blocks:, :] = counts
    most_ref[0] = jnp.max(counts).astype(jnp.int32) + 1
    match = jnp.where(owner == me, offset_ref[...], -1)
    match_ref[...] = jnp.concatenate([match[b : b + 1, :] for b in range(blocks)], axis=1)
    seat = jnp.concatenate(seats, axis=1)
    candidate = jnp.concatenate(candidates, axis=1)
    ids = lax.broadcasted_iota(jnp.int32, (BLOCK, blocks * width), 0)
    seat_hit = (ids == seat).astype(jnp.float32).astype(jnp.bfloat16)
    candidate_hit = (ids == candidate).astype(jnp.float32).astype(jnp.bfloat16)
    comb_ref[...] = product(seat_hit, candidate_hit, ((1,), (1,)))

    for load in loads[2:]:
        load.wait()
    feat_ref[:3, :] = points_ref[...]
    feat_ref[3:4, :] = amp_ref[...]
    feat_ref[4:5, :] = noise_ref[...]
    feat_ref[5:, :] = jnp.zeros((3, local_rows), jnp.float32)
    diagonal = sub == lane
    scale = (5.0**0.5) / LENGTH_SCALE
    order = (0, 0, 1, 1, 0, 2)

    def step(t, carry):
        at = pl.ds(pl.multiple_of(t * BLOCK, BLOCK), BLOCK)
        cov = cov_ref[at, :]
        high, middle, low = parts_of(cov)
        high_ref[at, :] = high
        middle_ref[at, :] = middle
        low_ref[at, :] = low
        squares = cov * cov
        line = jnp.sum(squares[:, :half] + squares[:, half:], axis=1, keepdims=True)
        total = jnp.sum(jnp.where(diagonal, line, 0.0), axis=0, keepdims=True)
        points = (points_ref[:, at] - 0.5) * scale
        point_parts = [part.astype(jnp.float32) for part in parts_of(points)]
        length = jnp.sum(points * points, axis=0, keepdims=True)
        lines = [point_parts[k][i : i + 1, :] for i in range(3) for k in order]
        lines += [part.astype(jnp.float32) for part in parts_of(length)] + [jnp.ones((3, BLOCK), jnp.float32)]
        lines.append(jnp.zeros((BLOCK - 6 * len(order) + 12, BLOCK), jnp.float32))
        left_ref[at, :] = jnp.concatenate(lines, axis=0).T.astype(jnp.bfloat16)
        amplitude = amp_ref[:, at]
        base_ref[pl.ds(t, 1), :] = amplitude * amplitude + noise_ref[:, at] + total
        return carry

    lax.fori_loop(0, local_rows // BLOCK, step, 0)


def seat_kernel(me_ref, comb_ref, got_ref, out_ref):
    core = lax.rem(me_ref[0], 2)
    senders = got_ref.shape[0]
    slots = (got_ref.shape[1] - SUB) // 2
    seats = out_ref.shape[1] - SUB
    comb = comb_ref[...].astype(jnp.bfloat16)
    left = jnp.concatenate([got_ref[i, :slots, :] for i in range(senders)], axis=0)
    right = jnp.concatenate([got_ref[i, slots : 2 * slots, :] for i in range(senders)], axis=0)
    rows = jnp.where(core == 0, left, right)
    packed = pick_rows(comb[: -(-seats // 16) * 16], rows, ((1,), (0,)))[:seats]
    lane = lax.broadcasted_iota(jnp.int32, (SUB, BLOCK), 1)
    scalars = jnp.zeros((SUB, BLOCK), jnp.float32)
    for i in range(senders):
        piece = got_ref[i, 2 * slots :, :]
        piece = pltpu.roll(piece, i * slots, 1) if i else piece
        scalars = jnp.where(lane // slots == i, piece, scalars)
    high, middle, low = parts_of(scalars)
    dims = ((1,), (1,))
    seated = product(high, comb, dims) + product(middle, comb, dims) + product(low, comb, dims)
    for i in range(out_ref.shape[0]):
        out_ref[i, :seats, :] = packed
        out_ref[i, seats:, :] = seated


def field_kernel(mine_ref, info_ref, match_ref, feat_ref, left_ref, scal_ref, field_ref, col_ref):
    pivots = match_ref.shape[1]
    local_rows = feat_ref.shape[1]
    planes, plane_rows, _ = mine_ref.shape
    seats = plane_rows - SUB
    blocks = pivots // BLOCK
    nt = ((1,), (1,))
    packed = BLOCK // plane_rows if BLOCK % plane_rows == 0 else 1
    stride = BLOCK // packed
    lane = lax.broadcasted_iota(jnp.int32, (SUB, BLOCK), 1)
    lines = []
    for q in range(planes // packed):
        line = mine_ref[q * packed, seats:, :]
        for t in range(1, packed):
            piece = pltpu.roll(mine_ref[q * packed + t, seats:, :], t * stride, 1)
            line = jnp.where(lane // stride == t, piece, line)
        lines.append(line)
    line_parts = parts_of(jnp.concatenate(lines, axis=1))
    info_t = info_ref[...].T
    for b in range(blocks):
        here = pl.ds(b * BLOCK, BLOCK)
        xy, seat = info_t[:, b : b + 1], info_t[:, blocks + b : blocks + b + 1]
        place = (xy * stride + seat).astype(jnp.int32)
        ids = lax.broadcasted_iota(jnp.int32, (BLOCK, planes * stride), 1)
        line_pick = (ids == place).astype(jnp.float32).astype(jnp.bfloat16)
        scal_ref[:, here] = (
            product(line_parts[0], line_pick, nt)
            + product(line_parts[1], line_pick, nt)
            + product(line_parts[2], line_pick, nt)
        )
    for t in range(local_rows // BLOCK):
        at = pl.ds(t * BLOCK, BLOCK)
        col_ref[at, :] = feat_ref[:, at].T
    piv = scal_ref[...]
    piv_scale = piv[3:4, :]
    match = match_ref[...]

    scale = (5.0**0.5) / LENGTH_SCALE
    points = (piv[:3, :] - 0.5) * scale
    length = jnp.sum(points * points, axis=0, keepdims=True)
    point_parts = [part.astype(jnp.float32) * -2.0 for part in parts_of(points)]
    lines = [point_parts[k][i : i + 1, :] for i in range(3) for k in (0, 1, 0, 1, 2, 0)]
    lines += [jnp.ones((3, pivots), jnp.float32)] + [part.astype(jnp.float32) for part in parts_of(length)]
    lines.append(jnp.zeros((BLOCK - 24, pivots), jnp.float32))
    right = jnp.concatenate(lines, axis=0).astype(jnp.bfloat16)

    def step(t, carry):
        at = pl.ds(pl.multiple_of(t * WIDE, WIDE), WIDE)
        cols = col_ref[at, :]
        dist_sq = jnp.maximum(product(left_ref[at, :], right, ((1,), (0,))), 1e-30)
        scaled = dist_sq * lax.rsqrt(dist_sq)
        value = (1.0 + scaled + dist_sq * (1.0 / 3.0)) * jnp.exp2(scaled * -LOG2E)
        value = cols[:, 3:4] * piv_scale * value
        row_ids = lax.broadcasted_iota(jnp.int32, (WIDE, 1), 0) + t * WIDE
        field_ref[at, :] = value + jnp.where(row_ids == match, cols[:, 4:5], 0.0)
        return carry

    lax.fori_loop(0, local_rows // WIDE, step, 0)


def main_kernel(
    me_ref,
    mine_ref,
    other_ref,
    info_ref,
    scal_ref,
    field_ref,
    base_ref,
    high_hbm,
    middle_hbm,
    low_hbm,
    out_hbm,
    resid_ref,
    sums_ref,
    cov_high,
    cov_middle,
    cov_low,
    table_high,
    table_middle,
    table_low,
    kernel_high,
    kernel_middle,
    kernel_low,
    z_ref,
    r_ref,
    tile_ref,
    load_sem,
    store_sem,
):
    core = lax.rem(me_ref[0], 2)
    pivots = z_ref.shape[0]
    local_rows, cov_width = cov_high.shape
    planes, plane_rows, half = mine_ref.shape
    blocks = pivots // BLOCK
    loads = [
        pltpu.make_async_copy(source, target, load_sem.at[i])
        for i, (source, target) in enumerate(
            ((high_hbm, cov_high), (middle_hbm, cov_middle), (low_hbm, cov_low))
        )
    ]
    for load in loads:
        load.start()
    nt = ((1,), (1,))

    scale = (5.0**0.5) / LENGTH_SCALE
    candidates = planes * plane_rows
    mine = mine_ref[...].reshape(candidates, half)
    other = other_ref[...].reshape(candidates, half)
    both = jnp.concatenate([jnp.where(core == 0, mine, other), jnp.where(core == 0, other, mine)], axis=1)
    both_parts = parts_of(both)
    info_t = info_ref[...].T
    for b in range(blocks):
        here = pl.ds(b * BLOCK, BLOCK)
        xy, seat = info_t[:, b : b + 1], info_t[:, blocks + b : blocks + b + 1]
        place = (xy * plane_rows + seat).astype(jnp.int32)
        ids = lax.broadcasted_iota(jnp.int32, (BLOCK, candidates), 1)
        pick = (ids == place).astype(jnp.float32).astype(jnp.bfloat16)
        for part, table in zip(both_parts, (table_high, table_middle, table_low)):
            table[here, :] = product(pick, part, ((1,), (0,))).astype(jnp.bfloat16)

    piv = scal_ref[...]
    piv_rows = [piv[i : i + 1, :] * scale for i in range(3)]
    piv_scale, piv_noise = piv[3:4, :], piv[4:5, :]

    for b in range(blocks):
        here = pl.ds(b * BLOCK, BLOCK)
        right = slice(b * BLOCK, pivots)
        cols = scal_ref[:, here].T
        piece = matern(
            [cols[:, i : i + 1] * scale for i in range(3)],
            [row[:, right] for row in piv_rows],
            cols[:, 3:4],
            piv_scale[:, right],
        )
        same = lax.broadcasted_iota(jnp.int32, (BLOCK, 1), 0) == lax.broadcasted_iota(
            jnp.int32, (1, pivots - b * BLOCK), 1
        )
        piece = piece + jnp.where(same, piv_noise[:, right], 0.0)
        left_parts = [table[here, :] for table in (table_high, table_middle, table_low)]
        right_parts = [table[right, :] for table in (table_high, table_middle, table_low)]
        z_ref[here, right] = piece + dot_parts(left_parts, right_parts, nt)
        if b:
            z_ref[here, : b * BLOCK] = jnp.zeros((BLOCK, b * BLOCK), jnp.float32)
    for load in loads:
        load.wait()
    def kernel_tile(t):
        at = pl.ds(pl.multiple_of(t * WIDE, WIDE), WIDE)
        cov = [part[at, :] for part in (cov_high, cov_middle, cov_low)]
        kernel = field_ref[at, :] + dot_parts(cov, (table_high[...], table_middle[...], table_low[...]), nt)
        for part, target in zip(parts_of(kernel), (kernel_high, kernel_middle, kernel_low)):
            target[at, :] = part

    per_step = local_rows // WIDE // blocks

    def step(b, carry):
        at = pl.ds(pl.multiple_of(b * BLOCK, BLOCK), BLOCK)
        pieces = [
            z_ref[pl.ds(pl.multiple_of(b * BLOCK + SUB * i, SUB), SUB), at]
            for i in range(BLOCK // SUB)
        ]
        inverse = jnp.concatenate(block_inverse(pieces), axis=0)
        for i in range(per_step):
            kernel_tile(b * per_step + i)
        r_ref[...] = dot_parts(parts_of(inverse), parts_of(z_ref[at, :]), ((1,), (0,)))
        r_ref[:, at] = inverse
        z_ref[:, at] = jnp.zeros((pivots, BLOCK), jnp.float32)
        row = r_ref[...]
        for s in range(blocks - 1):

            @pl.when(b == s)
            def _():
                later = slice((s + 1) * BLOCK, pivots)
                coef = parts_of(row[:, later].T)
                z_ref[later, :] -= dot_parts(coef, parts_of(row), ((1,), (0,)))

        z_ref[at, :] = row
        return carry

    lax.fori_loop(0, blocks, step, 0)

    diagonal = lax.broadcasted_iota(jnp.int32, (BLOCK, BLOCK), 0) == lax.broadcasted_iota(
        jnp.int32, (BLOCK, BLOCK), 1
    )
    left = pivots // 2
    half_tiles = WIDE // BLOCK
    tiles = local_rows // WIDE
    inverse_parts = parts_of(z_ref[...])
    for part, target in zip(inverse_parts, (table_high, table_middle, table_low)):
        target[:, :] = part[:, :left]
    late = [part[left:, left:] for part in inverse_parts]

    def tile_step(t, taken):
        at = pl.ds(pl.multiple_of(t * WIDE, WIDE), WIDE)
        slot = lax.rem(t, 2)

        @pl.when(t >= 2)
        def _():
            pltpu.make_async_copy(tile_ref.at[slot], out_hbm.at[at, :], store_sem.at[slot]).wait()

        kernels = [part[at, :] for part in (kernel_high, kernel_middle, kernel_low)]
        early = [part[:, :left] for part in kernels]
        first = dot_parts(early, [table[:left, :] for table in (table_high, table_middle, table_low)], nt)
        second = dot_parts(early, [table[left:, :] for table in (table_high, table_middle, table_low)], nt)
        second = second + dot_parts([part[:, left:] for part in kernels], late, nt)
        tile_ref[slot, :, :left] = first
        tile_ref[slot, :, left:] = second
        pltpu.make_async_copy(tile_ref.at[slot], out_hbm.at[at, :], store_sem.at[slot]).start()
        total = jnp.zeros((WIDE, BLOCK), jnp.float32)
        new_taken = []
        for b in range(blocks):
            source = first if b * BLOCK < left else second
            piece = source[:, (b * BLOCK) % left : (b * BLOCK) % left + BLOCK]
            square = piece * piece
            total = total + square
            new_taken.append(taken[b] + jnp.sum(square.reshape(WIDE // SUB, SUB, BLOCK), axis=0))
        line = jnp.sum(total, axis=1, keepdims=True)
        for h in range(half_tiles):
            spread = jnp.where(diagonal, line[h * BLOCK : (h + 1) * BLOCK, :], 0.0)
            where = pl.ds(t * half_tiles + h, 1)
            resid_ref[where, :] = base_ref[where, :] - jnp.sum(spread, axis=0, keepdims=True)
        return tuple(new_taken)

    zero = jnp.zeros((SUB, BLOCK), jnp.float32)
    taken = lax.fori_loop(0, tiles, tile_step, (zero,) * blocks)
    for tile in (tiles - 2, tiles - 1):
        at = pl.ds(tile * WIDE, WIDE)
        pltpu.make_async_copy(tile_ref.at[tile % 2], out_hbm.at[at, :], store_sem.at[tile % 2]).wait()

    total = jnp.sum(base_ref[...])
    lanes = lax.broadcasted_iota(jnp.int32, sums_ref.shape, 1)
    sums = jnp.zeros(sums_ref.shape, jnp.float32)
    for b in range(blocks):
        total = total - jnp.sum(taken[b])
        sums = jnp.where(lanes == b, total, sums)
    sums_ref[...] = sums


def last_kernel(sums_ref, resid_ref, weights_ref, mean_ref, *, rows):
    devices, _, width = sums_ref.shape
    total = jnp.sum(sums_ref[...].reshape(devices, width), axis=0, keepdims=True)
    mean = total * (1.0 / rows)
    count = mean_ref.shape[1]
    mean_ref[...] = mean[:, :count]
    weights_ref[...] = resid_ref[...] / mean[:, count - 1 : count]


def shape(dims, dtype=jnp.float32):
    return jax.ShapeDtypeStruct(dims, dtype)


VMEM = pl.BlockSpec(memory_space=pltpu.VMEM)
SMEM = pl.BlockSpec(memory_space=pltpu.SMEM)
ANY = pl.BlockSpec(memory_space=pl.ANY)
PARAMS = pltpu.CompilerParams(vmem_limit_bytes=40 << 20)
AUX_PARAMS = pltpu.CompilerParams(vmem_limit_bytes=55 << 20)


def prep(me, owner, offset, points, amp, noise, cov, copies):
    slots = CAP * owner.shape[0]
    return pl.pallas_call(
        prep_kernel,
        out_shape=shape((copies, 2 * slots + SUB, BLOCK)),
        in_specs=[SMEM] + [ANY] * 6,
        out_specs=VMEM,
        scratch_shapes=[pltpu.VMEM(value.shape, value.dtype) for value in (owner, offset, points, amp, noise)]
        + [
            pltpu.VMEM((slots, cov.shape[1]), jnp.float32),
            pltpu.SemaphoreType.DMA((slots,)),
            pltpu.SemaphoreType.DMA((5,)),
        ],
        compiler_params=pltpu.CompilerParams(vmem_limit_bytes=60 << 20),
        name="prep",
    )(me, owner, offset, points, amp, noise, cov)


def aux(me, owner, offset, points, amp, noise, cov):
    rows, width = cov.shape
    return pl.pallas_call(
        aux_kernel,
        out_shape=(
            shape((rows, width), jnp.bfloat16),
            shape((rows, width), jnp.bfloat16),
            shape((rows, width), jnp.bfloat16),
            shape((SUB, rows)),
            shape((rows // BLOCK, BLOCK)),
            shape((SUB, BLOCK)),
            shape((1, owner.size), jnp.int32),
            shape((BLOCK, BLOCK)),
            shape((rows, BLOCK), jnp.bfloat16),
            shape((1,), jnp.int32),
        ),
        in_specs=[SMEM] + [ANY] * 6,
        out_specs=(VMEM,) * 9 + (SMEM,),
        scratch_shapes=[pltpu.VMEM(value.shape, value.dtype) for value in (owner, offset, points, amp, noise, cov)]
        + [pltpu.SemaphoreType.DMA((6,))],
        compiler_params=AUX_PARAMS,
        cost_estimate=pl.CostEstimate(flops=10**8, bytes_accessed=6 << 20, transcendentals=0),
        name="aux",
    )(me, owner, offset, points, amp, noise, cov)


def seat(me, comb, got, copies, seats):
    return pl.pallas_call(
        seat_kernel,
        out_shape=shape((copies, seats + SUB, BLOCK)),
        in_specs=[SMEM, VMEM, VMEM],
        out_specs=VMEM,
        compiler_params=PARAMS,
        name="seat",
    )(me, comb, got)


def field(mine, info, match, feat, left):
    pivots, rows = match.shape[1], feat.shape[1]
    return pl.pallas_call(
        field_kernel,
        out_shape=(shape((SUB, pivots)), shape((rows, pivots))),
        in_specs=[VMEM] * 5,
        out_specs=(VMEM, VMEM),
        scratch_shapes=[pltpu.VMEM((rows, SUB), jnp.float32)],
        compiler_params=PARAMS,
        cost_estimate=pl.CostEstimate(flops=10**8, bytes_accessed=6 << 20, transcendentals=0),
        name="field",
    )(mine, info, match, feat, left)


def main(me, mine, other, info, scal, local_field, base, high, middle, low, devices):
    rows, width = high.shape
    pivots = scal.shape[1]
    bf = jnp.bfloat16
    return pl.pallas_call(
        main_kernel,
        out_shape=(shape((rows, pivots)), shape((rows // BLOCK, BLOCK)), shape((devices, BLOCK))),
        in_specs=[SMEM] + [VMEM] * 6 + [ANY] * 3,
        out_specs=(ANY, VMEM, VMEM),
        scratch_shapes=[pltpu.VMEM((rows, width), bf)] * 3
        + [pltpu.VMEM((pivots, width), bf)] * 3
        + [pltpu.VMEM((rows, pivots), bf)] * 3
        + [
            pltpu.VMEM((pivots, pivots), jnp.float32),
            pltpu.VMEM((BLOCK, pivots), jnp.float32),
            pltpu.VMEM((2, WIDE, pivots), jnp.float32),
            pltpu.SemaphoreType.DMA((3,)),
            pltpu.SemaphoreType.DMA((2,)),
        ],
        compiler_params=PARAMS,
        name="factor_rows",
    )(me, mine, other, info, scal, local_field, base, high, middle, low)


def last(sums, resid, blocks, rows):
    return pl.pallas_call(
        functools.partial(last_kernel, rows=rows),
        out_shape=(shape(resid.shape), shape((1, blocks))),
        in_specs=[VMEM, VMEM],
        out_specs=(VMEM, VMEM),
        compiler_params=PARAMS,
        name="last",
    )(sums, resid)


def local(locations, amplitude, noise, covariates, pivot_owner, pivot_offset):
    me = lax.axis_index(AXES).astype(jnp.int32)[None]
    blocks = pivot_owner.shape[0]
    sizes = [lax.axis_size(name) for name in AXES]
    devices = sizes[0] * sizes[1] * sizes[2] * sizes[3]
    swap = [(0, 1), (1, 0)]
    amp, nugget = amplitude[None], noise[None]
    args = (me, pivot_owner, pivot_offset, locations, amp, nugget, covariates)

    column = lax.all_to_all(prep(*args, sizes[0] * sizes[3]), ("z", "c"), 0, 0, tiled=True)
    high, middle, low, feat, base, info, match, comb, left, most = aux(*args)

    def rest(seats):
        def run(column, comb, info, match, feat, left, base, high, middle, low):
            message = seat(me, comb, column, sizes[1] * sizes[2], seats)
            mine = lax.all_to_all(message, ("x", "y"), 0, 0, tiled=True)
            other = lax.ppermute(mine, "c", swap)
            scal, local_field = field(mine, info, match, feat, left)
            return main(me, mine, other, info, scal, local_field, base, high, middle, low, devices)

        return run

    operands = (column, comb, info, match, feat, left, base, high, middle, low)
    if FEW:
        factor, resid, sums = lax.cond(most[0] <= FEW, rest(FEW), rest(BLOCK), *operands)
    else:
        factor, resid, sums = rest(BLOCK)(*operands)
    all_sums = lax.all_to_all(sums[:, None, :], AXES, 0, 0, tiled=True)
    weights, mean_residual = last(all_sums, resid, blocks, locations.shape[1] * devices)
    return (factor, weights.reshape(-1), mean_residual.reshape(-1))


def solution(mesh):
    named = Mesh(mesh.devices.reshape(8, 4, 4, 2), AXES)
    return jax.shard_map(
        local,
        mesh=named,
        in_specs=(P(None, AXES), P(AXES), P(AXES), P(AXES, None), P(), P()),
        out_specs=(P(AXES, None), P(AXES), P()),
        check_vma=False,
    )
```

```python
import functools

import jax
import jax.numpy as jnp
from jax import lax
from jax.experimental import pallas as pl
from jax.experimental.pallas import tpu as pltpu
from jax.sharding import Mesh
from jax.sharding import PartitionSpec as P

LENGTH_SCALE = 0.3
CAP = 2
AXES = ("z", "x", "y", "c")
HIGHEST = lax.Precision.HIGHEST
BLOCK = 128
PANEL = 16
SUB = 8
TILE = 256
FEW = 56
WIDE = 512
LOG2E = 1.4426950408889634


def dot(left, right, dims):
    return lax.dot_general(
        left, right, (dims, ((), ())), precision=HIGHEST, preferred_element_type=jnp.float32
    )


def panel_rows(low, high, near, top, bottom, near_rows):
    sub = lax.broadcasted_iota(jnp.int32, (SUB, BLOCK), 0)
    low, high, near, near_rows = list(low), list(high), [list(one) for one in near], list(near_rows)
    root_low = jnp.zeros((SUB, BLOCK), jnp.float32)
    root_high = root_low

    def entry(j, i):
        piece = low[j][i : i + 1, :] if i < SUB else high[j][i - SUB : i - SUB + 1, :]
        return jnp.broadcast_to(piece, (SUB, BLOCK))

    pivot = entry(0, 0)
    for k in range(PANEL):
        inverse = pl.reciprocal(pivot, approx=True)
        root = lax.rsqrt(pivot)
        if k + 1 < PANEL:
            side = entry(k, k + 1)
            pivot = entry(k + 1, k + 1) - (side * side) * inverse
        take_near = [one[k] * inverse for one in near]
        if k < SUB:
            take_low = jnp.where(sub > k, low[k], 0.0) * inverse
            take_high = high[k] * inverse
            root_low = jnp.where(sub == k, root, root_low)
            line = top[k : k + 1, :]
        else:
            take_high = jnp.where(sub > k - SUB, high[k], 0.0) * inverse
            root_high = jnp.where(sub == k - SUB, root, root_high)
            line = bottom[k - SUB : k - SUB + 1, :]
        for j in range(k + 1, PANEL):
            across = entry(k, j)
            if j < SUB:
                low[j] = low[j] - take_low * across
            high[j] = high[j] - take_high * across
            for one, take in zip(near, take_near):
                one[j] = one[j] - take * across
        if k < SUB:
            top = top - take_low * line
        bottom = bottom - take_high * line
        near_rows = [row - take * line for row, take in zip(near_rows, take_near)]
    return top * root_low, bottom * root_high, near_rows


def block_inverse(rows):
    lane = lax.broadcasted_iota(jnp.int32, (SUB, BLOCK), 1)
    sub = lax.broadcasted_iota(jnp.int32, (SUB, BLOCK), 0)
    rows = list(rows)
    out = [None] * len(rows)
    for panel in range(BLOCK // PANEL):
        first = PANEL * panel
        at = 2 * panel

        def splat(piece, j):
            return jnp.broadcast_to(piece[:, first + j : first + j + 1], (SUB, BLOCK))

        rest = range(at + 2, len(rows))
        near, far = rest[:2], rest[2:]
        low = [splat(rows[at], j) for j in range(SUB)]
        high = [splat(rows[at + 1], j) for j in range(PANEL)]
        next_columns = [[splat(rows[r], j) for j in range(PANEL)] for r in near]
        in_panel = (lane >= first) & (lane < first + PANEL)
        top = jnp.where(in_panel, jnp.where(lane - first == sub, 1.0, 0.0), rows[at])
        bottom = jnp.where(in_panel, jnp.where(lane - first - SUB == sub, 1.0, 0.0), rows[at + 1])
        next_rows = [jnp.where(in_panel, 0.0, rows[r]) for r in near]
        new_low, new_high, next_rows = panel_rows(low, high, next_columns, top, bottom, next_rows)
        out[at] = jnp.where(lane <= first + sub, new_low, 0.0)
        out[at + 1] = jnp.where(lane <= first + SUB + sub, new_high, 0.0)
        for r, row in zip(near, next_rows):
            rows[r] = row
        if len(far):
            new_rows = jnp.concatenate([new_low, new_high], axis=0)
            filler = jnp.zeros((BLOCK - PANEL, BLOCK), jnp.float32)
            flipped = jnp.concatenate([new_rows, filler], axis=0).T
            far_parts = parts_of(flipped[SUB * far[0] : SUB * (far[-1] + 1), :])
            spread = [
                jnp.concatenate([part, filler.astype(jnp.bfloat16)], axis=0) for part in parts_of(new_rows)
            ]
            change = dot_parts(far_parts, spread, ((1,), (0,)))
            for i, r in enumerate(far):
                rows[r] = jnp.where(in_panel, 0.0, rows[r]) - change[SUB * i : SUB * (i + 1)]
    return out


def parts_of(value):
    high = value.astype(jnp.bfloat16)
    rest = value - high.astype(jnp.float32)
    middle = rest.astype(jnp.bfloat16)
    low = (rest - middle.astype(jnp.float32)).astype(jnp.bfloat16)
    return high, middle, low


def product(left, right, dims):
    return lax.dot_general(left, right, (dims, ((), ())), preferred_element_type=jnp.float32)


def dot_parts(left, right, dims):
    high, middle, low = left
    other_high, other_middle, other_low = right
    one = jnp.concatenate([low, high, middle, middle, high, high], axis=dims[0][0])
    two = jnp.concatenate(
        [other_high, other_low, other_middle, other_high, other_middle, other_high], axis=dims[1][0]
    )
    return product(one, two, dims)


def pick_rows(pick, value, dims):
    high, middle, low = parts_of(value)
    return product(pick, high, dims) + product(pick, middle, dims) + product(pick, low, dims)


def matern(cols, rows, col_scale, row_scale):
    dist_sq = None
    for axis_id in range(3):
        offset = cols[axis_id] - rows[axis_id]
        dist_sq = offset * offset if dist_sq is None else dist_sq + offset * offset
    scaled = dist_sq * lax.rsqrt(jnp.maximum(dist_sq, 1e-30))
    shape_term = (1.0 + scaled + dist_sq * (1.0 / 3.0)) * jnp.exp(-scaled)
    return col_scale * row_scale * shape_term


def prep_kernel(
    me_ref,
    owner_hbm,
    offset_hbm,
    points_hbm,
    amp_hbm,
    noise_hbm,
    cov_hbm,
    out_ref,
    owner_ref,
    offset_ref,
    points_ref,
    amp_ref,
    noise_ref,
    rows_ref,
    sem,
    load_sem,
):
    pairs = (
        (owner_hbm, owner_ref),
        (offset_hbm, offset_ref),
        (points_hbm, points_ref),
        (amp_hbm, amp_ref),
        (noise_hbm, noise_ref),
    )
    loads = [pltpu.make_async_copy(*pair, load_sem.at[i]) for i, pair in enumerate(pairs)]
    for load in loads:
        load.start()
    me = me_ref[0]
    blocks, width = owner_ref.shape
    slots = CAP * blocks
    for load in loads[:2]:
        load.wait()
    lane = lax.broadcasted_iota(jnp.int32, (blocks, width), 1).astype(jnp.float32)
    block = lax.broadcasted_iota(jnp.int32, (blocks, width), 0)
    mine = owner_ref[...] == me
    offset = offset_ref[...].astype(jnp.float32)
    first = jnp.min(jnp.where(mine, lane, 1e4), axis=1, keepdims=True)
    last = jnp.max(jnp.where(mine, lane, -1.0), axis=1, keepdims=True)
    chosen = [jnp.where(mine & (lane == at), offset, 0.0) for at in (first, last)]
    copies = []
    slot_row = lax.broadcasted_iota(jnp.int32, (slots, 1), 0)
    offsets = jnp.zeros((slots, 1), jnp.int32)
    for s in range(slots):
        value = jnp.sum(jnp.where(block == s // CAP, chosen[s % CAP], 0.0)).astype(jnp.int32)
        copy = pltpu.make_async_copy(cov_hbm.at[pl.ds(value, 1), :], rows_ref.at[pl.ds(s, 1), :], sem.at[s])
        copy.start()
        copies.append(copy)
        offsets = jnp.where(slot_row == s, value, offsets)
    for load in loads[2:]:
        load.wait()
    local_rows = points_ref.shape[1]
    hit = lax.broadcasted_iota(jnp.int32, (slots, local_rows), 1) == offsets
    sources = [points_ref[i : i + 1, :] for i in range(3)] + [amp_ref[...], noise_ref[...]]
    sub = lax.broadcasted_iota(jnp.int32, (SUB, BLOCK), 0)
    diagonal = sub == lax.broadcasted_iota(jnp.int32, (SUB, BLOCK), 1)
    scalars = jnp.zeros((SUB, BLOCK), jnp.float32)
    for i, source in enumerate(sources):
        column = jnp.sum(jnp.where(hit, source, 0.0), axis=1, keepdims=True)
        line = jnp.sum(jnp.where(diagonal, column, 0.0), axis=0, keepdims=True)
        scalars = jnp.where(sub == i, line, scalars)
    for copy in copies:
        copy.wait()
    half = rows_ref.shape[1] // 2
    left, right = rows_ref[:, :half], rows_ref[:, half:]
    for i in range(out_ref.shape[0]):
        out_ref[i, :slots, :] = left
        out_ref[i, slots : 2 * slots, :] = right
        out_ref[i, 2 * slots :, :] = scalars


def aux_kernel(
    me_ref,
    owner_hbm,
    offset_hbm,
    points_hbm,
    amp_hbm,
    noise_hbm,
    cov_hbm,
    high_ref,
    middle_ref,
    low_ref,
    feat_ref,
    base_ref,
    info_ref,
    match_ref,
    comb_ref,
    left_ref,
    most_ref,
    owner_ref,
    offset_ref,
    points_ref,
    amp_ref,
    noise_ref,
    cov_ref,
    load_sem,
):
    pairs = (
        (owner_hbm, owner_ref),
        (offset_hbm, offset_ref),
        (points_hbm, points_ref),
        (amp_hbm, amp_ref),
        (noise_hbm, noise_ref),
        (cov_hbm, cov_ref),
    )
    loads = [pltpu.make_async_copy(*pair, load_sem.at[i]) for i, pair in enumerate(pairs)]
    for load in loads:
        load.start()
    me = me_ref[0]
    blocks, width = owner_ref.shape
    for load in loads[:2]:
        load.wait()
    local_rows, cov_width = cov_ref.shape
    half = cov_width // 2
    owner = owner_ref[...]
    padded = jnp.concatenate([owner, jnp.zeros((SUB - blocks, width), jnp.int32)], axis=0)
    owner_t = padded.astype(jnp.float32).T.astype(jnp.int32)
    sub = lax.broadcasted_iota(jnp.int32, (width, width), 0)
    lane = lax.broadcasted_iota(jnp.int32, (width, width), 1)
    xy = (owner >> 1) & 15
    xy_t = (owner_t >> 1) & 15
    my_xy = lax.rem(lax.div(me, 2), 16)
    seats = []
    candidates = []
    infos = []
    for b in range(blocks):
        count = jnp.zeros((1, width), jnp.float32)
        for earlier in range(b + 1):
            same = xy_t[:, earlier : earlier + 1] == xy[b : b + 1, :]
            if earlier == b:
                same = same & (sub < lane)
            count = count + jnp.sum(jnp.where(same, 1.0, 0.0), axis=0, keepdims=True)
        twin = (owner_t[:, b : b + 1] == owner[b : b + 1, :]) & (sub < lane)
        rank = jnp.sum(jnp.where(twin, 1.0, 0.0), axis=0, keepdims=True).astype(jnp.int32)
        count = count.astype(jnp.int32)
        row = owner[b : b + 1, :]
        seats.append(jnp.where(xy[b : b + 1, :] == my_xy, count, -1))
        candidates.append((row >> 5) * 16 + (row & 1) * SUB + CAP * b + rank)
        infos.append(count)
    info_ref[:blocks, :] = xy.astype(jnp.float32)
    counts = jnp.concatenate(infos, axis=0).astype(jnp.float32)
    info_ref[blocks:, :] = counts
    most_ref[0] = jnp.max(counts).astype(jnp.int32) + 1
    match = jnp.where(owner == me, offset_ref[...], -1)
    match_ref[...] = jnp.concatenate([match[b : b + 1, :] for b in range(blocks)], axis=1)
    seat = jnp.concatenate(seats, axis=1)
    candidate = jnp.concatenate(candidates, axis=1)
    ids = lax.broadcasted_iota(jnp.int32, (BLOCK, blocks * width), 0)
    seat_hit = (ids == seat).astype(jnp.float32).astype(jnp.bfloat16)
    candidate_hit = (ids == candidate).astype(jnp.float32).astype(jnp.bfloat16)
    comb_ref[...] = product(seat_hit, candidate_hit, ((1,), (1,)))

    for load in loads[2:]:
        load.wait()
    feat_ref[:3, :] = points_ref[...]
    feat_ref[3:4, :] = amp_ref[...]
    feat_ref[4:5, :] = noise_ref[...]
    feat_ref[5:, :] = jnp.zeros((3, local_rows), jnp.float32)
    diagonal = sub == lane
    scale = (5.0**0.5) / LENGTH_SCALE
    order = (0, 0, 1, 1, 0, 2)

    def step(t, carry):
        at = pl.ds(pl.multiple_of(t * BLOCK, BLOCK), BLOCK)
        cov = cov_ref[at, :]
        high, middle, low = parts_of(cov)
        high_ref[at, :] = high
        middle_ref[at, :] = middle
        low_ref[at, :] = low
        squares = cov * cov
        line = jnp.sum(squares[:, :half] + squares[:, half:], axis=1, keepdims=True)
        total = jnp.sum(jnp.where(diagonal, line, 0.0), axis=0, keepdims=True)
        points = (points_ref[:, at] - 0.5) * scale
        point_parts = [part.astype(jnp.float32) for part in parts_of(points)]
        length = jnp.sum(points * points, axis=0, keepdims=True)
        lines = [point_parts[k][i : i + 1, :] for i in range(3) for k in order]
        lines += [part.astype(jnp.float32) for part in parts_of(length)] + [jnp.ones((3, BLOCK), jnp.float32)]
        lines.append(jnp.zeros((BLOCK - 6 * len(order) + 12, BLOCK), jnp.float32))
        left_ref[at, :] = jnp.concatenate(lines, axis=0).T.astype(jnp.bfloat16)
        amplitude = amp_ref[:, at]
        base_ref[pl.ds(t, 1), :] = amplitude * amplitude + noise_ref[:, at] + total
        return carry

    lax.fori_loop(0, local_rows // BLOCK, step, 0)


def seat_kernel(me_ref, comb_ref, got_ref, out_ref):
    core = lax.rem(me_ref[0], 2)
    senders = got_ref.shape[0]
    slots = (got_ref.shape[1] - SUB) // 2
    seats = out_ref.shape[1] - SUB
    comb = comb_ref[...].astype(jnp.bfloat16)
    left = jnp.concatenate([got_ref[i, :slots, :] for i in range(senders)], axis=0)
    right = jnp.concatenate([got_ref[i, slots : 2 * slots, :] for i in range(senders)], axis=0)
    rows = jnp.where(core == 0, left, right)
    packed = pick_rows(comb[: -(-seats // 16) * 16], rows, ((1,), (0,)))[:seats]
    lane = lax.broadcasted_iota(jnp.int32, (SUB, BLOCK), 1)
    scalars = jnp.zeros((SUB, BLOCK), jnp.float32)
    for i in range(senders):
        piece = got_ref[i, 2 * slots :, :]
        piece = pltpu.roll(piece, i * slots, 1) if i else piece
        scalars = jnp.where(lane // slots == i, piece, scalars)
    high, middle, low = parts_of(scalars)
    dims = ((1,), (1,))
    seated = product(high, comb, dims) + product(middle, comb, dims) + product(low, comb, dims)
    for i in range(out_ref.shape[0]):
        out_ref[i, :seats, :] = packed
        out_ref[i, seats:, :] = seated


def field_kernel(mine_ref, info_ref, match_ref, feat_ref, left_ref, scal_ref, field_ref, col_ref):
    pivots = match_ref.shape[1]
    local_rows = feat_ref.shape[1]
    planes, plane_rows, _ = mine_ref.shape
    seats = plane_rows - SUB
    blocks = pivots // BLOCK
    nt = ((1,), (1,))
    packed = BLOCK // plane_rows if BLOCK % plane_rows == 0 else 1
    stride = BLOCK // packed
    lane = lax.broadcasted_iota(jnp.int32, (SUB, BLOCK), 1)
    lines = []
    for q in range(planes // packed):
        line = mine_ref[q * packed, seats:, :]
        for t in range(1, packed):
            piece = pltpu.roll(mine_ref[q * packed + t, seats:, :], t * stride, 1)
            line = jnp.where(lane // stride == t, piece, line)
        lines.append(line)
    line_parts = [part.astype(jnp.float32) for part in parts_of(jnp.concatenate(lines, axis=1))]
    line_parts = jnp.concatenate(line_parts + [jnp.zeros_like(line_parts[0])], axis=0).astype(jnp.bfloat16)
    info_t = info_ref[...].T
    for b in range(blocks):
        here = pl.ds(b * BLOCK, BLOCK)
        xy, seat = info_t[:, b : b + 1], info_t[:, blocks + b : blocks + b + 1]
        place = (xy * stride + seat).astype(jnp.int32)
        ids = lax.broadcasted_iota(jnp.int32, (BLOCK, planes * stride), 1)
        line_pick = (ids == place).astype(jnp.float32).astype(jnp.bfloat16)
        picked = product(line_parts, line_pick, nt)
        scal_ref[:, here] = picked[:SUB] + picked[SUB : 2 * SUB] + picked[2 * SUB : 3 * SUB]
    for t in range(local_rows // BLOCK):
        at = pl.ds(t * BLOCK, BLOCK)
        col_ref[at, :] = feat_ref[:, at].T
    piv = scal_ref[...]
    piv_scale = piv[3:4, :]
    match = match_ref[...]

    scale = (5.0**0.5) / LENGTH_SCALE
    points = (piv[:3, :] - 0.5) * scale
    length = jnp.sum(points * points, axis=0, keepdims=True)
    point_parts = [part.astype(jnp.float32) * -2.0 for part in parts_of(points)]
    lines = [point_parts[k][i : i + 1, :] for i in range(3) for k in (0, 1, 0, 1, 2, 0)]
    lines += [jnp.ones((3, pivots), jnp.float32)] + [part.astype(jnp.float32) for part in parts_of(length)]
    lines.append(jnp.zeros((BLOCK - 24, pivots), jnp.float32))
    right = jnp.concatenate(lines, axis=0).astype(jnp.bfloat16)

    def step(t, carry):
        at = pl.ds(pl.multiple_of(t * WIDE, WIDE), WIDE)
        cols = col_ref[at, :]
        dist_sq = jnp.maximum(product(left_ref[at, :], right, ((1,), (0,))), 1e-30)
        scaled = dist_sq * lax.rsqrt(dist_sq)
        value = (1.0 + scaled + dist_sq * (1.0 / 3.0)) * jnp.exp2(scaled * -LOG2E)
        value = cols[:, 3:4] * piv_scale * value
        row_ids = lax.broadcasted_iota(jnp.int32, (WIDE, 1), 0) + t * WIDE
        field_ref[at, :] = value + jnp.where(row_ids == match, cols[:, 4:5], 0.0)
        return carry

    lax.fori_loop(0, local_rows // WIDE, step, 0)


def main_kernel(
    me_ref,
    mine_ref,
    other_ref,
    info_ref,
    scal_ref,
    field_ref,
    base_ref,
    high_hbm,
    middle_hbm,
    low_hbm,
    out_hbm,
    resid_ref,
    sums_ref,
    cov_high,
    cov_middle,
    cov_low,
    table_high,
    table_middle,
    table_low,
    kernel_high,
    kernel_middle,
    kernel_low,
    z_ref,
    r_ref,
    tile_ref,
    load_sem,
    store_sem,
):
    core = lax.rem(me_ref[0], 2)
    pivots = z_ref.shape[0]
    local_rows, cov_width = cov_high.shape
    planes, plane_rows, half = mine_ref.shape
    blocks = pivots // BLOCK
    loads = [
        pltpu.make_async_copy(source, target, load_sem.at[i])
        for i, (source, target) in enumerate(
            ((high_hbm, cov_high), (middle_hbm, cov_middle), (low_hbm, cov_low))
        )
    ]
    for load in loads:
        load.start()
    nt = ((1,), (1,))

    scale = (5.0**0.5) / LENGTH_SCALE
    candidates = planes * plane_rows
    mine = mine_ref[...].reshape(candidates, half)
    other = other_ref[...].reshape(candidates, half)
    both = jnp.concatenate([jnp.where(core == 0, mine, other), jnp.where(core == 0, other, mine)], axis=1)
    both_parts = parts_of(both)
    info_t = info_ref[...].T
    for b in range(blocks):
        here = pl.ds(b * BLOCK, BLOCK)
        xy, seat = info_t[:, b : b + 1], info_t[:, blocks + b : blocks + b + 1]
        place = (xy * plane_rows + seat).astype(jnp.int32)
        ids = lax.broadcasted_iota(jnp.int32, (BLOCK, candidates), 1)
        pick = (ids == place).astype(jnp.float32).astype(jnp.bfloat16)
        for part, table in zip(both_parts, (table_high, table_middle, table_low)):
            table[here, :] = product(pick, part, ((1,), (0,))).astype(jnp.bfloat16)

    piv = scal_ref[...]
    piv_rows = [piv[i : i + 1, :] * scale for i in range(3)]
    piv_scale, piv_noise = piv[3:4, :], piv[4:5, :]

    for b in range(blocks):
        here = pl.ds(b * BLOCK, BLOCK)
        right = slice(b * BLOCK, pivots)
        cols = scal_ref[:, here].T
        piece = matern(
            [cols[:, i : i + 1] * scale for i in range(3)],
            [row[:, right] for row in piv_rows],
            cols[:, 3:4],
            piv_scale[:, right],
        )
        same = lax.broadcasted_iota(jnp.int32, (BLOCK, 1), 0) == lax.broadcasted_iota(
            jnp.int32, (1, pivots - b * BLOCK), 1
        )
        piece = piece + jnp.where(same, piv_noise[:, right], 0.0)
        left_parts = [table[here, :] for table in (table_high, table_middle, table_low)]
        right_parts = [table[right, :] for table in (table_high, table_middle, table_low)]
        z_ref[here, right] = piece + dot_parts(left_parts, right_parts, nt)
        if b:
            z_ref[here, : b * BLOCK] = jnp.zeros((BLOCK, b * BLOCK), jnp.float32)
    for load in loads:
        load.wait()
    def kernel_tile(t):
        at = pl.ds(pl.multiple_of(t * WIDE, WIDE), WIDE)
        cov = [part[at, :] for part in (cov_high, cov_middle, cov_low)]
        kernel = field_ref[at, :] + dot_parts(cov, (table_high[...], table_middle[...], table_low[...]), nt)
        for part, target in zip(parts_of(kernel), (kernel_high, kernel_middle, kernel_low)):
            target[at, :] = part

    per_step = local_rows // WIDE // blocks

    def step(b, carry):
        at = pl.ds(pl.multiple_of(b * BLOCK, BLOCK), BLOCK)
        pieces = [
            z_ref[pl.ds(pl.multiple_of(b * BLOCK + SUB * i, SUB), SUB), at]
            for i in range(BLOCK // SUB)
        ]
        inverse = jnp.concatenate(block_inverse(pieces), axis=0)
        for i in range(per_step):
            kernel_tile(b * per_step + i)
        r_ref[...] = dot_parts(parts_of(inverse), parts_of(z_ref[at, :]), ((1,), (0,)))
        r_ref[:, at] = inverse
        z_ref[:, at] = jnp.zeros((pivots, BLOCK), jnp.float32)
        row = r_ref[...]
        for s in range(blocks - 1):

            @pl.when(b == s)
            def _():
                later = slice((s + 1) * BLOCK, pivots)
                coef = parts_of(row[:, later].T)
                z_ref[later, :] -= dot_parts(coef, parts_of(row), ((1,), (0,)))

        z_ref[at, :] = row
        return carry

    lax.fori_loop(0, blocks, step, 0)

    diagonal = lax.broadcasted_iota(jnp.int32, (BLOCK, BLOCK), 0) == lax.broadcasted_iota(
        jnp.int32, (BLOCK, BLOCK), 1
    )
    left = pivots // 2
    half_tiles = WIDE // BLOCK
    tiles = local_rows // WIDE
    inverse_parts = parts_of(z_ref[...])
    for part, target in zip(inverse_parts, (table_high, table_middle, table_low)):
        target[:, :] = part[:, :left]
    late = [part[left:, left:] for part in inverse_parts]

    def tile_step(t, taken):
        at = pl.ds(pl.multiple_of(t * WIDE, WIDE), WIDE)
        slot = lax.rem(t, 2)

        @pl.when(t >= 2)
        def _():
            pltpu.make_async_copy(tile_ref.at[slot], out_hbm.at[at, :], store_sem.at[slot]).wait()

        kernels = [part[at, :] for part in (kernel_high, kernel_middle, kernel_low)]
        early = [part[:, :left] for part in kernels]
        first = dot_parts(early, [table[:left, :] for table in (table_high, table_middle, table_low)], nt)
        second = dot_parts(early, [table[left:, :] for table in (table_high, table_middle, table_low)], nt)
        second = second + dot_parts([part[:, left:] for part in kernels], late, nt)
        tile_ref[slot, :, :left] = first
        tile_ref[slot, :, left:] = second
        pltpu.make_async_copy(tile_ref.at[slot], out_hbm.at[at, :], store_sem.at[slot]).start()
        total = jnp.zeros((WIDE, BLOCK), jnp.float32)
        new_taken = []
        for b in range(blocks):
            source = first if b * BLOCK < left else second
            piece = source[:, (b * BLOCK) % left : (b * BLOCK) % left + BLOCK]
            square = piece * piece
            total = total + square
            new_taken.append(taken[b] + jnp.sum(square.reshape(WIDE // SUB, SUB, BLOCK), axis=0))
        line = jnp.sum(total, axis=1, keepdims=True)
        for h in range(half_tiles):
            spread = jnp.where(diagonal, line[h * BLOCK : (h + 1) * BLOCK, :], 0.0)
            where = pl.ds(t * half_tiles + h, 1)
            resid_ref[where, :] = base_ref[where, :] - jnp.sum(spread, axis=0, keepdims=True)
        return tuple(new_taken)

    zero = jnp.zeros((SUB, BLOCK), jnp.float32)
    taken = lax.fori_loop(0, tiles, tile_step, (zero,) * blocks)
    for tile in (tiles - 2, tiles - 1):
        at = pl.ds(tile * WIDE, WIDE)
        pltpu.make_async_copy(tile_ref.at[tile % 2], out_hbm.at[at, :], store_sem.at[tile % 2]).wait()

    total = jnp.sum(base_ref[...])
    lanes = lax.broadcasted_iota(jnp.int32, sums_ref.shape, 1)
    sums = jnp.zeros(sums_ref.shape, jnp.float32)
    for b in range(blocks):
        total = total - jnp.sum(taken[b])
        sums = jnp.where(lanes == b, total, sums)
    sums_ref[...] = sums


def last_kernel(sums_ref, resid_ref, weights_ref, mean_ref, *, rows):
    devices, _, width = sums_ref.shape
    total = jnp.sum(sums_ref[...].reshape(devices, width), axis=0, keepdims=True)
    mean = total * (1.0 / rows)
    count = mean_ref.shape[1]
    mean_ref[...] = mean[:, :count]
    weights_ref[...] = resid_ref[...] / mean[:, count - 1 : count]


def shape(dims, dtype=jnp.float32):
    return jax.ShapeDtypeStruct(dims, dtype)


VMEM = pl.BlockSpec(memory_space=pltpu.VMEM)
SMEM = pl.BlockSpec(memory_space=pltpu.SMEM)
ANY = pl.BlockSpec(memory_space=pl.ANY)
PARAMS = pltpu.CompilerParams(vmem_limit_bytes=40 << 20)
AUX_PARAMS = pltpu.CompilerParams(vmem_limit_bytes=55 << 20)


def prep(me, owner, offset, points, amp, noise, cov, copies):
    slots = CAP * owner.shape[0]
    return pl.pallas_call(
        prep_kernel,
        out_shape=shape((copies, 2 * slots + SUB, BLOCK)),
        in_specs=[SMEM] + [ANY] * 6,
        out_specs=VMEM,
        scratch_shapes=[pltpu.VMEM(value.shape, value.dtype) for value in (owner, offset, points, amp, noise)]
        + [
            pltpu.VMEM((slots, cov.shape[1]), jnp.float32),
            pltpu.SemaphoreType.DMA((slots,)),
            pltpu.SemaphoreType.DMA((5,)),
        ],
        compiler_params=pltpu.CompilerParams(vmem_limit_bytes=60 << 20),
        name="prep",
    )(me, owner, offset, points, amp, noise, cov)


def aux(me, owner, offset, points, amp, noise, cov):
    rows, width = cov.shape
    return pl.pallas_call(
        aux_kernel,
        out_shape=(
            shape((rows, width), jnp.bfloat16),
            shape((rows, width), jnp.bfloat16),
            shape((rows, width), jnp.bfloat16),
            shape((SUB, rows)),
            shape((rows // BLOCK, BLOCK)),
            shape((SUB, BLOCK)),
            shape((1, owner.size), jnp.int32),
            shape((BLOCK, BLOCK)),
            shape((rows, BLOCK), jnp.bfloat16),
            shape((1,), jnp.int32),
        ),
        in_specs=[SMEM] + [ANY] * 6,
        out_specs=(VMEM,) * 9 + (SMEM,),
        scratch_shapes=[pltpu.VMEM(value.shape, value.dtype) for value in (owner, offset, points, amp, noise, cov)]
        + [pltpu.SemaphoreType.DMA((6,))],
        compiler_params=AUX_PARAMS,
        cost_estimate=pl.CostEstimate(flops=10**8, bytes_accessed=6 << 20, transcendentals=0),
        name="aux",
    )(me, owner, offset, points, amp, noise, cov)


def seat(me, comb, got, copies, seats):
    return pl.pallas_call(
        seat_kernel,
        out_shape=shape((copies, seats + SUB, BLOCK)),
        in_specs=[SMEM, VMEM, VMEM],
        out_specs=VMEM,
        compiler_params=PARAMS,
        name="seat",
    )(me, comb, got)


def field(mine, info, match, feat, left):
    pivots, rows = match.shape[1], feat.shape[1]
    return pl.pallas_call(
        field_kernel,
        out_shape=(shape((SUB, pivots)), shape((rows, pivots))),
        in_specs=[VMEM] * 5,
        out_specs=(VMEM, VMEM),
        scratch_shapes=[pltpu.VMEM((rows, SUB), jnp.float32)],
        compiler_params=PARAMS,
        cost_estimate=pl.CostEstimate(flops=10**8, bytes_accessed=6 << 20, transcendentals=0),
        name="field",
    )(mine, info, match, feat, left)


def main(me, mine, other, info, scal, local_field, base, high, middle, low, devices):
    rows, width = high.shape
    pivots = scal.shape[1]
    bf = jnp.bfloat16
    return pl.pallas_call(
        main_kernel,
        out_shape=(shape((rows, pivots)), shape((rows // BLOCK, BLOCK)), shape((devices, BLOCK))),
        in_specs=[SMEM] + [VMEM] * 6 + [ANY] * 3,
        out_specs=(ANY, VMEM, VMEM),
        scratch_shapes=[pltpu.VMEM((rows, width), bf)] * 3
        + [pltpu.VMEM((pivots, width), bf)] * 3
        + [pltpu.VMEM((rows, pivots), bf)] * 3
        + [
            pltpu.VMEM((pivots, pivots), jnp.float32),
            pltpu.VMEM((BLOCK, pivots), jnp.float32),
            pltpu.VMEM((2, WIDE, pivots), jnp.float32),
            pltpu.SemaphoreType.DMA((3,)),
            pltpu.SemaphoreType.DMA((2,)),
        ],
        compiler_params=PARAMS,
        name="factor_rows",
    )(me, mine, other, info, scal, local_field, base, high, middle, low)


def last(sums, resid, blocks, rows):
    return pl.pallas_call(
        functools.partial(last_kernel, rows=rows),
        out_shape=(shape(resid.shape), shape((1, blocks))),
        in_specs=[VMEM, VMEM],
        out_specs=(VMEM, VMEM),
        compiler_params=PARAMS,
        name="last",
    )(sums, resid)


def local(locations, amplitude, noise, covariates, pivot_owner, pivot_offset):
    me = lax.axis_index(AXES).astype(jnp.int32)[None]
    blocks = pivot_owner.shape[0]
    sizes = [lax.axis_size(name) for name in AXES]
    devices = sizes[0] * sizes[1] * sizes[2] * sizes[3]
    swap = [(0, 1), (1, 0)]
    amp, nugget = amplitude[None], noise[None]
    args = (me, pivot_owner, pivot_offset, locations, amp, nugget, covariates)

    column = lax.all_to_all(prep(*args, sizes[0] * sizes[3]), ("z", "c"), 0, 0, tiled=True)
    high, middle, low, feat, base, info, match, comb, left, most = aux(*args)

    def rest(seats):
        def run(column, comb, info, match, feat, left, base, high, middle, low):
            message = seat(me, comb, column, sizes[1] * sizes[2], seats)
            mine = lax.all_to_all(message, ("x", "y"), 0, 0, tiled=True)
            other = lax.ppermute(mine, "c", swap)
            scal, local_field = field(mine, info, match, feat, left)
            return main(me, mine, other, info, scal, local_field, base, high, middle, low, devices)

        return run

    operands = (column, comb, info, match, feat, left, base, high, middle, low)
    if FEW:
        factor, resid, sums = lax.cond(most[0] <= FEW, rest(FEW), rest(BLOCK), *operands)
    else:
        factor, resid, sums = rest(BLOCK)(*operands)
    all_sums = lax.all_to_all(sums[:, None, :], AXES, 0, 0, tiled=True)
    weights, mean_residual = last(all_sums, resid, blocks, locations.shape[1] * devices)
    return (factor, weights.reshape(-1), mean_residual.reshape(-1))


def solution(mesh):
    named = Mesh(mesh.devices.reshape(8, 4, 4, 2), AXES)
    return jax.shard_map(
        local,
        mesh=named,
        in_specs=(P(None, AXES), P(AXES), P(AXES), P(AXES, None), P(), P()),
        out_specs=(P(AXES, None), P(AXES), P()),
        check_vma=False,
    )
```
